32 devices in a mesh: domain: 8 (over y, x, core), band: 4 (over z).
Axes of the slice: x: 2, y: 2, z: 4, core: 2. Of those that a mesh axis runs over, the one named last changes fastest.
Arguments:
- states_block: bfloat16 [27648, 512], P('domain', 'band')
- cell_matrix: bfloat16 [343, 343], replicated, as said below
- cell_scale: float32 [128], P('domain'), may hold values from 0.5 to 2
- potential: float32 [27648], P('domain'), may hold values from -1 to 1
- connectivity: int32 [128, 343], P('domain'), may hold values from 0 to 3743, as said below
- boundary_nodes: int32 [2304], P('domain'), may hold values from 0 to 3455, as said below
Outputs:
- orthonormal_block: float32 [27648, 512], P('domain', 'band')
The draws below stay inside these ranges and needn't reach their ends.
Inputs may be any that keep to these rules, and one draw needn't show every extreme that they name: `cell_matrix`: symmetric. `connectivity`: block d names rows of subdomain d's extended array: values under 3456 are its own nodes, 3456 + p the p-th entry of block d + 1 (cyclically) of boundary_nodes; only the last 8 cells of a block name values of 3456 or more; every own node of a block is named by some cell. `boundary_nodes`: each block holds 288 distinct nodes of its subdomain.
All inputs are finite; a program needn't handle non-finite values.
Results may differ from the reference program's by a relative error of at most 0.0057.
Values may be sent and summed in bfloat16 or wider, within the bound.
No kernel may reach another device: no remote copies, remote signals or barrier semaphores. Data moves between devices by JAX's collectives and lax.ppermute only.
A program may use at most 64 MiB of HBM per device.

```python
import math
from functools import partial
import jax
import jax.numpy as jnp
from jax import lax

CX = 2
CY = 4
CZ = 2
STATES = 512
NPC = 343
DEGREE = 2
NODES_DEV = 3456
PLANE = 288
CELLS_DEV = 16
NODES = 27648
CELLS = 128
BOUNDARY = 2304
N_DOMAIN = 8


def single_order(single):
    order = jax.random.permutation(single, NODES_DEV).astype(jnp.int32)
    top = jnp.int32(NODES_DEV - 1)
    where_top = jnp.argmax(order == top)
    order = order.at[where_top].set(order[0]).at[0].set(top)
    where_zero = jnp.argmax(order == 0)
    order = order.at[where_zero].set(order[1]).at[1].set(jnp.int32(0))
    return order


def node_orders(key):
    count = CELLS // CELLS_DEV
    keys = jax.random.split(key, count)
    return jax.vmap(single_order)(keys).astype(jnp.int32)


def draw_connectivity(key, part):
    orders = node_orders(key)
    cell_index = jnp.arange(CELLS_DEV, dtype=jnp.int32)
    node_index = jnp.arange(NPC, dtype=jnp.int32)
    layer = cell_index // (CX * CY)
    column_x = cell_index // CY % CX
    column_y = cell_index % CY
    along_z = node_index // 49
    along_x = node_index // 7 % 7
    along_y = node_index % 7
    pos_x = (6 * column_x[:, None] + along_x[None, :]) % (6 * CX)
    pos_y = (6 * column_y[:, None] + along_y[None, :]) % (6 * CY)
    plane_pos = pos_x * (6 * CY) + pos_y
    height = 6 * layer[:, None] + along_z[None, :]
    structured = jnp.minimum(height * PLANE + plane_pos, NODES_DEV - 1)
    local = orders[:, structured]
    linked = jnp.where(height[None] == 6 * CZ, NODES_DEV + plane_pos[None], local)
    return linked.reshape(CELLS, NPC).astype(jnp.int32)


def draw_boundary_nodes(key, part):
    orders = node_orders(key)
    return orders[:, :PLANE].reshape(BOUNDARY).astype(jnp.int32)


def draw_cell_matrix(key, part):
    key = jax.random.fold_in(key, 5)
    off_key, diag_key = jax.random.split(key, 2)
    offdiag = jax.random.normal(off_key, (NPC, NPC))
    offdiag = (offdiag + offdiag.T) * (0.3 / math.sqrt(NPC))
    diagonal = jax.random.uniform(diag_key, (NPC,), minval=1.2, maxval=2.4)
    identity = jnp.eye(NPC, dtype=jnp.float32)
    matrix = offdiag * (1.0 - identity) + diagonal[:, None] * identity
    return matrix.astype(jnp.bfloat16)


def draw_states_block(key, part):
    key = jax.random.fold_in(key, 7)
    base_key, row_key, col_key = jax.random.split(key, 3)
    row_scale = jnp.exp(jax.random.uniform(row_key, (NODES, 1), minval=0.0, maxval=math.log(10.0)))
    col_scale = jnp.exp(jax.random.uniform(col_key, (1, STATES), minval=0.0, maxval=math.log(10.0)))
    base = jax.random.normal(base_key, (NODES, STATES))
    return (base * row_scale * col_scale * 0.25).astype(jnp.bfloat16)


def block_levels(key, dims, pieces, low, largest):
    def one(position, shards_of):
        draws = jax.random.uniform(jax.random.fold_in(jax.random.fold_in(key, 6), position), (shards_of,), jnp.float32, low / len(pieces), largest / len(pieces))
        return jnp.repeat(jnp.exp(draws), dims[position] // shards_of).reshape((-1,) + (1,) * (len(dims) - position - 1))

    loudness = one(*pieces[0])
    for cut in pieces[1:]:
        loudness = loudness * one(*cut)
    return loudness


def setup_inputs(seed: int = 0) -> dict:
    seeds = jax.random.split(jax.random.key(seed), 7)
    states_block = draw_states_block(jax.random.fold_in(seeds[6], 71), 0)
    cell_matrix = draw_cell_matrix(jax.random.fold_in(seeds[6], 71), 0)
    cell_scale = jnp.clip(jnp.exp(math.log(2.0) - 1.3862944 * jax.random.uniform(seeds[2], (CELLS,), jnp.float32) ** block_levels(seeds[2], (CELLS,), ((0, 8),), -0.2, 0.2)), 0.5, 2.0)
    potential = jnp.clip(jax.random.uniform(seeds[3], (NODES,), jnp.float32, -1.0, 1.0) * block_levels(seeds[3], (NODES,), ((0, 8),), -0.4, 0.0), -1.0, 1.0)
    connectivity = draw_connectivity(jax.random.fold_in(seeds[6], 71), 0)
    boundary_nodes = draw_boundary_nodes(jax.random.fold_in(seeds[6], 71), 0)
    return dict(states_block=states_block, cell_matrix=cell_matrix, cell_scale=cell_scale, potential=potential, connectivity=connectivity, boundary_nodes=boundary_nodes)


CENTER = 1.5
HALF_WIDTH = 1.25

def device_cells(items, cell_matrix):
    extended, links, scales = items
    picked = extended[links].astype(jnp.float32)
    products = jnp.einsum('mn,cns->cms', cell_matrix.astype(jnp.float32), picked)
    products = products * scales[:, None, None]
    return jax.ops.segment_sum(products.reshape(-1, products.shape[-1]), links.reshape(-1), num_segments=extended.shape[0])

def apply_operator(rounded, widened, cell_matrix, scales, potential, links, boundary):
    following = jnp.roll(rounded, -1, axis=0)
    next_lists = jnp.roll(boundary, -1, axis=0)
    ghost_rows = jnp.take_along_axis(following, next_lists[:, :, None], axis=1)
    extended = jnp.concatenate([rounded, ghost_rows], axis=1)
    assembled = lax.map(partial(device_cells, cell_matrix=cell_matrix), (extended, links, scales))
    owned = rounded.shape[1]
    own_sums = assembled[:, :owned]
    returned = jnp.roll(assembled[:, owned:], 1, axis=0)
    own_sums = jax.vmap(lambda sums, where, extra: sums.at[where].add(extra))(own_sums, boundary, returned)
    return own_sums + potential[:, :, None] * widened

def reference(states_block, cell_matrix, cell_scale, potential, connectivity, boundary_nodes):
    rounded = states_block.reshape(N_DOMAIN, NODES_DEV, STATES)
    scales = cell_scale.reshape(N_DOMAIN, CELLS_DEV)
    node_potential = potential.reshape(N_DOMAIN, NODES_DEV)
    links = connectivity.reshape(N_DOMAIN, CELLS_DEV, NPC)
    boundary = boundary_nodes.reshape(N_DOMAIN, PLANE)
    previous = rounded.astype(jnp.float32)
    image = apply_operator(rounded, previous, cell_matrix, scales, node_potential, links, boundary)
    current = (image - CENTER * previous) / HALF_WIDTH
    for rounds in range(1, DEGREE):
        image = apply_operator(current.astype(jnp.bfloat16), current, cell_matrix, scales, node_potential, links, boundary)
        following = 2.0 * (image - CENTER * current) / HALF_WIDTH - previous
        previous, current = (current, following)
    filtered = current.reshape(NODES, STATES)
    gram = jnp.dot(filtered.T.astype(jnp.float32), filtered.astype(jnp.float32), precision=lax.Precision.HIGHEST, preferred_element_type=jnp.float32) / NODES
    lower = jnp.linalg.cholesky(gram)
    return jax.scipy.linalg.solve_triangular(lower, filtered.T, lower=True).T
```

```python
import functools

import jax
import jax.numpy as jnp
from jax import lax
from jax.experimental import pallas as pl
from jax.experimental.pallas import tpu as pltpu
from jax.sharding import PartitionSpec as P

CENTER = 1.5
HALF_WIDTH = 1.25
LANES = 128
CHAINS = 4
EXACT = lax.Precision.HIGHEST
F32 = jnp.float32
BF16 = jnp.bfloat16
VM = pl.BlockSpec(memory_space=pltpu.VMEM)
SM = pl.BlockSpec(memory_space=pltpu.SMEM)
PARAMS = pltpu.CompilerParams(vmem_limit_bytes=48 << 20)


def shifted(value, axis, steps):
    count = lax.axis_size(axis)
    return lax.ppermute(value, axis, [(i, (i + steps) % count) for i in range(count)])


def upward(value, axis, steps):
    count = lax.axis_size(axis)
    return lax.ppermute(value, axis, [(i, i + steps) for i in range(count - steps)])


def pick_kernel(nodes, rows_ref, out_ref, wide, picked):
    wide[...] = rows_ref[...].astype(F32)
    count = nodes.shape[0]

    def body(step, _):
        for k in range(16):
            i = step * 16 + k
            picked[pl.ds(i, 1), :] = wide[pl.ds(nodes[i], 1), :]
        return 0

    lax.fori_loop(0, count // 16, body, 0)
    out_ref[...] = picked[...].astype(BF16)


def pick(nodes, rows):
    count = nodes.shape[0]
    return pl.pallas_call(
        pick_kernel,
        out_shape=jax.ShapeDtypeStruct((count, LANES), BF16),
        in_specs=[SM, VM],
        out_specs=VM,
        scratch_shapes=[pltpu.VMEM(rows.shape, F32), pltpu.VMEM((count, LANES), F32)],
        compiler_params=PARAMS,
        name="pick",
    )(nodes, rows)


def cells_kernel(
    links, scale, rows_ref, ghost_ref, matrix_ref, potential_ref, out_ref, back_ref, ext, *scratch
):
    gathered, products, sums = scratch[:2], scratch[2:4], scratch[4:]
    owned = rows_ref.shape[0]
    cells, npc = links.shape
    for block in range(owned // LANES):
        here = slice(block * LANES, (block + 1) * LANES)
        wide = rows_ref[here, :].astype(F32)
        level = jnp.broadcast_to(potential_ref[block : block + 1, :], (LANES, LANES)).T
        sums[0][here, :] = (level - CENTER) * wide
        ext[here, :] = wide.astype(BF16).astype(F32)
    ext[owned:, :] = ghost_ref[...].astype(F32)
    sums[0][owned:, :] = jnp.zeros_like(ghost_ref[...], F32)
    for total in sums[1:]:
        total[...] = jnp.zeros_like(total)
    for rows in gathered:
        rows[npc:, :] = jnp.zeros_like(rows[npc:, :])

    def pair(step, _):
        for r in range(npc):
            for half in range(2):
                gathered[half][r : r + 1, :] = ext[pl.ds(links[2 * step + half, r], 1), :]
        both = jnp.concatenate([rows[...].astype(BF16) for rows in gathered], axis=1)
        made = jnp.dot(matrix_ref[...], both[:npc], preferred_element_type=F32)
        for half in range(2):
            products[half][0:npc, :] = (
                made[:, half * LANES : (half + 1) * LANES] * scale[2 * step + half]
            )
        for r in range(npc):
            for half in range(2):
                total = sums[(2 * r + half) % CHAINS]
                row = pl.ds(links[2 * step + half, r], 1)
                total[row, :] = total[row, :] + products[half][r : r + 1, :]
        return 0

    lax.fori_loop(0, cells // 2, pair, 0)
    out_ref[...] = sum(total[0:owned, :] for total in sums)
    back_ref[...] = sum(total[owned:, :] for total in sums)


def cells(links, scale, rows, ghost, matrix, potential):
    owned, plane, npc = rows.shape[0], ghost.shape[0], links.shape[1]
    padded = (npc + 15) // 16 * 16
    return pl.pallas_call(
        cells_kernel,
        out_shape=(
            jax.ShapeDtypeStruct((owned, LANES), F32),
            jax.ShapeDtypeStruct((plane, LANES), F32),
        ),
        in_specs=[SM, SM, VM, VM, VM, VM],
        out_specs=(VM, VM),
        scratch_shapes=[pltpu.VMEM((owned + plane, LANES), F32)]
        + [pltpu.VMEM((padded, LANES), F32)] * 4
        + [pltpu.VMEM((owned + plane, LANES), F32)] * CHAINS,
        compiler_params=PARAMS,
        name="cells",
    )(links, scale, rows, ghost, matrix, potential)


def add_back(nodes, target, back_ref, factor, picked=None):
    def body(step, _):
        at = [step * 16 + k for k in range(16)]
        rows = [pl.ds(nodes[i], 1) for i in at]
        new = [target[r, :] + factor * back_ref[pl.ds(i, 1), :] for i, r in zip(at, rows)]
        for i, r, value in zip(at, rows, new):
            target[r, :] = value
            if picked is not None:
                picked[pl.ds(i, 1), :] = value
        return 0

    lax.fori_loop(0, nodes.shape[0] // 16, body, 0)


def first_kernel(nodes, sums_ref, back_ref, out_ref, picked_ref, picked):
    out_ref[...] = sums_ref[...] * (1.0 / HALF_WIDTH)
    add_back(nodes, out_ref, back_ref, 1.0 / HALF_WIDTH, picked)
    picked_ref[...] = picked[...].astype(BF16)


def first_term(nodes, sums, back):
    return pl.pallas_call(
        first_kernel,
        out_shape=(
            jax.ShapeDtypeStruct(sums.shape, F32),
            jax.ShapeDtypeStruct(back.shape, BF16),
        ),
        in_specs=[SM, VM, VM],
        out_specs=(VM, VM),
        scratch_shapes=[pltpu.VMEM(back.shape, F32)],
        compiler_params=PARAMS,
        name="first_term",
    )(nodes, sums, back)


def second_kernel(band, nodes, sums_ref, back_ref, previous_ref, *refs):
    pieces, total = refs[:-1], refs[-1]
    total[...] = sums_ref[...] * (2.0 / HALF_WIDTH) - previous_ref[...].astype(F32)
    add_back(nodes, total, back_ref, 2.0 / HALF_WIDTH)
    count = len(pieces)
    rows = total.shape[0] // count
    for k, piece in enumerate(pieces):
        start = pl.multiple_of(lax.rem(band[0] + k, count) * rows, rows)
        piece[...] = total[pl.ds(start, rows), :].astype(BF16)


def second_term(band, nodes, sums, back, previous, count):
    owned = sums.shape[0]
    return pl.pallas_call(
        second_kernel,
        out_shape=[jax.ShapeDtypeStruct((owned // count, LANES), BF16)] * count,
        in_specs=[SM, SM, VM, VM, VM],
        out_specs=[VM] * count,
        scratch_shapes=[pltpu.VMEM(sums.shape, F32)],
        compiler_params=PARAMS,
        name="second_term",
    )(band, nodes, sums, back, previous)


def gram_kernel(band, *refs):
    pieces, out_ref, held = refs[:-2], refs[-2], refs[-1]
    count = len(pieces)
    for s, piece in enumerate(pieces):
        held[lax.rem(band[0] + (count - s), count)] = piece[...]
    at = 0
    for i in range(count):
        for j in range(i + 1):
            out_ref[at : at + LANES, :] = lax.dot_general(
                held[i], held[j], (((0,), (0,)), ((), ())), preferred_element_type=F32
            )
            at += LANES


def partial_gram(band, pieces):
    count = len(pieces)
    blocks = count * (count + 1) // 2
    return pl.pallas_call(
        gram_kernel,
        out_shape=jax.ShapeDtypeStruct((blocks * LANES, LANES), F32),
        in_specs=[SM] + [VM] * count,
        out_specs=VM,
        scratch_shapes=[pltpu.VMEM((count,) + pieces[0].shape, BF16)],
        compiler_params=PARAMS,
        name="partial_gram",
    )(band, *pieces)


def summed(value):
    count = lax.axis_size("domain")
    if count > 8:
        return lax.psum(value, ("domain", "band"))
    chunks = value.reshape(count, -1, LANES)
    me = lax.axis_index("domain")
    taken = [
        lax.dynamic_index_in_dim(chunks, lax.rem(me + k, count), 0, keepdims=False)
        for k in range(count)
    ]
    total = taken[0]
    for part in [shifted(taken[k], "domain", k) for k in range(1, count)]:
        total = total + part
    whole = total
    for k in range(1, lax.axis_size("band")):
        whole = whole + shifted(total, "band", k)
    parts = [whole] + [shifted(whole, "domain", k) for k in range(1, count)]
    order = lax.rem(me - jnp.arange(count) + count, count)
    return jnp.stack(parts)[order].reshape(value.shape)


def small_inverse(tiles, lane):
    count, tiles, done = len(tiles), list(tiles), []
    sub = lax.broadcasted_iota(jnp.int32, tiles[0].shape, 0)

    def along_lanes(tile, column):
        return jnp.broadcast_to(tile[:, column : column + 1], tile.shape)

    def along_rows(tile, row):
        return jnp.broadcast_to(tile[row : row + 1, :], tile.shape)

    for p in range(count):
        base = 8 * p
        group = (lane >= base) & (lane < base + 8)
        columns = [along_lanes(tiles[p], base + m) for m in range(8)]
        entry = {(i, j): along_rows(columns[j], i) for j in range(8) for i in range(j, 8)}
        start = jnp.where(group, (lane - base == sub).astype(F32), tiles[p])
        solved = [along_rows(start, i) for i in range(8)]
        following = None
        if p + 1 < count:
            ahead = [along_lanes(tiles[p + 1], base + m) for m in range(8)]
            following = jnp.where(group, 0.0, tiles[p + 1])
        inverse, factor = [], {}
        for j in range(8):
            pivot = 1.0 / entry[j, j]
            inverse.append(pivot)
            for i in range(j + 1, 8):
                factor[i, j] = entry[i, j] * pivot
            for i in range(j + 1, 8):
                for k in range(j + 1, i + 1):
                    entry[i, k] = entry[i, k] - factor[i, j] * entry[k, j]
                solved[i] = solved[i] - factor[i, j] * solved[j]
            if following is not None:
                scaled = ahead[j] * pivot
                following = following - scaled * solved[j]
                for m in range(j + 1, 8):
                    ahead[m] = ahead[m] - scaled * entry[m, j]
        result = solved[0] * lax.rsqrt(entry[0, 0])
        for i in range(1, 8):
            result = jnp.where(sub == i, solved[i] * lax.rsqrt(entry[i, i]), result)
        done.append(jnp.where(lane <= base + sub, result, 0.0))
        if p + 2 < count:
            back = [None] * 8
            for i in range(7, -1, -1):
                value = solved[i] * inverse[i]
                for k in range(i + 1, 8):
                    value = value - factor[k, i] * back[k]
                back[i] = value
            for i in range(p + 2, count):
                value = jnp.where(group, 0.0, tiles[i])
                for m in range(8):
                    value = value - along_lanes(tiles[i], base + m) * back[m]
                tiles[i] = value
        if following is not None:
            tiles[p + 1] = following
    return done


def exact_dot(a, b, dims=(((1,), (0,)), ((), ()))):
    return lax.dot_general(a, b, dims, precision=EXACT, preferred_element_type=F32)


def inverse_kernel(over, packed_ref, out_ref, work, small):
    size = work.shape[0]
    blocks = size // LANES
    at = 0
    for i in range(blocks):
        for j in range(i + 1):
            block = packed_ref[at : at + LANES, :] * over
            work[i * LANES : (i + 1) * LANES, j * LANES : (j + 1) * LANES] = block
            if i != j:
                work[j * LANES : (j + 1) * LANES, i * LANES : (i + 1) * LANES] = block.T
            at += LANES
    out_ref[...] = jnp.zeros_like(out_ref)
    lane = lax.broadcasted_iota(jnp.int32, (8, LANES), 1)

    def step(k, _):
        base = pl.multiple_of(k * LANES, LANES)
        tiles = [
            work[pl.ds(pl.multiple_of(base + 8 * i, 8), 8), pl.ds(base, LANES)]
            for i in range(LANES // 8)
        ]
        for i, tile in enumerate(small_inverse(tiles, lane)):
            small[8 * i : 8 * i + 8, :] = tile
        for which in range(blocks):

            @pl.when(k == which)
            def _():
                a, b = which * LANES, (which + 1) * LANES
                diagonal = small[...]
                out_ref[a:b, a:b] = diagonal
                if which:
                    left = exact_dot(diagonal, work[a:b, 0:a])
                    out_ref[a:b, 0:a] = left
                if b < size:
                    right = exact_dot(diagonal, work[a:b, b:size])
                    column = exact_dot(work[b:size, a:b], diagonal, (((1,), (1,)), ((), ())))
                    work[b:size, b:size] = work[b:size, b:size] - exact_dot(column, right)
                    work[b:size, a:b] = -exact_dot(column, diagonal)
                    if which:
                        work[b:size, 0:a] = work[b:size, 0:a] - exact_dot(column, left)

        return 0

    lax.fori_loop(0, blocks, step, 0)


def inverse_factor(packed, size, over):
    return pl.pallas_call(
        functools.partial(inverse_kernel, over),
        out_shape=jax.ShapeDtypeStruct((size, size), F32),
        in_specs=[VM],
        out_specs=VM,
        scratch_shapes=[pltpu.VMEM((size, size), F32), pltpu.VMEM((LANES, LANES), F32)],
        compiler_params=PARAMS,
        name="inverse_factor",
    )(packed)


def output_kernel(band, factor_ref, *refs):
    pieces, out_ref = refs[:-1], refs[-1]
    count = factor_ref.shape[0] // LANES
    total = None
    for s in range(count):
        source = band[0] - s
        there = source >= 0
        column = pl.multiple_of(jnp.maximum(source, 0) * LANES, LANES)
        row = pl.multiple_of(band[0] * LANES, LANES)
        block = factor_ref[pl.ds(row, LANES), pl.ds(column, LANES)]
        block = jnp.where(there, block, 0.0)
        high = block.astype(BF16)
        low = (block - high.astype(F32)).astype(BF16)
        dims = (((1,), (1,)), ((), ()))
        piece = pieces[s][...]
        part = lax.dot_general(piece, high, dims, preferred_element_type=F32)
        part = part + lax.dot_general(piece, low, dims, preferred_element_type=F32)
        total = part if total is None else total + part
    out_ref[...] = total


def output(band, factor, received):
    count = len(received)
    owned = received[0].shape[0]
    rows = owned // count
    return pl.pallas_call(
        output_kernel,
        out_shape=jax.ShapeDtypeStruct((owned, LANES), F32),
        grid_spec=pltpu.PrefetchScalarGridSpec(
            num_scalar_prefetch=1,
            grid=(count,),
            in_specs=[pl.BlockSpec(factor.shape, lambda j, band: (0, 0))]
            + [pl.BlockSpec((rows, LANES), lambda j, band: (j, 0))] * count,
            out_specs=pl.BlockSpec((rows, LANES), lambda j, band: (lax.rem(band[0] + j, count), 0)),
        ),
        compiler_params=PARAMS,
        name="output",
    )(band, factor, *received)


def shards(states_block, cell_matrix, cell_scale, potential, connectivity, boundary_nodes):
    owned = states_block.shape[0]
    count = lax.axis_size("band")
    band = lax.axis_index("band").astype(jnp.int32).reshape(1)
    levels = potential.reshape(owned // LANES, LANES)

    ghost = shifted(pick(boundary_nodes, states_block), "domain", -1)
    sums, back = cells(connectivity, cell_scale, states_block, ghost, cell_matrix, levels)
    current, edge = first_term(boundary_nodes, sums, shifted(back, "domain", 1))
    ghost = shifted(edge, "domain", -1)
    sums, back = cells(connectivity, cell_scale, current, ghost, cell_matrix, levels)
    back = shifted(back, "domain", 1)
    pieces = second_term(band, boundary_nodes, sums, back, states_block, count)

    arrived = [pieces[0]] + [shifted(pieces[s], "band", s) for s in range(1, count)]
    packed = summed(partial_gram(band, arrived))
    factor = inverse_factor(
        packed, count * LANES, 1.0 / (owned * lax.axis_size("domain"))
    )
    received = [jnp.concatenate(pieces)]
    for s in range(1, count):
        sent = jnp.concatenate([pieces[(j + s) % count] for j in range(1, count)])
        received.append(jnp.concatenate([arrived[s], upward(sent, "band", s)]))
    return output(band, factor, received)


def solution(mesh):
    return jax.shard_map(
        shards,
        mesh=mesh,
        in_specs=(
            P("domain", "band"),
            P(),
            P("domain"),
            P("domain"),
            P("domain", None),
            P("domain"),
        ),
        out_specs=P("domain", "band"),
        check_vma=False,
    )
```

```python
import functools

import jax
import jax.numpy as jnp
from jax import lax
from jax.experimental import pallas as pl
from jax.experimental.pallas import tpu as pltpu
from jax.sharding import PartitionSpec as P

CENTER = 1.5
HALF_WIDTH = 1.25
LANES = 128
CHAINS = 4
EXACT = lax.Precision.HIGHEST
F32 = jnp.float32
BF16 = jnp.bfloat16
VM = pl.BlockSpec(memory_space=pltpu.VMEM)
SM = pl.BlockSpec(memory_space=pltpu.SMEM)
PARAMS = pltpu.CompilerParams(vmem_limit_bytes=48 << 20)


def shifted(value, axis, steps):
    count = lax.axis_size(axis)
    return lax.ppermute(value, axis, [(i, (i + steps) % count) for i in range(count)])


def spread_levels(potential_ref, block):
    return jnp.broadcast_to(potential_ref[block : block + 1, :], (LANES, LANES)).T - CENTER


def rows_out(rows_of, potential_ref, owned, base_ref, ext_ref):
    for block in range(owned // LANES):
        here = slice(block * LANES, (block + 1) * LANES)
        wide = rows_of(here)
        base_ref[here, :] = spread_levels(potential_ref, block) * wide
        ext_ref[here, :] = wide.astype(BF16).astype(F32)
    base_ref[owned:, :] = jnp.zeros_like(base_ref[owned:, :])


def prepare_kernel(nodes, rows_ref, potential_ref, base_ref, ext_ref, edge_ref, picked):
    owned = rows_ref.shape[0]
    rows_out(lambda here: rows_ref[here, :].astype(F32), potential_ref, owned, base_ref, ext_ref)

    def body(step, _):
        for k in range(16):
            i = step * 16 + k
            picked[pl.ds(i, 1), :] = ext_ref[pl.ds(nodes[i], 1), :]
        return 0

    lax.fori_loop(0, nodes.shape[0] // 16, body, 0)
    edge_ref[...] = picked[...].astype(BF16)


def prepared_shapes(owned, plane):
    return (
        jax.ShapeDtypeStruct((owned + plane, LANES), F32),
        jax.ShapeDtypeStruct((owned + plane, LANES), F32),
        jax.ShapeDtypeStruct((plane, LANES), BF16),
    )


def prepare(nodes, rows, potential):
    owned, plane = rows.shape[0], nodes.shape[0]
    return pl.pallas_call(
        prepare_kernel,
        out_shape=prepared_shapes(owned, plane),
        in_specs=[SM, VM, VM],
        out_specs=(VM, VM, VM),
        scratch_shapes=[pltpu.VMEM((plane, LANES), F32)],
        compiler_params=PARAMS,
        name="prepare",
    )(nodes, rows, potential)


def gather_cells(links, ext_ref, gathered, first):
    cells, npc = gathered.shape[0], links.shape[1]

    def cell(c, _):
        for r in range(npc):
            gathered[c, r : r + 1, :] = ext_ref[pl.ds(links[first + c, r], 1), :]
        return 0

    lax.fori_loop(0, cells, cell, 0)


def multiply_cells(scale, matrix_ref, gathered, products, first):
    cells, npc = gathered.shape[0], matrix_ref.shape[0]
    for c in range(0, cells, 2):
        both = jnp.concatenate(
            [gathered[c, 0:npc, :].astype(BF16), gathered[c + 1, 0:npc, :].astype(BF16)], axis=1
        )
        made = jnp.dot(matrix_ref[...], both, preferred_element_type=F32)
        for half in range(2):
            products[c + half, 0:npc, :] = (
                made[:, half * LANES : (half + 1) * LANES] * scale[first + c + half]
            )


def scatter_cells(links, products, sums, first):
    cells, npc = products.shape[0], links.shape[1]
    chains = len(sums)

    def cell(c, _):
        for r in range(npc):
            total = sums[r % chains]
            row = pl.ds(links[first + c, r], 1)
            total[row, :] = total[row, :] + products[c, r : r + 1, :]
        return 0

    lax.fori_loop(0, cells, cell, 0)


def near_products_kernel(links, scale, ext_ref, matrix_ref, out_ref, gathered):
    gather_cells(links, ext_ref, gathered, 0)
    multiply_cells(scale, matrix_ref, gathered, out_ref, 0)


def far_cells_kernel(
    links, scale, ext_ref, ghost_ref, matrix_ref, base_ref, out_ref, back_ref, ext, gathered,
    products, *sums
):
    owned = out_ref.shape[0]
    half = gathered.shape[0]
    ext[0:owned, :] = ext_ref[0:owned, :]
    ext[owned:, :] = ghost_ref[...].astype(F32)
    sums[0][...] = base_ref[...]
    for total in sums[1:]:
        total[...] = jnp.zeros_like(total)
    gather_cells(links, ext, gathered, half)
    multiply_cells(scale, matrix_ref, gathered, products, half)
    scatter_cells(links, products, sums, half)
    back_ref[...] = sum(total[owned:, :] for total in sums)
    out_ref[...] = sum(total[0:owned, :] for total in sums)


def near_sums_kernel(links, products_ref, start_ref, out_ref, *sums):
    sums = (out_ref,) + sums
    out_ref[...] = start_ref[...]
    for total in sums[1:]:
        total[...] = jnp.zeros_like(total)
    scatter_cells(links, products_ref, sums, 0)
    out_ref[...] = sum(total[...] for total in sums)


def cost(flops, moved):
    return pl.CostEstimate(flops=flops, bytes_accessed=moved, transcendentals=0)


def apply_operator(links, scale, matrix, base, ext, edge):
    cells, npc = links.shape
    half, padded = cells // 2, (npc + 7) // 8 * 8
    plane = edge.shape[0]
    whole = base.shape
    owned = whole[0] - plane
    held = (half, padded, LANES)
    ghost = shifted(edge, "domain", -1)
    products = pl.pallas_call(
        near_products_kernel,
        out_shape=jax.ShapeDtypeStruct(held, F32),
        in_specs=[SM, SM, VM, VM],
        out_specs=VM,
        scratch_shapes=[pltpu.VMEM(held, F32)],
        compiler_params=PARAMS,
        cost_estimate=cost(0, 14 << 20),
        name="near_products",
    )(links, scale, ext, matrix)
    ghost, products = ordered(ghost, products)
    sums, back = pl.pallas_call(
        far_cells_kernel,
        out_shape=(
            jax.ShapeDtypeStruct((owned, LANES), F32),
            jax.ShapeDtypeStruct((plane, LANES), F32),
        ),
        in_specs=[SM, SM, VM, VM, VM, VM],
        out_specs=(VM, VM),
        scratch_shapes=[pltpu.VMEM(whole, F32), pltpu.VMEM(held, F32), pltpu.VMEM(held, F32)]
        + [pltpu.VMEM(whole, F32)] * CHAINS,
        compiler_params=PARAMS,
        cost_estimate=cost(0, 28 << 20),
        name="far_cells",
    )(links, scale, ext, ghost, matrix, base)
    back = shifted(back, "domain", 1)
    sums = pl.pallas_call(
        near_sums_kernel,
        out_shape=jax.ShapeDtypeStruct((owned, LANES), F32),
        in_specs=[SM, VM, VM],
        out_specs=VM,
        scratch_shapes=[pltpu.VMEM((owned, LANES), F32)] * (CHAINS - 1),
        compiler_params=PARAMS,
        cost_estimate=cost(0, 14 << 20),
        name="near_sums",
    )(links, products, sums)
    return sums, back


def add_back(nodes, target, back_ref, factor, picked=None):
    def body(step, _):
        at = [step * 16 + k for k in range(16)]
        rows = [pl.ds(nodes[i], 1) for i in at]
        new = [target[r, :] + factor * back_ref[pl.ds(i, 1), :] for i, r in zip(at, rows)]
        for i, r, value in zip(at, rows, new):
            target[r, :] = value
            if picked is not None:
                picked[pl.ds(i, 1), :] = value
        return 0

    lax.fori_loop(0, nodes.shape[0] // 16, body, 0)


def first_kernel(nodes, sums_ref, back_ref, potential_ref, base_ref, ext_ref, edge_ref, picked, term):
    owned = sums_ref.shape[0]
    term[...] = sums_ref[...] * (1.0 / HALF_WIDTH)
    add_back(nodes, term, back_ref, 1.0 / HALF_WIDTH, picked)
    edge_ref[...] = picked[...].astype(BF16)
    rows_out(lambda here: term[here, :], potential_ref, owned, base_ref, ext_ref)


def first_term(nodes, sums, back, potential):
    owned, plane = sums.shape[0], nodes.shape[0]
    return pl.pallas_call(
        first_kernel,
        out_shape=prepared_shapes(owned, plane),
        in_specs=[SM, VM, VM, VM],
        out_specs=(VM, VM, VM),
        scratch_shapes=[pltpu.VMEM((plane, LANES), F32), pltpu.VMEM(sums.shape, F32)],
        compiler_params=PARAMS,
        name="first_term",
    )(nodes, sums, back, potential)


def second_kernel(band, nodes, sums_ref, back_ref, previous_ref, *refs):
    pieces, rest_ref, total = refs[:-2], refs[-2], refs[-1]
    total[...] = sums_ref[...] * (2.0 / HALF_WIDTH) - previous_ref[...].astype(F32)
    add_back(nodes, total, back_ref, 2.0 / HALF_WIDTH)
    count = len(pieces)
    rows = total.shape[0] // count
    for k, piece in enumerate(pieces):
        start = pl.multiple_of(lax.rem(band[0] + k, count) * rows, rows)
        part = total[pl.ds(start, rows), :].astype(BF16)
        piece[...] = part
        if k:
            rest_ref[(k - 1) * rows : k * rows, :] = part


def second_term(band, nodes, sums, back, previous, count):
    owned = sums.shape[0]
    rows = owned // count
    made = pl.pallas_call(
        second_kernel,
        out_shape=[jax.ShapeDtypeStruct((rows, LANES), BF16)] * count
        + [jax.ShapeDtypeStruct((owned - rows, LANES), BF16)],
        in_specs=[SM, SM, VM, VM, VM],
        out_specs=[VM] * (count + 1),
        scratch_shapes=[pltpu.VMEM(sums.shape, F32)],
        compiler_params=PARAMS,
        name="second_term",
    )(band, nodes, sums, back, previous)
    return made[:count], made[count]


def gram_kernel(band, *refs):
    pieces, out_ref, held = refs[:-2], refs[-2], refs[-1]
    count = len(pieces)
    for s, piece in enumerate(pieces):
        held[lax.rem(band[0] + (count - s), count)] = piece[...]
    at = 0
    for i in range(count):
        for j in range(i + 1):
            out_ref[at : at + LANES, :] = lax.dot_general(
                held[i], held[j], (((0,), (0,)), ((), ())), preferred_element_type=F32
            )
            at += LANES


def partial_gram(band, pieces):
    count = len(pieces)
    blocks = count * (count + 1) // 2
    return pl.pallas_call(
        gram_kernel,
        out_shape=jax.ShapeDtypeStruct((blocks * LANES, LANES), F32),
        in_specs=[SM] + [VM] * count,
        out_specs=VM,
        scratch_shapes=[pltpu.VMEM((count,) + pieces[0].shape, BF16)],
        compiler_params=PARAMS,
        name="partial_gram",
    )(band, *pieces)


def paired(value, axis, mask):
    count = lax.axis_size(axis)
    return lax.ppermute(value, axis, [(i, i ^ mask) for i in range(count)])


def chunk(value, count, index):
    rows = value.shape[0] // count
    return lax.dynamic_slice_in_dim(value, index * rows, rows, 0)


def reduced(value):
    me = lax.axis_index("domain")
    side, place = me % 2, me // 2
    half = chunk(value, 2, side) + paired(chunk(value, 2, 1 - side), "domain", 1)
    total = chunk(half, 4, place)
    for part in [paired(chunk(half, 4, place ^ m), "domain", 2 * m) for m in (1, 2, 3)]:
        total = total + part
    return total


def gathered_back(total):
    me = lax.axis_index("domain")
    side, place = me % 2, me // 2
    parts = jnp.stack([total] + [paired(total, "domain", 2 * m) for m in (1, 2, 3)])
    half = parts[place ^ jnp.arange(4)].reshape(-1, LANES)
    other = paired(half, "domain", 1)
    pair = jnp.where(side == 0, jnp.stack([half, other]), jnp.stack([other, half]))
    return pair.reshape(-1, LANES)


def passed_up(rests, firsts, held):
    rows = firsts[held].shape[0]
    count = lax.axis_size("band")
    onward = jnp.concatenate([rests[held][rows:], firsts[held]])
    return lax.ppermute(onward, "band", [(i, i + 1) for i in range(held, count - 1)])


def ordered(*values):
    return lax.optimization_barrier(values)


def summed_beside(gram, rests, firsts):
    count = lax.axis_size("band")
    split = lax.axis_size("domain") == 8 and count == 4
    total = reduced(gram) if split else lax.psum(gram, "domain")
    first = passed_up(rests, firsts, 0)
    total, first = ordered(total, first)
    rests.append(first)
    if split:
        for mask in (1, 2):
            total = total + paired(total, "band", mask)
    else:
        total = lax.psum(total, "band")
    for held in range(1, count - 1):
        total, rests[held] = ordered(total, rests[held])
        onward = passed_up(rests, firsts, held)
        if held == 1 and split:
            total = gathered_back(total)
        rests.append(onward)
    return total


def small_inverse(tiles, lane):
    count, tiles, done = len(tiles), list(tiles), []
    sub = lax.broadcasted_iota(jnp.int32, tiles[0].shape, 0)

    def along_lanes(tile, column):
        return jnp.broadcast_to(tile[:, column : column + 1], tile.shape)

    def along_rows(tile, row):
        return jnp.broadcast_to(tile[row : row + 1, :], tile.shape)

    for p in range(count):
        base = 8 * p
        group = (lane >= base) & (lane < base + 8)
        columns = [along_lanes(tiles[p], base + m) for m in range(8)]
        entry = {(i, j): along_rows(columns[j], i) for j in range(8) for i in range(j, 8)}
        start = jnp.where(group, (lane - base == sub).astype(F32), tiles[p])
        solved = [along_rows(start, i) for i in range(8)]
        following = None
        if p + 1 < count:
            ahead = [along_lanes(tiles[p + 1], base + m) for m in range(8)]
            following = jnp.where(group, 0.0, tiles[p + 1])
        inverse, factor = [], {}
        for j in range(8):
            pivot = 1.0 / entry[j, j]
            inverse.append(pivot)
            for i in range(j + 1, 8):
                factor[i, j] = entry[i, j] * pivot
            for i in range(j + 1, 8):
                for k in range(j + 1, i + 1):
                    entry[i, k] = entry[i, k] - factor[i, j] * entry[k, j]
                solved[i] = solved[i] - factor[i, j] * solved[j]
            if following is not None:
                scaled = ahead[j] * pivot
                following = following - scaled * solved[j]
                for m in range(j + 1, 8):
                    ahead[m] = ahead[m] - scaled * entry[m, j]
        result = solved[0] * lax.rsqrt(entry[0, 0])
        for i in range(1, 8):
            result = jnp.where(sub == i, solved[i] * lax.rsqrt(entry[i, i]), result)
        done.append(jnp.where(lane <= base + sub, result, 0.0))
        if p + 2 < count:
            back = [None] * 8
            for i in range(7, -1, -1):
                value = solved[i] * inverse[i]
                for k in range(i + 1, 8):
                    value = value - factor[k, i] * back[k]
                back[i] = value
            for i in range(p + 2, count):
                value = jnp.where(group, 0.0, tiles[i])
                for m in range(8):
                    value = value - along_lanes(tiles[i], base + m) * back[m]
                tiles[i] = value
        if following is not None:
            tiles[p + 1] = following
    return done


def exact_dot(a, b, dims=(((1,), (0,)), ((), ()))):
    return lax.dot_general(a, b, dims, precision=EXACT, preferred_element_type=F32)


def inverse_kernel(over, packed_ref, out_ref, work, small):
    size = work.shape[0]
    blocks = size // LANES
    at = 0
    for i in range(blocks):
        for j in range(i + 1):
            block = packed_ref[at : at + LANES, :] * over
            work[i * LANES : (i + 1) * LANES, j * LANES : (j + 1) * LANES] = block
            if i != j:
                work[j * LANES : (j + 1) * LANES, i * LANES : (i + 1) * LANES] = block.T
            at += LANES
    out_ref[...] = jnp.zeros_like(out_ref)
    lane = lax.broadcasted_iota(jnp.int32, (8, LANES), 1)

    def step(k, _):
        base = pl.multiple_of(k * LANES, LANES)
        tiles = [
            work[pl.ds(pl.multiple_of(base + 8 * i, 8), 8), pl.ds(base, LANES)]
            for i in range(LANES // 8)
        ]
        for i, tile in enumerate(small_inverse(tiles, lane)):
            small[8 * i : 8 * i + 8, :] = tile
        for which in range(blocks):

            @pl.when(k == which)
            def _():
                a, b = which * LANES, (which + 1) * LANES
                diagonal = small[...]
                out_ref[a:b, a:b] = diagonal
                if which:
                    left = exact_dot(diagonal, work[a:b, 0:a])
                    out_ref[a:b, 0:a] = left
                if b < size:
                    right = exact_dot(diagonal, work[a:b, b:size])
                    column = exact_dot(work[b:size, a:b], diagonal, (((1,), (1,)), ((), ())))
                    work[b:size, b:size] = work[b:size, b:size] - exact_dot(column, right)
                    work[b:size, a:b] = -exact_dot(column, diagonal)
                    if which:
                        work[b:size, 0:a] = work[b:size, 0:a] - exact_dot(column, left)

        return 0

    lax.fori_loop(0, blocks, step, 0)


def inverse_factor(packed, size, over):
    return pl.pallas_call(
        functools.partial(inverse_kernel, over),
        out_shape=jax.ShapeDtypeStruct((size, size), F32),
        in_specs=[VM],
        out_specs=VM,
        scratch_shapes=[pltpu.VMEM((size, size), F32), pltpu.VMEM((LANES, LANES), F32)],
        compiler_params=PARAMS,
        cost_estimate=cost(0, 70 << 20),
        name="inverse_factor",
    )(packed)


def output_kernel(band, factor_ref, *refs):
    out_ref, high_ref, low_ref = refs[-3:]
    count = factor_ref.shape[0] // LANES
    firsts, rests = refs[:count], refs[count:-3]
    j = pl.program_id(0)

    @pl.when(j == 0)
    def _():
        for s in range(count):
            source = band[0] - s
            column = pl.multiple_of(jnp.maximum(source, 0) * LANES, LANES)
            row = pl.multiple_of(band[0] * LANES, LANES)
            block = factor_ref[pl.ds(row, LANES), pl.ds(column, LANES)]
            block = jnp.where(source >= 0, block, 0.0)
            high = block.astype(BF16)
            high_ref[s] = high
            low_ref[s] = (block - high.astype(F32)).astype(BF16)

    def put(pieces):
        total = None
        dims = (((1,), (1,)), ((), ()))
        for s, piece in enumerate(pieces):
            for factor in (high_ref, low_ref):
                part = lax.dot_general(piece, factor[s], dims, preferred_element_type=F32)
                total = part if total is None else total + part
        out_ref[...] = total

    rows = out_ref.shape[0]

    @pl.when(j == 0)
    def _():
        put([piece[...] for piece in firsts])

    @pl.when(j > 0)
    def _():
        here = pl.ds(pl.multiple_of((j - 1) * rows, rows), rows)
        put([piece[here, :] for piece in rests])


def output(band, factor, firsts, rests):
    count = len(firsts)
    rows = firsts[0].shape[0]
    return pl.pallas_call(
        output_kernel,
        out_shape=jax.ShapeDtypeStruct((rows * count, LANES), F32),
        grid_spec=pltpu.PrefetchScalarGridSpec(
            num_scalar_prefetch=1,
            grid=(count,),
            in_specs=[VM] * (1 + 2 * count),
            out_specs=pl.BlockSpec((rows, LANES), lambda j, band: (lax.rem(band[0] + j, count), 0)),
            scratch_shapes=[pltpu.VMEM((count, LANES, LANES), BF16)] * 2,
        ),
        compiler_params=PARAMS,
        name="output",
    )(band, factor, *firsts, *rests)


def shards(states_block, cell_matrix, cell_scale, potential, connectivity, boundary_nodes):
    owned = states_block.shape[0]
    count = lax.axis_size("band")
    band = lax.axis_index("band").astype(jnp.int32).reshape(1)
    levels = potential.reshape(owned // LANES, LANES)

    operator = functools.partial(apply_operator, connectivity, cell_scale, cell_matrix)
    sums, back = operator(*prepare(boundary_nodes, states_block, levels))
    sums, back = operator(*first_term(boundary_nodes, sums, back, levels))
    pieces, rest = second_term(band, boundary_nodes, sums, back, states_block, count)

    firsts = [pieces[0]] + [shifted(pieces[s], "band", s) for s in range(1, count)]
    firsts = list(ordered(*firsts))
    rests = [rest]
    packed = summed_beside(partial_gram(band, firsts), rests, firsts)
    factor = inverse_factor(packed, count * LANES, 1.0 / (owned * lax.axis_size("domain")))
    return output(band, factor, firsts, rests)


def solution(mesh):
    return jax.shard_map(
        shards,
        mesh=mesh,
        in_specs=(
            P("domain", "band"),
            P(),
            P("domain"),
            P("domain"),
            P("domain", None),
            P("domain"),
        ),
        out_specs=P("domain", "band"),
        check_vma=False,
    )
```

```python
import functools

import jax
import jax.numpy as jnp
from jax import lax
from jax.experimental import pallas as pl
from jax.experimental.pallas import tpu as pltpu
from jax.sharding import PartitionSpec as P

CENTER = 1.5
HALF_WIDTH = 1.25
LANES = 128
CHAINS = 4
EXACT = lax.Precision.HIGHEST
F32 = jnp.float32
BF16 = jnp.bfloat16
VM = pl.BlockSpec(memory_space=pltpu.VMEM)
SM = pl.BlockSpec(memory_space=pltpu.SMEM)
PARAMS = pltpu.CompilerParams(vmem_limit_bytes=48 << 20)


def shifted(value, axis, steps):
    count = lax.axis_size(axis)
    return lax.ppermute(value, axis, [(i, (i + steps) % count) for i in range(count)])


def spread_levels(potential_ref, block):
    return jnp.broadcast_to(potential_ref[block : block + 1, :], (LANES, LANES)).T - CENTER


def rows_out(rows_of, potential_ref, owned, base_ref, ext_ref):
    for block in range(owned // LANES):
        here = slice(block * LANES, (block + 1) * LANES)
        wide = rows_of(here)
        base_ref[here, :] = spread_levels(potential_ref, block) * wide
        ext_ref[here, :] = wide.astype(BF16).astype(F32)
    base_ref[owned:, :] = jnp.zeros_like(base_ref[owned:, :])


def prepare_kernel(nodes, rows_ref, potential_ref, base_ref, ext_ref, edge_ref, picked):
    owned = rows_ref.shape[0]
    rows_out(lambda here: rows_ref[here, :].astype(F32), potential_ref, owned, base_ref, ext_ref)

    def body(step, _):
        for k in range(16):
            i = step * 16 + k
            picked[pl.ds(i, 1), :] = ext_ref[pl.ds(nodes[i], 1), :]
        return 0

    lax.fori_loop(0, nodes.shape[0] // 16, body, 0)
    edge_ref[...] = picked[...].astype(BF16)


def prepared_shapes(owned, plane):
    return (
        jax.ShapeDtypeStruct((owned + plane, LANES), F32),
        jax.ShapeDtypeStruct((owned + plane, LANES), F32),
        jax.ShapeDtypeStruct((plane, LANES), BF16),
    )


def prepare(nodes, rows, potential):
    owned, plane = rows.shape[0], nodes.shape[0]
    return pl.pallas_call(
        prepare_kernel,
        out_shape=prepared_shapes(owned, plane),
        in_specs=[SM, VM, VM],
        out_specs=(VM, VM, VM),
        scratch_shapes=[pltpu.VMEM((plane, LANES), F32)],
        compiler_params=PARAMS,
        name="prepare",
    )(nodes, rows, potential)


def gather_cells(links, ext_ref, gathered, first):
    cells, npc = gathered.shape[0], links.shape[1]

    def cell(c, _):
        for r in range(npc):
            gathered[c, r : r + 1, :] = ext_ref[pl.ds(links[first + c, r], 1), :]
        return 0

    lax.fori_loop(0, cells, cell, 0)


def multiply_cells(scale, matrix_ref, gathered, products, first):
    cells, npc = gathered.shape[0], matrix_ref.shape[0]
    for c in range(0, cells, 2):
        both = jnp.concatenate(
            [gathered[c, 0:npc, :].astype(BF16), gathered[c + 1, 0:npc, :].astype(BF16)], axis=1
        )
        made = jnp.dot(matrix_ref[...], both, preferred_element_type=F32)
        for half in range(2):
            products[c + half, 0:npc, :] = (
                made[:, half * LANES : (half + 1) * LANES] * scale[first + c + half]
            )


def scatter_cells(links, products, sums, first):
    cells, npc = products.shape[0], links.shape[1]
    chains = len(sums)

    def cell(c, _):
        for r in range(npc):
            total = sums[r % chains]
            row = pl.ds(links[first + c, r], 1)
            total[row, :] = total[row, :] + products[c, r : r + 1, :]
        return 0

    lax.fori_loop(0, cells, cell, 0)


def near_products_kernel(links, scale, ext_ref, matrix_ref, out_ref, gathered):
    gather_cells(links, ext_ref, gathered, 0)
    multiply_cells(scale, matrix_ref, gathered, out_ref, 0)


def far_cells_kernel(
    links, scale, ext_ref, ghost_ref, matrix_ref, base_ref, out_ref, back_ref, ext, gathered,
    products, *sums
):
    owned = out_ref.shape[0]
    half = gathered.shape[0]
    ext[0:owned, :] = ext_ref[0:owned, :]
    ext[owned:, :] = ghost_ref[...].astype(F32)
    sums[0][...] = base_ref[...]
    for total in sums[1:]:
        total[...] = jnp.zeros_like(total)
    gather_cells(links, ext, gathered, half)
    multiply_cells(scale, matrix_ref, gathered, products, half)
    scatter_cells(links, products, sums, half)
    back_ref[...] = sum(total[owned:, :] for total in sums)
    out_ref[...] = sum(total[0:owned, :] for total in sums)


def near_sums_kernel(links, products_ref, start_ref, out_ref, *sums):
    sums = (out_ref,) + sums
    out_ref[...] = start_ref[...]
    for total in sums[1:]:
        total[...] = jnp.zeros_like(total)
    scatter_cells(links, products_ref, sums, 0)
    out_ref[...] = sum(total[...] for total in sums)


def cost(flops, moved):
    return pl.CostEstimate(flops=flops, bytes_accessed=moved, transcendentals=0)


def apply_operator(links, scale, matrix, base, ext, edge):
    cells, npc = links.shape
    half, padded = cells // 2, (npc + 7) // 8 * 8
    plane = edge.shape[0]
    whole = base.shape
    owned = whole[0] - plane
    held = (half, padded, LANES)
    ghost = shifted(edge, "domain", -1)
    products = pl.pallas_call(
        near_products_kernel,
        out_shape=jax.ShapeDtypeStruct(held, F32),
        in_specs=[SM, SM, VM, VM],
        out_specs=VM,
        scratch_shapes=[pltpu.VMEM(held, F32)],
        compiler_params=PARAMS,
        cost_estimate=cost(0, 14 << 20),
        name="near_products",
    )(links, scale, ext, matrix)
    ghost, products = ordered(ghost, products)
    sums, back = pl.pallas_call(
        far_cells_kernel,
        out_shape=(
            jax.ShapeDtypeStruct((owned, LANES), F32),
            jax.ShapeDtypeStruct((plane, LANES), F32),
        ),
        in_specs=[SM, SM, VM, VM, VM, VM],
        out_specs=(VM, VM),
        scratch_shapes=[pltpu.VMEM(whole, F32), pltpu.VMEM(held, F32), pltpu.VMEM(held, F32)]
        + [pltpu.VMEM(whole, F32)] * CHAINS,
        compiler_params=PARAMS,
        cost_estimate=cost(0, 28 << 20),
        name="far_cells",
    )(links, scale, ext, ghost, matrix, base)
    back = shifted(back, "domain", 1)
    sums = pl.pallas_call(
        near_sums_kernel,
        out_shape=jax.ShapeDtypeStruct((owned, LANES), F32),
        in_specs=[SM, VM, VM],
        out_specs=VM,
        scratch_shapes=[pltpu.VMEM((owned, LANES), F32)] * (CHAINS - 1),
        compiler_params=PARAMS,
        cost_estimate=cost(0, 14 << 20),
        name="near_sums",
    )(links, products, sums)
    return sums, back


def add_back(nodes, target, back_ref, factor, picked=None):
    def body(step, _):
        at = [step * 16 + k for k in range(16)]
        rows = [pl.ds(nodes[i], 1) for i in at]
        new = [target[r, :] + factor * back_ref[pl.ds(i, 1), :] for i, r in zip(at, rows)]
        for i, r, value in zip(at, rows, new):
            target[r, :] = value
            if picked is not None:
                picked[pl.ds(i, 1), :] = value
        return 0

    lax.fori_loop(0, nodes.shape[0] // 16, body, 0)


def first_kernel(nodes, sums_ref, back_ref, potential_ref, base_ref, ext_ref, edge_ref, picked, term):
    owned = sums_ref.shape[0]
    term[...] = sums_ref[...] * (1.0 / HALF_WIDTH)
    add_back(nodes, term, back_ref, 1.0 / HALF_WIDTH, picked)
    edge_ref[...] = picked[...].astype(BF16)
    rows_out(lambda here: term[here, :], potential_ref, owned, base_ref, ext_ref)


def first_term(nodes, sums, back, potential):
    owned, plane = sums.shape[0], nodes.shape[0]
    return pl.pallas_call(
        first_kernel,
        out_shape=prepared_shapes(owned, plane),
        in_specs=[SM, VM, VM, VM],
        out_specs=(VM, VM, VM),
        scratch_shapes=[pltpu.VMEM((plane, LANES), F32), pltpu.VMEM(sums.shape, F32)],
        compiler_params=PARAMS,
        name="first_term",
    )(nodes, sums, back, potential)


def second_kernel(band, nodes, sums_ref, back_ref, previous_ref, *refs):
    pieces, rest_ref, total = refs[:-2], refs[-2], refs[-1]
    total[...] = sums_ref[...] * (2.0 / HALF_WIDTH) - previous_ref[...].astype(F32)
    add_back(nodes, total, back_ref, 2.0 / HALF_WIDTH)
    count = len(pieces)
    rows = total.shape[0] // count
    for k, piece in enumerate(pieces):
        start = pl.multiple_of(lax.rem(band[0] + k, count) * rows, rows)
        part = total[pl.ds(start, rows), :].astype(BF16)
        piece[...] = part
        if k:
            rest_ref[(k - 1) * rows : k * rows, :] = part


def second_term(band, nodes, sums, back, previous, count):
    owned = sums.shape[0]
    rows = owned // count
    made = pl.pallas_call(
        second_kernel,
        out_shape=[jax.ShapeDtypeStruct((rows, LANES), BF16)] * count
        + [jax.ShapeDtypeStruct((owned - rows, LANES), BF16)],
        in_specs=[SM, SM, VM, VM, VM],
        out_specs=[VM] * (count + 1),
        scratch_shapes=[pltpu.VMEM(sums.shape, F32)],
        compiler_params=PARAMS,
        name="second_term",
    )(band, nodes, sums, back, previous)
    return made[:count], made[count]


def gram_kernel(band, *refs):
    pieces, out_ref, held = refs[:-2], refs[-2], refs[-1]
    count = len(pieces)
    for s, piece in enumerate(pieces):
        held[lax.rem(band[0] + (count - s), count)] = piece[...]
    at = 0
    for i in range(count):
        for j in range(i + 1):
            out_ref[at : at + LANES, :] = lax.dot_general(
                held[i], held[j], (((0,), (0,)), ((), ())), preferred_element_type=F32
            )
            at += LANES


def partial_gram(band, pieces):
    count = len(pieces)
    blocks = count * (count + 1) // 2
    return pl.pallas_call(
        gram_kernel,
        out_shape=jax.ShapeDtypeStruct((blocks * LANES, LANES), F32),
        in_specs=[SM] + [VM] * count,
        out_specs=VM,
        scratch_shapes=[pltpu.VMEM((count,) + pieces[0].shape, BF16)],
        compiler_params=PARAMS,
        name="partial_gram",
    )(band, *pieces)


def paired(value, axis, mask):
    count = lax.axis_size(axis)
    return lax.ppermute(value, axis, [(i, i ^ mask) for i in range(count)])


def chunk(value, count, index):
    rows = value.shape[0] // count
    return lax.dynamic_slice_in_dim(value, index * rows, rows, 0)


def reduced(value):
    me = lax.axis_index("domain")
    side, place = me % 2, me // 2
    half = chunk(value, 2, side) + paired(chunk(value, 2, 1 - side), "domain", 1)
    total = chunk(half, 4, place)
    for part in [paired(chunk(half, 4, place ^ m), "domain", 2 * m) for m in (1, 2, 3)]:
        total = total + part
    return total


def gathered_back(total):
    me = lax.axis_index("domain")
    side, place = me % 2, me // 2
    parts = jnp.stack([total] + [paired(total, "domain", 2 * m) for m in (1, 2, 3)])
    half = parts[place ^ jnp.arange(4)].reshape(-1, LANES)
    other = paired(half, "domain", 1)
    pair = jnp.where(side == 0, jnp.stack([half, other]), jnp.stack([other, half]))
    return pair.reshape(-1, LANES)


def passed_up(rests, firsts, held):
    rows = firsts[held].shape[0]
    count = lax.axis_size("band")
    onward = jnp.concatenate([rests[held][rows:], firsts[held]])
    return lax.ppermute(onward, "band", [(i, i + 1) for i in range(held, count - 1)])


def ordered(*values):
    return lax.optimization_barrier(values)


def summed_beside(gram, rests, firsts):
    count = lax.axis_size("band")
    if lax.axis_size("domain") != 8 or count != 4:
        for held in range(count - 1):
            rests.append(passed_up(rests, firsts, held))
        return lax.psum(gram, ("domain", "band"))
    rests.append(passed_up(rests, firsts, 0))
    total = reduced(gram)
    total = total + paired(total, "band", 1)
    total, rests[1] = ordered(total, rests[1])
    rests.append(passed_up(rests, firsts, 1))
    total = total + paired(total, "band", 2)
    total = gathered_back(total)
    total, rests[2] = ordered(total, rests[2])
    rests.append(passed_up(rests, firsts, 2))
    return total


def small_inverse(tiles, lane):
    count, tiles, done = len(tiles), list(tiles), []
    sub = lax.broadcasted_iota(jnp.int32, tiles[0].shape, 0)

    def along_lanes(tile, column):
        return jnp.broadcast_to(tile[:, column : column + 1], tile.shape)

    def along_rows(tile, row):
        return jnp.broadcast_to(tile[row : row + 1, :], tile.shape)

    for p in range(count):
        base = 8 * p
        group = (lane >= base) & (lane < base + 8)
        columns = [along_lanes(tiles[p], base + m) for m in range(8)]
        entry = {(i, j): along_rows(columns[j], i) for j in range(8) for i in range(j, 8)}
        start = jnp.where(group, (lane - base == sub).astype(F32), tiles[p])
        solved = [along_rows(start, i) for i in range(8)]
        following = None
        if p + 1 < count:
            ahead = [along_lanes(tiles[p + 1], base + m) for m in range(8)]
            following = jnp.where(group, 0.0, tiles[p + 1])
        inverse, factor = [], {}
        for j in range(8):
            pivot = 1.0 / entry[j, j]
            inverse.append(pivot)
            for i in range(j + 1, 8):
                factor[i, j] = entry[i, j] * pivot
            for i in range(j + 1, 8):
                for k in range(j + 1, i + 1):
                    entry[i, k] = entry[i, k] - factor[i, j] * entry[k, j]
                solved[i] = solved[i] - factor[i, j] * solved[j]
            if following is not None:
                scaled = ahead[j] * pivot
                following = following - scaled * solved[j]
                for m in range(j + 1, 8):
                    ahead[m] = ahead[m] - scaled * entry[m, j]
        result = solved[0] * lax.rsqrt(entry[0, 0])
        for i in range(1, 8):
            result = jnp.where(sub == i, solved[i] * lax.rsqrt(entry[i, i]), result)
        done.append(jnp.where(lane <= base + sub, result, 0.0))
        if p + 2 < count:
            back = [None] * 8
            for i in range(7, -1, -1):
                value = solved[i] * inverse[i]
                for k in range(i + 1, 8):
                    value = value - factor[k, i] * back[k]
                back[i] = value
            for i in range(p + 2, count):
                value = jnp.where(group, 0.0, tiles[i])
                for m in range(8):
                    value = value - along_lanes(tiles[i], base + m) * back[m]
                tiles[i] = value
        if following is not None:
            tiles[p + 1] = following
    return done


def exact_dot(a, b, dims=(((1,), (0,)), ((), ()))):
    return lax.dot_general(a, b, dims, precision=EXACT, preferred_element_type=F32)


def inverse_kernel(over, packed_ref, out_ref, work, small):
    size = work.shape[0]
    blocks = size // LANES
    at = 0
    for i in range(blocks):
        for j in range(i + 1):
            block = packed_ref[at : at + LANES, :] * over
            work[i * LANES : (i + 1) * LANES, j * LANES : (j + 1) * LANES] = block
            if i != j:
                work[j * LANES : (j + 1) * LANES, i * LANES : (i + 1) * LANES] = block.T
            at += LANES
    out_ref[...] = jnp.zeros_like(out_ref)
    lane = lax.broadcasted_iota(jnp.int32, (8, LANES), 1)

    def step(k, _):
        base = pl.multiple_of(k * LANES, LANES)
        tiles = [
            work[pl.ds(pl.multiple_of(base + 8 * i, 8), 8), pl.ds(base, LANES)]
            for i in range(LANES // 8)
        ]
        for i, tile in enumerate(small_inverse(tiles, lane)):
            small[8 * i : 8 * i + 8, :] = tile
        for which in range(blocks):

            @pl.when(k == which)
            def _():
                a, b = which * LANES, (which + 1) * LANES
                diagonal = small[...]
                out_ref[a:b, a:b] = diagonal
                if which:
                    left = exact_dot(diagonal, work[a:b, 0:a])
                    out_ref[a:b, 0:a] = left
                if b < size:
                    right = exact_dot(diagonal, work[a:b, b:size])
                    column = exact_dot(work[b:size, a:b], diagonal, (((1,), (1,)), ((), ())))
                    work[b:size, b:size] = work[b:size, b:size] - exact_dot(column, right)
                    work[b:size, a:b] = -exact_dot(column, diagonal)
                    if which:
                        work[b:size, 0:a] = work[b:size, 0:a] - exact_dot(column, left)

        return 0

    lax.fori_loop(0, blocks, step, 0)


def inverse_factor(packed, size, over):
    return pl.pallas_call(
        functools.partial(inverse_kernel, over),
        out_shape=jax.ShapeDtypeStruct((size, size), F32),
        in_specs=[VM],
        out_specs=VM,
        scratch_shapes=[pltpu.VMEM((size, size), F32), pltpu.VMEM((LANES, LANES), F32)],
        compiler_params=PARAMS,
        cost_estimate=cost(0, 70 << 20),
        name="inverse_factor",
    )(packed)


def output_kernel(band, factor_ref, *refs):
    out_ref, high_ref, low_ref = refs[-3:]
    count = factor_ref.shape[0] // LANES
    firsts, rests = refs[:count], refs[count:-3]
    j = pl.program_id(0)

    @pl.when(j == 0)
    def _():
        for s in range(count):
            source = band[0] - s
            column = pl.multiple_of(jnp.maximum(source, 0) * LANES, LANES)
            row = pl.multiple_of(band[0] * LANES, LANES)
            block = factor_ref[pl.ds(row, LANES), pl.ds(column, LANES)]
            block = jnp.where(source >= 0, block, 0.0)
            high = block.astype(BF16)
            high_ref[s] = high
            low_ref[s] = (block - high.astype(F32)).astype(BF16)

    def put(pieces):
        total = None
        dims = (((1,), (1,)), ((), ()))
        for s, piece in enumerate(pieces):
            for factor in (high_ref, low_ref):
                part = lax.dot_general(piece, factor[s], dims, preferred_element_type=F32)
                total = part if total is None else total + part
        out_ref[...] = total

    rows = out_ref.shape[0]

    @pl.when(j == 0)
    def _():
        put([piece[...] for piece in firsts])

    @pl.when(j > 0)
    def _():
        here = pl.ds(pl.multiple_of((j - 1) * rows, rows), rows)
        put([piece[here, :] for piece in rests])


def output(band, factor, firsts, rests):
    count = len(firsts)
    rows = firsts[0].shape[0]
    return pl.pallas_call(
        output_kernel,
        out_shape=jax.ShapeDtypeStruct((rows * count, LANES), F32),
        grid_spec=pltpu.PrefetchScalarGridSpec(
            num_scalar_prefetch=1,
            grid=(count,),
            in_specs=[VM] * (1 + 2 * count),
            out_specs=pl.BlockSpec((rows, LANES), lambda j, band: (lax.rem(band[0] + j, count), 0)),
            scratch_shapes=[pltpu.VMEM((count, LANES, LANES), BF16)] * 2,
        ),
        compiler_params=PARAMS,
        name="output",
    )(band, factor, *firsts, *rests)


def shards(states_block, cell_matrix, cell_scale, potential, connectivity, boundary_nodes):
    owned = states_block.shape[0]
    count = lax.axis_size("band")
    band = lax.axis_index("band").astype(jnp.int32).reshape(1)
    levels = potential.reshape(owned // LANES, LANES)

    operator = functools.partial(apply_operator, connectivity, cell_scale, cell_matrix)
    sums, back = operator(*prepare(boundary_nodes, states_block, levels))
    sums, back = operator(*first_term(boundary_nodes, sums, back, levels))
    pieces, rest = second_term(band, boundary_nodes, sums, back, states_block, count)

    firsts = [pieces[0]] + [shifted(pieces[s], "band", s) for s in range(1, count)]
    firsts = list(ordered(*firsts))
    rests = [rest]
    packed = summed_beside(partial_gram(band, firsts), rests, firsts)
    factor = inverse_factor(packed, count * LANES, 1.0 / (owned * lax.axis_size("domain")))
    return output(band, factor, firsts, rests)


def solution(mesh):
    return jax.shard_map(
        shards,
        mesh=mesh,
        in_specs=(
            P("domain", "band"),
            P(),
            P("domain"),
            P("domain"),
            P("domain", None),
            P("domain"),
        ),
        out_specs=P("domain", "band"),
        check_vma=False,
    )
```

```python
import functools

import jax
import jax.numpy as jnp
from jax import lax
from jax.experimental import pallas as pl
from jax.experimental.pallas import tpu as pltpu
from jax.sharding import PartitionSpec as P

CENTER = 1.5
HALF_WIDTH = 1.25
LANES = 128
CHAINS = 6
F32 = jnp.float32
BF16 = jnp.bfloat16
VM = pl.BlockSpec(memory_space=pltpu.VMEM)
SM = pl.BlockSpec(memory_space=pltpu.SMEM)


def params(mebibytes):
    return pltpu.CompilerParams(vmem_limit_bytes=mebibytes << 20)


def cost(flops, moved):
    return pl.CostEstimate(flops=flops, bytes_accessed=moved, transcendentals=0)


def shifted(value, axis, steps):
    count = lax.axis_size(axis)
    return lax.ppermute(value, axis, [(i, (i + steps) % count) for i in range(count)])


def spread_levels(potential_ref, block):
    return jnp.broadcast_to(potential_ref[block : block + 1, :], (LANES, LANES)).T - CENTER


def rows_out(rows_of, potential_ref, owned, base_ref, ext_ref):
    for block in range(owned // LANES):
        here = slice(block * LANES, (block + 1) * LANES)
        wide = rows_of(here)
        base_ref[here, :] = spread_levels(potential_ref, block) * wide
        ext_ref[here, :] = wide.astype(BF16).astype(F32)
    base_ref[owned:, :] = jnp.zeros_like(base_ref[owned:, :])


def prepare_kernel(nodes, rows_ref, ext_ref, edge_ref, picked):
    owned = rows_ref.shape[0]
    ext_ref[0:owned, :] = rows_ref[...].astype(F32)

    def body(step, _):
        for k in range(16):
            i = step * 16 + k
            picked[pl.ds(i, 1), :] = ext_ref[pl.ds(nodes[i], 1), :]
        return 0

    lax.fori_loop(0, nodes.shape[0] // 16, body, 0)
    edge_ref[...] = picked[...].astype(BF16)


def prepare(nodes, rows):
    owned, plane = rows.shape[0], nodes.shape[0]
    ext, edge = pl.pallas_call(
        prepare_kernel,
        out_shape=(
            jax.ShapeDtypeStruct((owned + plane, LANES), F32),
            jax.ShapeDtypeStruct((plane, LANES), BF16),
        ),
        in_specs=[SM, VM],
        out_specs=(VM, VM),
        scratch_shapes=[pltpu.VMEM((plane, LANES), F32)],
        compiler_params=params(8),
        cost_estimate=cost(0, 12 << 20),
        name="prepare",
    )(nodes, rows)
    return ext, ext, edge


def gather_cells(links, npc, ext_ref, gathered, first):
    def cell(c, _):
        base = (first + c) * npc
        for r in range(npc):
            gathered[c, r : r + 1, :] = ext_ref[pl.ds(links[base + r], 1), :]
        return 0

    lax.fori_loop(0, gathered.shape[0], cell, 0)


def multiply_cells(scale, matrix_ref, gathered, products, first):
    cells, npc = gathered.shape[0], matrix_ref.shape[0]
    for c in range(0, cells, 2):
        both = jnp.concatenate(
            [gathered[c, 0:npc, :].astype(BF16), gathered[c + 1, 0:npc, :].astype(BF16)], axis=1
        )
        made = jnp.dot(matrix_ref[...], both, preferred_element_type=F32)
        for half in range(2):
            products[c + half, 0:npc, :] = (
                made[:, half * LANES : (half + 1) * LANES] * scale[first + c + half]
            )


def scatter_cells(links, npc, products, sums, first):
    chains = len(sums)

    def cell(c, _):
        base = (first + c) * npc
        for r in range(npc):
            total = sums[r % chains]
            row = pl.ds(links[base + r], 1)
            total[row, :] = total[row, :] + products[c, r : r + 1, :]
        return 0

    lax.fori_loop(0, products.shape[0], cell, 0)


def near_products_kernel(links, scale, ext_ref, matrix_ref, out_ref, gathered):
    gather_cells(links, matrix_ref.shape[0], ext_ref, gathered, 0)
    multiply_cells(scale, matrix_ref, gathered, out_ref, 0)


def far_cells_kernel(
    links, scale, ext_ref, ghost_ref, matrix_ref, wide_ref, potential_ref, out_ref, back_ref, ext, gathered,
    products, *sums
):
    owned = out_ref.shape[0]
    half = gathered.shape[0]
    ext[0:owned, :] = ext_ref[0:owned, :]
    ext[owned:, :] = ghost_ref[...].astype(F32)
    for block in range(owned // LANES):
        here = slice(block * LANES, (block + 1) * LANES)
        sums[0][here, :] = spread_levels(potential_ref, block) * wide_ref[here, :]
    sums[0][owned:, :] = jnp.zeros_like(sums[0][owned:, :])
    for total in sums[1:]:
        total[...] = jnp.zeros_like(total)
    npc = matrix_ref.shape[0]
    gather_cells(links, npc, ext, gathered, half)
    multiply_cells(scale, matrix_ref, gathered, products, half)
    scatter_cells(links, npc, products, sums, half)
    back_ref[...] = sum(total[owned:, :] for total in sums)
    out_ref[...] = sum(total[0:owned, :] for total in sums)


def near_sums_kernel(npc, links, products_ref, start_ref, out_ref, *sums):
    sums = (out_ref,) + sums
    out_ref[...] = start_ref[...]
    for total in sums[1:]:
        total[...] = jnp.zeros_like(total)
    scatter_cells(links, npc, products_ref, sums, 0)
    out_ref[...] = sum(total[...] for total in sums)


def apply_operator(links, scale, matrix, potential, wide, ext, edge):
    cells, npc = scale.shape[0], matrix.shape[0]
    half, padded = cells // 2, (npc + 7) // 8 * 8
    plane = edge.shape[0]
    whole = ext.shape
    owned = whole[0] - plane
    held = (half, padded, LANES)
    ghost = shifted(edge, "domain", -1)
    products = pl.pallas_call(
        near_products_kernel,
        out_shape=jax.ShapeDtypeStruct(held, F32),
        in_specs=[SM, SM, VM, VM],
        out_specs=VM,
        scratch_shapes=[pltpu.VMEM(held, F32)],
        compiler_params=params(16),
        cost_estimate=cost(0, 14 << 20),
        name="near_products",
    )(links, scale, ext, matrix)
    ghost, products = ordered(ghost, products)
    sums, back = pl.pallas_call(
        far_cells_kernel,
        out_shape=(
            jax.ShapeDtypeStruct((owned, LANES), F32),
            jax.ShapeDtypeStruct((plane, LANES), F32),
        ),
        in_specs=[SM, SM, VM, VM, VM, VM, VM],
        out_specs=(VM, VM),
        scratch_shapes=[pltpu.VMEM(whole, F32), pltpu.VMEM(held, F32), pltpu.VMEM(held, F32)]
        + [pltpu.VMEM(whole, F32)] * CHAINS,
        compiler_params=params(22),
        cost_estimate=cost(0, 28 << 20),
        name="far_cells",
    )(links, scale, ext, ghost, matrix, wide, potential)
    back = shifted(back, "domain", 1)
    sums = pl.pallas_call(
        functools.partial(near_sums_kernel, npc),
        out_shape=jax.ShapeDtypeStruct((owned, LANES), F32),
        in_specs=[SM, VM, VM],
        out_specs=VM,
        scratch_shapes=[pltpu.VMEM((owned, LANES), F32)] * (CHAINS - 1),
        compiler_params=params(16),
        cost_estimate=cost(0, 14 << 20),
        name="near_sums",
    )(links, products, sums)
    return sums, back


def add_back(nodes, target, back_ref, factor, picked=None):
    def body(step, _):
        at = [step * 16 + k for k in range(16)]
        rows = [pl.ds(nodes[i], 1) for i in at]
        new = [target[r, :] + factor * back_ref[pl.ds(i, 1), :] for i, r in zip(at, rows)]
        for i, r, value in zip(at, rows, new):
            target[r, :] = value
            if picked is not None:
                picked[pl.ds(i, 1), :] = value
        return 0

    lax.fori_loop(0, nodes.shape[0] // 16, body, 0)


def first_kernel(nodes, sums_ref, back_ref, term_ref, ext_ref, edge_ref, picked):
    owned = sums_ref.shape[0]
    term_ref[...] = sums_ref[...] * (1.0 / HALF_WIDTH)
    add_back(nodes, term_ref, back_ref, 1.0 / HALF_WIDTH, picked)
    edge_ref[...] = picked[...].astype(BF16)
    ext_ref[0:owned, :] = term_ref[...].astype(BF16).astype(F32)


def first_term(nodes, sums, back):
    owned, plane = sums.shape[0], nodes.shape[0]
    return pl.pallas_call(
        first_kernel,
        out_shape=(
            jax.ShapeDtypeStruct((owned, LANES), F32),
            jax.ShapeDtypeStruct((owned + plane, LANES), F32),
            jax.ShapeDtypeStruct((plane, LANES), BF16),
        ),
        in_specs=[SM, VM, VM],
        out_specs=(VM, VM, VM),
        scratch_shapes=[pltpu.VMEM((plane, LANES), F32)],
        compiler_params=params(16),
        cost_estimate=cost(0, 8 << 20),
        name="first_term",
    )(nodes, sums, back)


def second_kernel(band, nodes, sums_ref, back_ref, previous_ref, *refs):
    pieces, rest_ref, total = refs[:-2], refs[-2], refs[-1]
    total[...] = sums_ref[...] * (2.0 / HALF_WIDTH) - previous_ref[...].astype(F32)
    add_back(nodes, total, back_ref, 2.0 / HALF_WIDTH)
    count = len(pieces)
    rows = total.shape[0] // count
    for k, piece in enumerate(pieces):
        start = pl.multiple_of(lax.rem(band[0] + k, count) * rows, rows)
        part = total[pl.ds(start, rows), :].astype(BF16)
        piece[...] = part
        if k:
            rest_ref[(k - 1) * rows : k * rows, :] = part


def second_term(band, nodes, sums, back, previous, count):
    owned = sums.shape[0]
    rows = owned // count
    made = pl.pallas_call(
        second_kernel,
        out_shape=[jax.ShapeDtypeStruct((rows, LANES), BF16)] * count
        + [jax.ShapeDtypeStruct((owned - rows, LANES), BF16)],
        in_specs=[SM, SM, VM, VM, VM],
        out_specs=[VM] * (count + 1),
        scratch_shapes=[pltpu.VMEM(sums.shape, F32)],
        compiler_params=params(16),
        cost_estimate=cost(0, 6 << 20),
        name="second_term",
    )(band, nodes, sums, back, previous)
    return made[:count], made[count]


def gram_kernel(band, *refs):
    pieces, out_ref, held = refs[:-2], refs[-2], refs[-1]
    count = len(pieces)
    for s, piece in enumerate(pieces):
        held[lax.rem(band[0] + (count - s), count)] = piece[...]
    at = 0
    for i in range(count):
        for j in range(i + 1):
            out_ref[at : at + LANES, :] = lax.dot_general(
                held[i], held[j], (((0,), (0,)), ((), ())), preferred_element_type=F32
            )
            at += LANES


def partial_gram(band, pieces):
    count = len(pieces)
    blocks = count * (count + 1) // 2
    return pl.pallas_call(
        gram_kernel,
        out_shape=jax.ShapeDtypeStruct((blocks * LANES, LANES), F32),
        in_specs=[SM] + [VM] * count,
        out_specs=VM,
        scratch_shapes=[pltpu.VMEM((count,) + pieces[0].shape, BF16)],
        compiler_params=params(16),
        cost_estimate=cost(0, 4 << 20),
        name="partial_gram",
    )(band, *pieces)


def paired(value, axis, mask):
    count = lax.axis_size(axis)
    return lax.ppermute(value, axis, [(i, i ^ mask) for i in range(count)])


def chunk(value, count, index):
    rows = value.shape[0] // count
    return lax.dynamic_slice_in_dim(value, index * rows, rows, 0)


def reduced(value):
    me = lax.axis_index("domain")
    side, place = me % 2, me // 2
    half = chunk(value, 2, side) + paired(chunk(value, 2, 1 - side), "domain", 1)
    total = chunk(half, 4, place)
    for part in [paired(chunk(half, 4, place ^ m), "domain", 2 * m) for m in (1, 2, 3)]:
        total = total + part
    return total


def gathered_back(total):
    me = lax.axis_index("domain")
    side, place = me % 2, me // 2
    parts = jnp.stack([total] + [paired(total, "domain", 2 * m) for m in (1, 2, 3)])
    half = parts[place ^ jnp.arange(4)].reshape(-1, LANES)
    other = paired(half, "domain", 1)
    pair = jnp.where(side == 0, jnp.stack([half, other]), jnp.stack([other, half]))
    return pair.reshape(-1, LANES)


def passed_up(rests, firsts, held):
    rows = firsts[held].shape[0]
    count = lax.axis_size("band")
    onward = jnp.concatenate([rests[held][rows:], firsts[held]])
    return lax.ppermute(onward, "band", [(i, i + 1) for i in range(held, count - 1)])


def ordered(*values):
    return lax.optimization_barrier(values)


def summed_beside(gram, rests, firsts):
    count = lax.axis_size("band")
    if lax.axis_size("domain") != 8 or count != 4:
        for held in range(count - 1):
            rests.append(passed_up(rests, firsts, held))
        return lax.psum(gram, ("domain", "band"))
    rests.append(passed_up(rests, firsts, 0))
    total = reduced(gram)
    total = total + paired(total, "band", 1)
    total, rests[1] = ordered(total, rests[1])
    rests.append(passed_up(rests, firsts, 1))
    total = total + paired(total, "band", 2)
    total = gathered_back(total)
    total, rests[2] = ordered(total, rests[2])
    rests.append(passed_up(rests, firsts, 2))
    return total


def split_dot(a, b, dims=(((1,), (0,)), ((), ()))):
    def parts(x):
        high = x.astype(BF16)
        return high, (x - high.astype(F32)).astype(BF16)

    def dot(x, y):
        return lax.dot_general(x, y, dims, preferred_element_type=F32)

    (a_high, a_low), (b_high, b_low) = parts(a), parts(b)
    return dot(a_high, b_high) + (dot(a_high, b_low) + dot(a_low, b_high))


def small_inverse(tiles, lane):
    count, tiles, done = len(tiles), list(tiles), []
    shape = tiles[0].shape
    sub = lax.broadcasted_iota(jnp.int32, shape, 0)

    def along_lanes(tile, column):
        return jnp.broadcast_to(tile[:, column : column + 1], shape)

    def along_rows(tile, row):
        return jnp.broadcast_to(tile[row : row + 1, :], shape)

    def stacked(rows):
        tile = rows[0]
        for i in range(1, 8):
            tile = jnp.where(sub == i, rows[i], tile)
        return tile

    columns = [along_lanes(tiles[0], m) for m in range(8)]
    for p in range(count):
        base = 8 * p
        group = (lane >= base) & (lane < base + 8)
        entry = {(i, j): along_rows(columns[j], i) for j in range(8) for i in range(j, 8)}
        start = jnp.where(group, (lane - base == sub).astype(F32), tiles[p])
        solved = [along_rows(start, i) for i in range(8)]
        following = None
        if p + 1 < count:
            ahead = [along_lanes(tiles[p + 1], base + m) for m in range(8)]
            columns = [along_lanes(tiles[p + 1], base + 8 + m) for m in range(8)]
            following = jnp.where(group, 0.0, tiles[p + 1])
        inverse, factor = [], {}
        for j in range(8):
            pivot = 1.0 / entry[j, j]
            inverse.append(pivot)
            if following is not None:
                scaled = ahead[j] * pivot
                columns = [c - scaled * along_rows(ahead[j], m) for m, c in enumerate(columns)]
                following = following - scaled * solved[j]
                for m in range(j + 1, 8):
                    ahead[m] = ahead[m] - scaled * entry[m, j]
            for i in range(j + 1, 8):
                factor[i, j] = entry[i, j] * pivot
            for i in range(j + 1, 8):
                for k in range(j + 1, i + 1):
                    entry[i, k] = entry[i, k] - factor[i, j] * entry[k, j]
                solved[i] = solved[i] - factor[i, j] * solved[j]
        result = stacked([solved[i] * lax.rsqrt(entry[i, i]) for i in range(8)])
        done.append(jnp.where(lane <= base + sub, result, 0.0))
        if p + 2 < count:
            back = [None] * 8
            for i in range(7, -1, -1):
                value = solved[i] * inverse[i]
                for k in range(i + 1, 8):
                    value = value - factor[k, i] * back[k]
                back[i] = value
            value = jnp.where(group, 0.0, tiles[p + 2])
            for m in range(8):
                value = value - along_lanes(tiles[p + 2], base + m) * back[m]
            tiles[p + 2] = value
            if p + 3 < count:
                spread = [stacked(back), jnp.zeros((LANES - 8 - base, LANES), F32)]
                if base:
                    spread = [jnp.zeros((base, LANES), F32)] + spread
                made = split_dot(
                    jnp.concatenate(tiles[p + 3 :], axis=0), jnp.concatenate(spread, axis=0)
                )
                for i in range(p + 3, count):
                    row = 8 * (i - p - 3)
                    tiles[i] = jnp.where(group, 0.0, tiles[i]) - made[row : row + 8, :]
        if following is not None:
            tiles[p + 1] = following
    return done


def inverse_kernel(over, packed_ref, out_ref, work, small):
    size = work.shape[0]
    blocks = size // LANES
    at = 0
    for i in range(blocks):
        for j in range(i + 1):
            block = packed_ref[at : at + LANES, :] * over
            work[i * LANES : (i + 1) * LANES, j * LANES : (j + 1) * LANES] = block
            if i != j:
                work[j * LANES : (j + 1) * LANES, i * LANES : (i + 1) * LANES] = block.T
            at += LANES
    out_ref[...] = jnp.zeros_like(out_ref)
    lane = lax.broadcasted_iota(jnp.int32, (8, LANES), 1)

    def step(k, _):
        base = pl.multiple_of(k * LANES, LANES)
        tiles = [
            work[pl.ds(pl.multiple_of(base + 8 * i, 8), 8), pl.ds(base, LANES)]
            for i in range(LANES // 8)
        ]
        for i, tile in enumerate(small_inverse(tiles, lane)):
            small[8 * i : 8 * i + 8, :] = tile
        for which in range(blocks):

            @pl.when(k == which)
            def _():
                a, b = which * LANES, (which + 1) * LANES
                diagonal = small[...]
                out_ref[a:b, a:b] = diagonal
                if which:
                    left = split_dot(diagonal, work[a:b, 0:a])
                    out_ref[a:b, 0:a] = left
                if b < size:
                    right = split_dot(diagonal, work[a:b, b:size])
                    column = split_dot(work[b:size, a:b], diagonal, (((1,), (1,)), ((), ())))
                    work[b:size, b:size] = work[b:size, b:size] - split_dot(column, right)
                    work[b:size, a:b] = -split_dot(column, diagonal)
                    if which:
                        work[b:size, 0:a] = work[b:size, 0:a] - split_dot(column, left)

        return 0

    lax.fori_loop(0, blocks, step, 0)


def inverse_factor(packed, size, over):
    return pl.pallas_call(
        functools.partial(inverse_kernel, over),
        out_shape=jax.ShapeDtypeStruct((size, size), F32),
        in_specs=[VM],
        out_specs=VM,
        scratch_shapes=[pltpu.VMEM((size, size), F32), pltpu.VMEM((LANES, LANES), F32)],
        compiler_params=params(16),
        cost_estimate=cost(0, 70 << 20),
        name="inverse_factor",
    )(packed)


def output_kernel(band, factor_ref, *refs):
    out_ref, blocks_ref = refs[-2:]
    count = factor_ref.shape[0] // LANES
    firsts, rests = refs[:count], refs[count:-2]
    j = pl.program_id(0)

    @pl.when(j == 0)
    def _():
        row = pl.ds(pl.multiple_of(band[0] * LANES, LANES), LANES)
        for s in range(count):
            source = band[0] - s
            column = pl.ds(pl.multiple_of(jnp.maximum(source, 0) * LANES, LANES), LANES)
            block = jnp.where(source >= 0, factor_ref[row, column], 0.0).T
            high = block.astype(BF16)
            here = slice(s * LANES, (s + 1) * LANES)
            blocks_ref[here, 0:LANES] = high
            blocks_ref[here, LANES:] = (block - high.astype(F32)).astype(BF16)

    def put(pieces):
        rows = jnp.concatenate(pieces, axis=1)
        made = jnp.dot(rows, blocks_ref[...], preferred_element_type=F32)
        out_ref[...] = made[:, 0:LANES] + made[:, LANES:]

    rows = out_ref.shape[0]

    @pl.when(j == 0)
    def _():
        put([piece[...] for piece in firsts])

    @pl.when(j > 0)
    def _():
        here = pl.ds(pl.multiple_of((j - 1) * rows, rows), rows)
        put([piece[here, :] for piece in rests])


def output(band, factor, firsts, rests):
    count = len(firsts)
    rows = firsts[0].shape[0]
    return pl.pallas_call(
        output_kernel,
        out_shape=jax.ShapeDtypeStruct((rows * count, LANES), F32),
        grid_spec=pltpu.PrefetchScalarGridSpec(
            num_scalar_prefetch=1,
            grid=(count,),
            in_specs=[VM] * (1 + 2 * count),
            out_specs=pl.BlockSpec((rows, LANES), lambda j, band: (lax.rem(band[0] + j, count), 0)),
            scratch_shapes=[pltpu.VMEM((count * LANES, 2 * LANES), BF16)],
        ),
        compiler_params=params(24),
        cost_estimate=cost(0, 10 << 20),
        name="output",
    )(band, factor, *firsts, *rests)


def shards(states_block, cell_matrix, cell_scale, potential, connectivity, boundary_nodes):
    owned = states_block.shape[0]
    count = lax.axis_size("band")
    band = lax.axis_index("band").astype(jnp.int32).reshape(1)
    levels = potential.reshape(owned // LANES, LANES)

    operator = functools.partial(
        apply_operator, connectivity.reshape(-1), cell_scale, cell_matrix, levels
    )
    sums, back = operator(*prepare(boundary_nodes, states_block))
    sums, back = operator(*first_term(boundary_nodes, sums, back))
    pieces, rest = second_term(band, boundary_nodes, sums, back, states_block, count)

    firsts = [pieces[0]] + [shifted(pieces[s], "band", s) for s in range(1, count)]
    firsts = list(ordered(*firsts))
    rests = [rest]
    packed = summed_beside(partial_gram(band, firsts), rests, firsts)
    factor = inverse_factor(packed, count * LANES, 1.0 / (owned * lax.axis_size("domain")))
    return output(band, factor, firsts, rests)


def solution(mesh):
    return jax.shard_map(
        shards,
        mesh=mesh,
        in_specs=(
            P("domain", "band"),
            P(),
            P("domain"),
            P("domain"),
            P("domain", None),
            P("domain"),
        ),
        out_specs=P("domain", "band"),
        check_vma=False,
    )
```

```python
import functools

import jax
import jax.numpy as jnp
from jax import lax
from jax.experimental import pallas as pl
from jax.experimental.pallas import tpu as pltpu
from jax.sharding import PartitionSpec as P

CENTER = 1.5
HALF_WIDTH = 1.25
LANES = 128
CHAINS = 6
F32 = jnp.float32
BF16 = jnp.bfloat16
VM = pl.BlockSpec(memory_space=pltpu.VMEM)
SM = pl.BlockSpec(memory_space=pltpu.SMEM)


def params(mebibytes):
    return pltpu.CompilerParams(vmem_limit_bytes=mebibytes << 20)


def cost(flops, moved):
    return pl.CostEstimate(flops=flops, bytes_accessed=moved, transcendentals=0)


def shifted(value, axis, steps):
    count = lax.axis_size(axis)
    return lax.ppermute(value, axis, [(i, (i + steps) % count) for i in range(count)])


def spread_levels(potential_ref, block):
    return jnp.broadcast_to(potential_ref[block : block + 1, :], (LANES, LANES)).T - CENTER


def rows_out(rows_of, potential_ref, owned, base_ref, ext_ref):
    for block in range(owned // LANES):
        here = slice(block * LANES, (block + 1) * LANES)
        wide = rows_of(here)
        base_ref[here, :] = spread_levels(potential_ref, block) * wide
        ext_ref[here, :] = wide.astype(BF16).astype(F32)
    base_ref[owned:, :] = jnp.zeros_like(base_ref[owned:, :])


def prepare_kernel(nodes, rows_ref, ext_ref, edge_ref, picked):
    owned = rows_ref.shape[0]
    ext_ref[0:owned, :] = rows_ref[...].astype(F32)

    def body(step, _):
        for k in range(16):
            i = step * 16 + k
            picked[pl.ds(i, 1), :] = ext_ref[pl.ds(nodes[i], 1), :]
        return 0

    lax.fori_loop(0, nodes.shape[0] // 16, body, 0)
    edge_ref[...] = picked[...].astype(BF16)


def prepare(nodes, rows):
    owned, plane = rows.shape[0], nodes.shape[0]
    ext, edge = pl.pallas_call(
        prepare_kernel,
        out_shape=(
            jax.ShapeDtypeStruct((owned + plane, LANES), F32),
            jax.ShapeDtypeStruct((plane, LANES), BF16),
        ),
        in_specs=[SM, VM],
        out_specs=(VM, VM),
        scratch_shapes=[pltpu.VMEM((plane, LANES), F32)],
        compiler_params=params(8),
        cost_estimate=cost(0, 12 << 20),
        name="prepare",
    )(nodes, rows)
    return ext, ext, edge


def packed_links(links):
    npc = links.shape[1]
    half = (npc + 1) // 2
    later = jnp.pad(links[:, half:], ((0, 0), (0, 2 * half - npc)))
    return (links[:, :half] | (later << 16)).reshape(-1)


def each_row(words, npc, cell, visit):
    half = (npc + 1) // 2
    for r in range(half):
        word = words[cell * half + r]
        visit(r, pl.ds(word & 0xFFFF, 1))
        if r + half < npc:
            visit(r + half, pl.ds(word >> 16, 1))


def gather_cells(words, npc, ext_ref, gathered, first):
    def cell(c, _):
        def visit(r, row):
            gathered[c, r : r + 1, :] = ext_ref[row, :]

        each_row(words, npc, first + c, visit)
        return 0

    lax.fori_loop(0, gathered.shape[0], cell, 0)


def multiply_cells(scale, matrix_ref, gathered, products, first):
    cells, npc = gathered.shape[0], matrix_ref.shape[0]
    for c in range(0, cells, 2):
        both = jnp.concatenate(
            [gathered[c, 0:npc, :].astype(BF16), gathered[c + 1, 0:npc, :].astype(BF16)], axis=1
        )
        made = jnp.dot(matrix_ref[...], both, preferred_element_type=F32)
        for half in range(2):
            products[c + half, 0:npc, :] = (
                made[:, half * LANES : (half + 1) * LANES] * scale[first + c + half]
            )


def scatter_cells(words, npc, products, sums, first):
    def cell(c, _):
        seen = []

        def visit(r, row):
            total = sums[len(seen) % len(sums)]
            seen.append(r)
            total[row, :] = total[row, :] + products[c, r : r + 1, :]

        each_row(words, npc, first + c, visit)
        return 0

    lax.fori_loop(0, products.shape[0], cell, 0)


def near_products_kernel(links, scale, ext_ref, matrix_ref, out_ref, gathered):
    gather_cells(links, matrix_ref.shape[0], ext_ref, gathered, 0)
    multiply_cells(scale, matrix_ref, gathered, out_ref, 0)


def far_cells_kernel(
    links, scale, ext_ref, ghost_ref, matrix_ref, wide_ref, potential_ref, out_ref, back_ref, ext, gathered,
    products, *sums
):
    owned = out_ref.shape[0]
    half = gathered.shape[0]
    ext[0:owned, :] = ext_ref[0:owned, :]
    ext[owned:, :] = ghost_ref[...].astype(F32)
    for block in range(owned // LANES):
        here = slice(block * LANES, (block + 1) * LANES)
        sums[0][here, :] = spread_levels(potential_ref, block) * wide_ref[here, :]
    sums[0][owned:, :] = jnp.zeros_like(sums[0][owned:, :])
    for total in sums[1:]:
        total[...] = jnp.zeros_like(total)
    npc = matrix_ref.shape[0]
    gather_cells(links, npc, ext, gathered, half)
    multiply_cells(scale, matrix_ref, gathered, products, half)
    scatter_cells(links, npc, products, sums, half)
    back_ref[...] = sum(total[owned:, :] for total in sums)
    out_ref[...] = sum(total[0:owned, :] for total in sums)


def near_sums_kernel(npc, links, products_ref, start_ref, out_ref, *sums):
    sums = (out_ref,) + sums
    out_ref[...] = start_ref[...]
    for total in sums[1:]:
        total[...] = jnp.zeros_like(total)
    scatter_cells(links, npc, products_ref, sums, 0)
    out_ref[...] = sum(total[...] for total in sums)


def apply_operator(links, scale, matrix, potential, wide, ext, edge):
    cells, npc = scale.shape[0], matrix.shape[0]
    half, padded = cells // 2, (npc + 7) // 8 * 8
    plane = edge.shape[0]
    whole = ext.shape
    owned = whole[0] - plane
    held = (half, padded, LANES)
    ghost = shifted(edge, "domain", -1)
    products = pl.pallas_call(
        near_products_kernel,
        out_shape=jax.ShapeDtypeStruct(held, F32),
        in_specs=[SM, SM, VM, VM],
        out_specs=VM,
        scratch_shapes=[pltpu.VMEM(held, F32)],
        compiler_params=params(16),
        cost_estimate=cost(0, 14 << 20),
        name="near_products",
    )(links, scale, ext, matrix)
    ghost, products = ordered(ghost, products)
    sums, back = pl.pallas_call(
        far_cells_kernel,
        out_shape=(
            jax.ShapeDtypeStruct((owned, LANES), F32),
            jax.ShapeDtypeStruct((plane, LANES), F32),
        ),
        in_specs=[SM, SM, VM, VM, VM, VM, VM],
        out_specs=(VM, VM),
        scratch_shapes=[pltpu.VMEM(whole, F32), pltpu.VMEM(held, F32), pltpu.VMEM(held, F32)]
        + [pltpu.VMEM(whole, F32)] * CHAINS,
        compiler_params=params(22),
        cost_estimate=cost(0, 28 << 20),
        name="far_cells",
    )(links, scale, ext, ghost, matrix, wide, potential)
    back = shifted(back, "domain", 1)
    sums = pl.pallas_call(
        functools.partial(near_sums_kernel, npc),
        out_shape=jax.ShapeDtypeStruct((owned, LANES), F32),
        in_specs=[SM, VM, VM],
        out_specs=VM,
        scratch_shapes=[pltpu.VMEM((owned, LANES), F32)] * (CHAINS - 1),
        compiler_params=params(16),
        cost_estimate=cost(0, 14 << 20),
        name="near_sums",
    )(links, products, sums)
    return sums, back


def add_back(nodes, target, back_ref, factor, picked=None):
    def body(step, _):
        at = [step * 16 + k for k in range(16)]
        rows = [pl.ds(nodes[i], 1) for i in at]
        new = [target[r, :] + factor * back_ref[pl.ds(i, 1), :] for i, r in zip(at, rows)]
        for i, r, value in zip(at, rows, new):
            target[r, :] = value
            if picked is not None:
                picked[pl.ds(i, 1), :] = value
        return 0

    lax.fori_loop(0, nodes.shape[0] // 16, body, 0)


def first_kernel(nodes, sums_ref, back_ref, term_ref, ext_ref, edge_ref, picked):
    owned = sums_ref.shape[0]
    term_ref[...] = sums_ref[...] * (1.0 / HALF_WIDTH)
    add_back(nodes, term_ref, back_ref, 1.0 / HALF_WIDTH, picked)
    edge_ref[...] = picked[...].astype(BF16)
    ext_ref[0:owned, :] = term_ref[...].astype(BF16).astype(F32)


def first_term(nodes, sums, back):
    owned, plane = sums.shape[0], nodes.shape[0]
    return pl.pallas_call(
        first_kernel,
        out_shape=(
            jax.ShapeDtypeStruct((owned, LANES), F32),
            jax.ShapeDtypeStruct((owned + plane, LANES), F32),
            jax.ShapeDtypeStruct((plane, LANES), BF16),
        ),
        in_specs=[SM, VM, VM],
        out_specs=(VM, VM, VM),
        scratch_shapes=[pltpu.VMEM((plane, LANES), F32)],
        compiler_params=params(16),
        cost_estimate=cost(0, 8 << 20),
        name="first_term",
    )(nodes, sums, back)


def second_kernel(band, nodes, sums_ref, back_ref, previous_ref, *refs):
    pieces, rest_ref, total = refs[:-2], refs[-2], refs[-1]
    total[...] = sums_ref[...] * (2.0 / HALF_WIDTH) - previous_ref[...].astype(F32)
    add_back(nodes, total, back_ref, 2.0 / HALF_WIDTH)
    count = len(pieces)
    rows = total.shape[0] // count
    for k, piece in enumerate(pieces):
        start = pl.multiple_of(lax.rem(band[0] + k, count) * rows, rows)
        part = total[pl.ds(start, rows), :].astype(BF16)
        piece[...] = part
        if k:
            rest_ref[(k - 1) * rows : k * rows, :] = part


def second_term(band, nodes, sums, back, previous, count):
    owned = sums.shape[0]
    rows = owned // count
    made = pl.pallas_call(
        second_kernel,
        out_shape=[jax.ShapeDtypeStruct((rows, LANES), BF16)] * count
        + [jax.ShapeDtypeStruct((owned - rows, LANES), BF16)],
        in_specs=[SM, SM, VM, VM, VM],
        out_specs=[VM] * (count + 1),
        scratch_shapes=[pltpu.VMEM(sums.shape, F32)],
        compiler_params=params(16),
        cost_estimate=cost(0, 6 << 20),
        name="second_term",
    )(band, nodes, sums, back, previous)
    return made[:count], made[count]


def gram_kernel(place, *refs):
    pieces, (keep_ref, send_ref, held, whole) = refs[:-4], refs[-4:]
    count = len(pieces)
    for s, piece in enumerate(pieces):
        held[lax.rem(place[0] + (count - s), count)] = piece[...]
    at = 0
    for i in range(count):
        for j in range(i + 1):
            whole[at : at + LANES, :] = lax.dot_general(
                held[i], held[j], (((0,), (0,)), ((), ())), preferred_element_type=F32
            )
            at += LANES
    half = at // 2
    mine = pl.multiple_of(place[1] * half, half)
    keep_ref[...] = whole[pl.ds(mine, half), :]
    send_ref[...] = whole[pl.ds(half - mine, half), :]


def partial_gram(place, pieces):
    count = len(pieces)
    rows = count * (count + 1) // 2 * LANES
    return pl.pallas_call(
        gram_kernel,
        out_shape=[jax.ShapeDtypeStruct((rows // 2, LANES), F32)] * 2,
        in_specs=[SM] + [VM] * count,
        out_specs=[VM] * 2,
        scratch_shapes=[
            pltpu.VMEM((count,) + pieces[0].shape, BF16),
            pltpu.VMEM((rows, LANES), F32),
        ],
        compiler_params=params(16),
        cost_estimate=cost(0, 4 << 20),
        name="partial_gram",
    )(place, *pieces)


def quarters_kernel(place, a_ref, b_ref, *refs):
    outs, total = refs[:-1], refs[-1]
    total[...] = a_ref[...] + b_ref[...]
    rows = outs[0].shape[0]
    for m, out in enumerate(outs):
        out[...] = total[pl.ds(pl.multiple_of((place[2] ^ m) * rows, rows), rows), :]


def quarters(place, a, b, count):
    rows = a.shape[0] // count
    return pl.pallas_call(
        quarters_kernel,
        out_shape=[jax.ShapeDtypeStruct((rows, LANES), F32)] * count,
        in_specs=[SM, VM, VM],
        out_specs=[VM] * count,
        scratch_shapes=[pltpu.VMEM(a.shape, F32)],
        compiler_params=params(4),
        cost_estimate=cost(0, 1 << 20),
        name="quarters",
    )(place, a, b)


def joined_kernel(place, *refs):
    parts, out_ref = refs[:-1], refs[-1]
    rows = parts[0].shape[0]
    for m, part in enumerate(parts):
        out_ref[pl.ds(pl.multiple_of((place[2] ^ m) * rows, rows), rows), :] = part[...]


def joined(place, parts):
    rows = parts[0].shape[0] * len(parts)
    return pl.pallas_call(
        joined_kernel,
        out_shape=jax.ShapeDtypeStruct((rows, LANES), F32),
        in_specs=[SM] + [VM] * len(parts),
        out_specs=VM,
        compiler_params=params(4),
        cost_estimate=cost(0, 1 << 20),
        name="joined",
    )(place, *parts)


def paired(value, axis, mask):
    count = lax.axis_size(axis)
    return lax.ppermute(value, axis, [(i, i ^ mask) for i in range(count)])


def passed_up(rests, firsts, held):
    rows = firsts[held].shape[0]
    count = lax.axis_size("band")
    onward = jnp.concatenate([rests[held][rows:], firsts[held]])
    return lax.ppermute(onward, "band", [(i, i + 1) for i in range(held, count - 1)])


def ordered(*values):
    return lax.optimization_barrier(values)


def summed_beside(place, keep, send, rests, firsts):
    count = lax.axis_size("band")
    half = keep + paired(send, "domain", 1)
    if lax.axis_size("domain") != 8 or count != 4:
        for held in range(count - 1):
            rests.append(passed_up(rests, firsts, held))
        side = lax.axis_index("domain") % 2
        both = jnp.stack([half, jnp.zeros_like(half)])
        both = lax.psum(jnp.where(side == 0, both, both[::-1]) * 1.0, ("domain", "band"))
        return both[side], both[1 - side]
    rests.append(passed_up(rests, firsts, 0))
    total, *others = quarters(place, keep, paired(send, "domain", 1), 4)
    for part in [paired(other, "domain", 2 * m) for m, other in enumerate(others, 1)]:
        total = total + part
    parts = [total] + [shifted(total, "band", s) for s in range(1, count)]
    parts[1], rests[1] = ordered(parts[1], rests[1])
    rests.append(passed_up(rests, firsts, 1))
    rows = firsts[1].shape[0]
    skipping = jnp.concatenate([rests[1][2 * rows :], firsts[1], rests[1][:rows]])
    rests.append(lax.ppermute(skipping, "band", [(1, 3)]))
    total = sum(parts[1:], parts[0])
    half = joined(place, [total] + [paired(total, "domain", 2 * m) for m in (1, 2, 3)])
    return half, paired(half, "domain", 1)


def split_dot(a, b, dims=(((1,), (0,)), ((), ()))):
    def parts(x):
        high = x.astype(BF16)
        return high, (x - high.astype(F32)).astype(BF16)

    def dot(x, y):
        return lax.dot_general(x, y, dims, preferred_element_type=F32)

    (a_high, a_low), (b_high, b_low) = parts(a), parts(b)
    return dot(a_high, b_high) + (dot(a_high, b_low) + dot(a_low, b_high))


def small_inverse(tiles, lane):
    count, tiles, done = len(tiles), list(tiles), []
    shape = tiles[0].shape
    sub = lax.broadcasted_iota(jnp.int32, shape, 0)

    def along_lanes(tile, column):
        return jnp.broadcast_to(tile[:, column : column + 1], shape)

    def along_rows(tile, row):
        return jnp.broadcast_to(tile[row : row + 1, :], shape)

    def stacked(rows):
        tile = rows[0]
        for i in range(1, 8):
            tile = jnp.where(sub == i, rows[i], tile)
        return tile

    columns = [along_lanes(tiles[0], m) for m in range(8)]
    for p in range(count):
        base = 8 * p
        group = (lane >= base) & (lane < base + 8)
        entry = {(i, j): along_rows(columns[j], i) for j in range(8) for i in range(j, 8)}
        start = jnp.where(group, (lane - base == sub).astype(F32), tiles[p])
        solved = [along_rows(start, i) for i in range(8)]
        following = None
        if p + 1 < count:
            ahead = [along_lanes(tiles[p + 1], base + m) for m in range(8)]
            columns = [along_lanes(tiles[p + 1], base + 8 + m) for m in range(8)]
            following = jnp.where(group, 0.0, tiles[p + 1])
        inverse, factor = [], {}
        for j in range(8):
            pivot = 1.0 / entry[j, j]
            inverse.append(pivot)
            if following is not None:
                scaled = ahead[j] * pivot
                columns = [c - scaled * along_rows(ahead[j], m) for m, c in enumerate(columns)]
                following = following - scaled * solved[j]
                for m in range(j + 1, 8):
                    ahead[m] = ahead[m] - scaled * entry[m, j]
            for i in range(j + 1, 8):
                factor[i, j] = entry[i, j] * pivot
            for i in range(j + 1, 8):
                for k in range(j + 1, i + 1):
                    entry[i, k] = entry[i, k] - factor[i, j] * entry[k, j]
                solved[i] = solved[i] - factor[i, j] * solved[j]
        result = stacked([solved[i] * lax.rsqrt(entry[i, i]) for i in range(8)])
        done.append(jnp.where(lane <= base + sub, result, 0.0))
        if p + 2 < count:
            back = [None] * 8
            for i in range(7, -1, -1):
                value = solved[i] * inverse[i]
                for k in range(i + 1, 8):
                    value = value - factor[k, i] * back[k]
                back[i] = value
            value = jnp.where(group, 0.0, tiles[p + 2])
            for m in range(8):
                value = value - along_lanes(tiles[p + 2], base + m) * back[m]
            tiles[p + 2] = value
            if p + 3 < count:
                spread = [stacked(back), jnp.zeros((LANES - 8 - base, LANES), F32)]
                if base:
                    spread = [jnp.zeros((base, LANES), F32)] + spread
                made = split_dot(
                    jnp.concatenate(tiles[p + 3 :], axis=0), jnp.concatenate(spread, axis=0)
                )
                for i in range(p + 3, count):
                    row = 8 * (i - p - 3)
                    tiles[i] = jnp.where(group, 0.0, tiles[i]) - made[row : row + 8, :]
        if following is not None:
            tiles[p + 1] = following
    return done


def inverse_kernel(over, place, mine_ref, other_ref, out_ref, packed_ref, work, small):
    half = mine_ref.shape[0]
    mine = pl.multiple_of(place[1] * half, half)
    packed_ref[pl.ds(mine, half), :] = mine_ref[...]
    packed_ref[pl.ds(half - mine, half), :] = other_ref[...]
    size = work.shape[0]
    blocks = size // LANES
    at = 0
    for i in range(blocks):
        for j in range(i + 1):
            block = packed_ref[at : at + LANES, :] * over
            work[i * LANES : (i + 1) * LANES, j * LANES : (j + 1) * LANES] = block
            if i != j:
                work[j * LANES : (j + 1) * LANES, i * LANES : (i + 1) * LANES] = block.T
            at += LANES
    out_ref[...] = jnp.zeros_like(out_ref)
    lane = lax.broadcasted_iota(jnp.int32, (8, LANES), 1)

    def step(k, _):
        base = pl.multiple_of(k * LANES, LANES)
        tiles = [
            work[pl.ds(pl.multiple_of(base + 8 * i, 8), 8), pl.ds(base, LANES)]
            for i in range(LANES // 8)
        ]
        for i, tile in enumerate(small_inverse(tiles, lane)):
            small[8 * i : 8 * i + 8, :] = tile
        for which in range(blocks):

            @pl.when(k == which)
            def _():
                a, b = which * LANES, (which + 1) * LANES
                diagonal = small[...]
                out_ref[a:b, a:b] = diagonal
                if which:
                    left = split_dot(diagonal, work[a:b, 0:a])
                    out_ref[a:b, 0:a] = left
                if b < size:
                    right = split_dot(diagonal, work[a:b, b:size])
                    column = split_dot(work[b:size, a:b], diagonal, (((1,), (1,)), ((), ())))
                    work[b:size, b:size] = work[b:size, b:size] - split_dot(column, right)
                    work[b:size, a:b] = -split_dot(column, diagonal)
                    if which:
                        work[b:size, 0:a] = work[b:size, 0:a] - split_dot(column, left)

        return 0

    lax.fori_loop(0, blocks, step, 0)


def inverse_factor(place, mine, other, size, over):
    return pl.pallas_call(
        functools.partial(inverse_kernel, over),
        out_shape=jax.ShapeDtypeStruct((size, size), F32),
        in_specs=[SM, VM, VM],
        out_specs=VM,
        scratch_shapes=[
            pltpu.VMEM((2 * mine.shape[0], LANES), F32),
            pltpu.VMEM((size, size), F32),
            pltpu.VMEM((LANES, LANES), F32),
        ],
        compiler_params=params(16),
        cost_estimate=cost(0, 70 << 20),
        name="inverse_factor",
    )(place, mine, other)


def output_kernel(band, factor_ref, *refs):
    out_ref, blocks_ref = refs[-2:]
    count = factor_ref.shape[0] // LANES
    firsts, rests = refs[:count], refs[count:-2]
    j = pl.program_id(0)

    @pl.when(j == 0)
    def _():
        row = pl.ds(pl.multiple_of(band[0] * LANES, LANES), LANES)
        for s in range(count):
            source = band[0] - s
            column = pl.ds(pl.multiple_of(jnp.maximum(source, 0) * LANES, LANES), LANES)
            block = jnp.where(source >= 0, factor_ref[row, column], 0.0).T
            high = block.astype(BF16)
            here = slice(s * LANES, (s + 1) * LANES)
            blocks_ref[here, 0:LANES] = high
            blocks_ref[here, LANES:] = (block - high.astype(F32)).astype(BF16)

    def put(pieces):
        rows = jnp.concatenate(pieces, axis=1)
        made = jnp.dot(rows, blocks_ref[...], preferred_element_type=F32)
        out_ref[...] = made[:, 0:LANES] + made[:, LANES:]

    rows = out_ref.shape[0]

    @pl.when(j == 0)
    def _():
        put([piece[...] for piece in firsts])

    @pl.when(j > 0)
    def _():
        here = pl.ds(pl.multiple_of((j - 1) * rows, rows), rows)
        put([piece[here, :] for piece in rests])


def output(band, factor, firsts, rests):
    count = len(firsts)
    rows = firsts[0].shape[0]
    return pl.pallas_call(
        output_kernel,
        out_shape=jax.ShapeDtypeStruct((rows * count, LANES), F32),
        grid_spec=pltpu.PrefetchScalarGridSpec(
            num_scalar_prefetch=1,
            grid=(count,),
            in_specs=[VM] * (1 + 2 * count),
            out_specs=pl.BlockSpec((rows, LANES), lambda j, band: (lax.rem(band[0] + j, count), 0)),
            scratch_shapes=[pltpu.VMEM((count * LANES, 2 * LANES), BF16)],
        ),
        compiler_params=params(24),
        cost_estimate=cost(0, 10 << 20),
        name="output",
    )(band, factor, *firsts, *rests)


def shards(states_block, cell_matrix, cell_scale, potential, connectivity, boundary_nodes):
    owned = states_block.shape[0]
    count = lax.axis_size("band")
    band = lax.axis_index("band").astype(jnp.int32).reshape(1)
    levels = potential.reshape(owned // LANES, LANES)

    operator = functools.partial(
        apply_operator, packed_links(connectivity), cell_scale, cell_matrix, levels
    )
    sums, back = operator(*prepare(boundary_nodes, states_block))
    sums, back = operator(*first_term(boundary_nodes, sums, back))
    pieces, rest = second_term(band, boundary_nodes, sums, back, states_block, count)

    firsts = [pieces[0]] + [shifted(pieces[s], "band", s) for s in range(1, count)]
    firsts = list(ordered(*firsts))
    rests = [rest]
    domain = lax.axis_index("domain")
    place = jnp.stack([lax.axis_index("band"), domain % 2, domain // 2]).astype(jnp.int32)
    keep, send = partial_gram(place, firsts)
    mine, other = summed_beside(place, keep, send, rests, firsts)
    over = 1.0 / (owned * lax.axis_size("domain"))
    factor = inverse_factor(place, mine, other, count * LANES, over)
    return output(band, factor, firsts, rests)


def solution(mesh):
    return jax.shard_map(
        shards,
        mesh=mesh,
        in_specs=(
            P("domain", "band"),
            P(),
            P("domain"),
            P("domain"),
            P("domain", None),
            P("domain"),
        ),
        out_specs=P("domain", "band"),
        check_vma=False,
    )
```

```python
import functools

import jax
import jax.numpy as jnp
from jax import lax
from jax.experimental import pallas as pl
from jax.experimental.pallas import tpu as pltpu
from jax.sharding import PartitionSpec as P

CENTER = 1.5
HALF_WIDTH = 1.25
LANES = 128
CHAINS = 6
F32 = jnp.float32
BF16 = jnp.bfloat16
VM = pl.BlockSpec(memory_space=pltpu.VMEM)
SM = pl.BlockSpec(memory_space=pltpu.SMEM)


def params(mebibytes):
    return pltpu.CompilerParams(vmem_limit_bytes=mebibytes << 20)


def cost(flops, moved):
    return pl.CostEstimate(flops=flops, bytes_accessed=moved, transcendentals=0)


def shifted(value, axis, steps):
    count = lax.axis_size(axis)
    return lax.ppermute(value, axis, [(i, (i + steps) % count) for i in range(count)])


def spread_levels(potential_ref, block):
    return jnp.broadcast_to(potential_ref[block : block + 1, :], (LANES, LANES)).T - CENTER


def rows_out(rows_of, potential_ref, owned, base_ref, ext_ref):
    for block in range(owned // LANES):
        here = slice(block * LANES, (block + 1) * LANES)
        wide = rows_of(here)
        base_ref[here, :] = spread_levels(potential_ref, block) * wide
        ext_ref[here, :] = wide.astype(BF16).astype(F32)
    base_ref[owned:, :] = jnp.zeros_like(base_ref[owned:, :])


def prepare_kernel(nodes, rows_ref, links_ref, ext_ref, edge_ref, words_ref, picked):
    owned = rows_ref.shape[0]
    ext_ref[0:owned, :] = rows_ref[...].astype(F32)
    pack_links(links_ref, words_ref)

    def body(step, _):
        for k in range(16):
            i = step * 16 + k
            picked[pl.ds(i, 1), :] = ext_ref[pl.ds(nodes[i], 1), :]
        return 0

    lax.fori_loop(0, nodes.shape[0] // 16, body, 0)
    edge_ref[...] = picked[...].astype(BF16)


def prepare(nodes, rows, links):
    owned, plane = rows.shape[0], nodes.shape[0]
    cells, npc = links.shape
    groups = ((npc + 1) // 2 + LANES - 1) // LANES
    ext, edge, words = pl.pallas_call(
        prepare_kernel,
        out_shape=(
            jax.ShapeDtypeStruct((owned + plane, LANES), F32),
            jax.ShapeDtypeStruct((plane, LANES), BF16),
            jax.ShapeDtypeStruct((groups * cells, LANES), jnp.int32),
        ),
        in_specs=[SM, VM, VM],
        out_specs=(VM, VM, VM),
        scratch_shapes=[pltpu.VMEM((plane, LANES), F32)],
        compiler_params=params(8),
        cost_estimate=cost(0, 12 << 20),
        name="prepare",
    )(nodes, rows, links)
    return (ext, ext, edge), words.reshape(-1)


def pack_links(links_ref, words_ref):
    cells, npc = links_ref.shape
    half = (npc + 1) // 2
    early = links_ref[:, 0:half]
    late = jnp.concatenate(
        [links_ref[:, half:npc], jnp.zeros((cells, 2 * half - npc), jnp.int32)], axis=1
    )
    words = early | (late << 16)
    for k in range(0, half, LANES):
        width = min(LANES, half - k)
        words_ref[k // LANES * cells : (k // LANES + 1) * cells, 0:width] = words[:, k : k + width]


def each_row(words, cells, npc, cell, visit):
    half = (npc + 1) // 2
    base = cell * LANES
    for r in range(half):
        word = words[base + (r // LANES * cells * LANES + r % LANES)]
        visit(r, pl.ds(word & 0xFFFF, 1))
        if r + half < npc:
            visit(r + half, pl.ds(word >> 16, 1))


def gather_cells(words, cells, npc, ext_ref, gathered, first):
    def cell(c, _):
        def visit(r, row):
            gathered[c, r : r + 1, :] = ext_ref[row, :]

        each_row(words, cells, npc, first + c, visit)
        return 0

    lax.fori_loop(0, gathered.shape[0], cell, 0)


def multiply_cells(scale, matrix_ref, gathered, products, first):
    cells, npc = gathered.shape[0], matrix_ref.shape[0]
    for c in range(0, cells, 2):
        both = jnp.concatenate(
            [gathered[c, 0:npc, :].astype(BF16), gathered[c + 1, 0:npc, :].astype(BF16)], axis=1
        )
        made = jnp.dot(matrix_ref[...], both, preferred_element_type=F32)
        for half in range(2):
            products[c + half, 0:npc, :] = (
                made[:, half * LANES : (half + 1) * LANES] * scale[first + c + half]
            )


def scatter_cells(words, cells, npc, products, sums, first):
    def cell(c, _):
        seen = []

        def visit(r, row):
            total = sums[len(seen) % len(sums)]
            seen.append(r)
            total[row, :] = total[row, :] + products[c, r : r + 1, :]

        each_row(words, cells, npc, first + c, visit)
        return 0

    lax.fori_loop(0, products.shape[0], cell, 0)


def near_products_kernel(words, scale, ext_ref, matrix_ref, out_ref, gathered):
    gather_cells(words, 2 * gathered.shape[0], matrix_ref.shape[0], ext_ref, gathered, 0)
    multiply_cells(scale, matrix_ref, gathered, out_ref, 0)


def far_cells_kernel(
    words_ref, scale, ext_ref, ghost_ref, matrix_ref, wide_ref, potential_ref, out_ref, back_ref,
    ext, gathered, products, words, sem, *sums
):
    copy = pltpu.make_async_copy(words_ref, words, sem)
    copy.start()
    owned = out_ref.shape[0]
    half, npc = gathered.shape[0], matrix_ref.shape[0]
    ext[0:owned, :] = ext_ref[0:owned, :]
    ext[owned:, :] = ghost_ref[...].astype(F32)
    for block in range(owned // LANES):
        here = slice(block * LANES, (block + 1) * LANES)
        sums[0][here, :] = spread_levels(potential_ref, block) * wide_ref[here, :]
    sums[0][owned:, :] = jnp.zeros_like(sums[0][owned:, :])
    for total in sums[1:]:
        total[...] = jnp.zeros_like(total)
    copy.wait()
    gather_cells(words, 2 * half, npc, ext, gathered, half)
    multiply_cells(scale, matrix_ref, gathered, products, half)
    scatter_cells(words, 2 * half, npc, products, sums, half)
    back_ref[...] = sum(total[owned:, :] for total in sums)
    out_ref[...] = sum(total[0:owned, :] for total in sums)


def near_sums_kernel(npc, words_ref, products_ref, start_ref, out_ref, words, sem, *sums):
    copy = pltpu.make_async_copy(words_ref, words, sem)
    copy.start()
    sums = (out_ref,) + sums
    out_ref[...] = start_ref[...]
    for total in sums[1:]:
        total[...] = jnp.zeros_like(total)
    copy.wait()
    scatter_cells(words, 2 * products_ref.shape[0], npc, products_ref, sums, 0)
    out_ref[...] = sum(total[...] for total in sums)


def apply_operator(links, scale, matrix, potential, wide, ext, edge):
    cells, npc = scale.shape[0], matrix.shape[0]
    half, padded = cells // 2, (npc + 7) // 8 * 8
    plane = edge.shape[0]
    whole = ext.shape
    owned = whole[0] - plane
    held = (half, padded, LANES)
    ghost = shifted(edge, "domain", -1)
    index = [pltpu.SMEM(links.shape, jnp.int32), pltpu.SemaphoreType.DMA]
    products = pl.pallas_call(
        near_products_kernel,
        out_shape=jax.ShapeDtypeStruct(held, F32),
        in_specs=[SM, SM, VM, VM],
        out_specs=VM,
        scratch_shapes=[pltpu.VMEM(held, F32)],
        compiler_params=params(16),
        cost_estimate=cost(0, 14 << 20),
        name="near_products",
    )(links, scale, ext, matrix)
    ghost, products = ordered(ghost, products)
    sums, back = pl.pallas_call(
        far_cells_kernel,
        out_shape=(
            jax.ShapeDtypeStruct((owned, LANES), F32),
            jax.ShapeDtypeStruct((plane, LANES), F32),
        ),
        in_specs=[VM, SM, VM, VM, VM, VM, VM],
        out_specs=(VM, VM),
        scratch_shapes=[pltpu.VMEM(whole, F32), pltpu.VMEM(held, F32), pltpu.VMEM(held, F32)]
        + index
        + [pltpu.VMEM(whole, F32)] * CHAINS,
        compiler_params=params(22),
        cost_estimate=cost(0, 28 << 20),
        name="far_cells",
    )(links, scale, ext, ghost, matrix, wide, potential)
    back = shifted(back, "domain", 1)
    sums = pl.pallas_call(
        functools.partial(near_sums_kernel, npc),
        out_shape=jax.ShapeDtypeStruct((owned, LANES), F32),
        in_specs=[VM] * 3,
        out_specs=VM,
        scratch_shapes=index + [pltpu.VMEM((owned, LANES), F32)] * (CHAINS - 1),
        compiler_params=params(16),
        cost_estimate=cost(0, 14 << 20),
        name="near_sums",
    )(links, products, sums)
    return sums, back


def add_back(nodes, target, back_ref, factor, picked=None):
    def body(step, _):
        at = [step * 16 + k for k in range(16)]
        rows = [pl.ds(nodes[i], 1) for i in at]
        new = [target[r, :] + factor * back_ref[pl.ds(i, 1), :] for i, r in zip(at, rows)]
        for i, r, value in zip(at, rows, new):
            target[r, :] = value
            if picked is not None:
                picked[pl.ds(i, 1), :] = value
        return 0

    lax.fori_loop(0, nodes.shape[0] // 16, body, 0)


def first_kernel(nodes, sums_ref, back_ref, term_ref, ext_ref, edge_ref, picked):
    owned = sums_ref.shape[0]
    term_ref[...] = sums_ref[...] * (1.0 / HALF_WIDTH)
    add_back(nodes, term_ref, back_ref, 1.0 / HALF_WIDTH, picked)
    edge_ref[...] = picked[...].astype(BF16)
    ext_ref[0:owned, :] = term_ref[...].astype(BF16).astype(F32)


def first_term(nodes, sums, back):
    owned, plane = sums.shape[0], nodes.shape[0]
    return pl.pallas_call(
        first_kernel,
        out_shape=(
            jax.ShapeDtypeStruct((owned, LANES), F32),
            jax.ShapeDtypeStruct((owned + plane, LANES), F32),
            jax.ShapeDtypeStruct((plane, LANES), BF16),
        ),
        in_specs=[SM, VM, VM],
        out_specs=(VM, VM, VM),
        scratch_shapes=[pltpu.VMEM((plane, LANES), F32)],
        compiler_params=params(16),
        cost_estimate=cost(0, 8 << 20),
        name="first_term",
    )(nodes, sums, back)


def second_kernel(band, nodes, sums_ref, back_ref, previous_ref, *refs):
    pieces, rest_ref, total = refs[:-2], refs[-2], refs[-1]
    total[...] = sums_ref[...] * (2.0 / HALF_WIDTH) - previous_ref[...].astype(F32)
    add_back(nodes, total, back_ref, 2.0 / HALF_WIDTH)
    count = len(pieces)
    rows = total.shape[0] // count
    for k, piece in enumerate(pieces):
        start = pl.multiple_of(lax.rem(band[0] + k, count) * rows, rows)
        part = total[pl.ds(start, rows), :].astype(BF16)
        piece[...] = part
        if k:
            rest_ref[(k - 1) * rows : k * rows, :] = part


def second_term(band, nodes, sums, back, previous, count):
    owned = sums.shape[0]
    rows = owned // count
    made = pl.pallas_call(
        second_kernel,
        out_shape=[jax.ShapeDtypeStruct((rows, LANES), BF16)] * count
        + [jax.ShapeDtypeStruct((owned - rows, LANES), BF16)],
        in_specs=[SM, SM, VM, VM, VM],
        out_specs=[VM] * (count + 1),
        scratch_shapes=[pltpu.VMEM(sums.shape, F32)],
        compiler_params=params(16),
        cost_estimate=cost(0, 6 << 20),
        name="second_term",
    )(band, nodes, sums, back, previous)
    return made[:count], made[count]


def gram_kernel(place, *refs):
    pieces, (keep_ref, send_ref, held, whole) = refs[:-4], refs[-4:]
    count = len(pieces)
    for s, piece in enumerate(pieces):
        held[lax.rem(place[0] + (count - s), count)] = piece[...]
    at = 0
    for i in range(count):
        for j in range(i + 1):
            whole[at : at + LANES, :] = lax.dot_general(
                held[i], held[j], (((0,), (0,)), ((), ())), preferred_element_type=F32
            )
            at += LANES
    half = at // 2
    mine = pl.multiple_of(place[1] * half, half)
    keep_ref[...] = whole[pl.ds(mine, half), :]
    send_ref[...] = whole[pl.ds(half - mine, half), :]


def partial_gram(place, pieces):
    count = len(pieces)
    rows = count * (count + 1) // 2 * LANES
    return pl.pallas_call(
        gram_kernel,
        out_shape=[jax.ShapeDtypeStruct((rows // 2, LANES), F32)] * 2,
        in_specs=[SM] + [VM] * count,
        out_specs=[VM] * 2,
        scratch_shapes=[
            pltpu.VMEM((count,) + pieces[0].shape, BF16),
            pltpu.VMEM((rows, LANES), F32),
        ],
        compiler_params=params(16),
        cost_estimate=cost(0, 4 << 20),
        name="partial_gram",
    )(place, *pieces)


def quarters_kernel(place, a_ref, b_ref, *refs):
    outs, total = refs[:-1], refs[-1]
    total[...] = a_ref[...] + b_ref[...]
    rows = outs[0].shape[0]
    for m, out in enumerate(outs):
        out[...] = total[pl.ds(pl.multiple_of((place[2] ^ m) * rows, rows), rows), :]


def quarters(place, a, b, count):
    rows = a.shape[0] // count
    return pl.pallas_call(
        quarters_kernel,
        out_shape=[jax.ShapeDtypeStruct((rows, LANES), F32)] * count,
        in_specs=[SM, VM, VM],
        out_specs=[VM] * count,
        scratch_shapes=[pltpu.VMEM(a.shape, F32)],
        compiler_params=params(4),
        cost_estimate=cost(0, 1 << 20),
        name="quarters",
    )(place, a, b)


def joined_kernel(place, *refs):
    parts, out_ref = refs[:-1], refs[-1]
    rows = parts[0].shape[0]
    for m, part in enumerate(parts):
        out_ref[pl.ds(pl.multiple_of((place[2] ^ m) * rows, rows), rows), :] = part[...]


def joined(place, parts):
    rows = parts[0].shape[0] * len(parts)
    return pl.pallas_call(
        joined_kernel,
        out_shape=jax.ShapeDtypeStruct((rows, LANES), F32),
        in_specs=[SM] + [VM] * len(parts),
        out_specs=VM,
        compiler_params=params(4),
        cost_estimate=cost(0, 1 << 20),
        name="joined",
    )(place, *parts)


def paired(value, axis, mask):
    count = lax.axis_size(axis)
    return lax.ppermute(value, axis, [(i, i ^ mask) for i in range(count)])


def passed_up(rests, firsts, held):
    rows = firsts[held].shape[0]
    count = lax.axis_size("band")
    onward = jnp.concatenate([rests[held][rows:], firsts[held]])
    return lax.ppermute(onward, "band", [(i, i + 1) for i in range(held, count - 1)])


def ordered(*values):
    return lax.optimization_barrier(values)


def summed_beside(place, keep, send, rests, firsts):
    count = lax.axis_size("band")
    half = keep + paired(send, "domain", 1)
    if lax.axis_size("domain") != 8 or count != 4:
        for held in range(count - 1):
            rests.append(passed_up(rests, firsts, held))
        side = lax.axis_index("domain") % 2
        both = jnp.stack([half, jnp.zeros_like(half)])
        both = lax.psum(jnp.where(side == 0, both, both[::-1]) * 1.0, ("domain", "band"))
        return both[side], both[1 - side]
    rests.append(passed_up(rests, firsts, 0))
    total, *others = quarters(place, keep, paired(send, "domain", 1), 4)
    for part in [paired(other, "domain", 2 * m) for m, other in enumerate(others, 1)]:
        total = total + part
    parts = [total] + [shifted(total, "band", s) for s in range(1, count)]
    parts[1], rests[1] = ordered(parts[1], rests[1])
    rests.append(passed_up(rests, firsts, 1))
    rows = firsts[1].shape[0]
    skipping = jnp.concatenate([rests[1][2 * rows :], firsts[1], rests[1][:rows]])
    rests.append(lax.ppermute(skipping, "band", [(1, 3)]))
    total = sum(parts[1:], parts[0])
    half = joined(place, [total] + [paired(total, "domain", 2 * m) for m in (1, 2, 3)])
    return half, paired(half, "domain", 1)


def split_dot(a, b, dims=(((1,), (0,)), ((), ()))):
    def parts(x):
        high = x.astype(BF16)
        return high, (x - high.astype(F32)).astype(BF16)

    def dot(x, y):
        return lax.dot_general(x, y, dims, preferred_element_type=F32)

    (a_high, a_low), (b_high, b_low) = parts(a), parts(b)
    return dot(a_high, b_high) + (dot(a_high, b_low) + dot(a_low, b_high))


def small_inverse(tiles, lane):
    count, tiles, done = len(tiles), list(tiles), []
    shape = tiles[0].shape
    sub = lax.broadcasted_iota(jnp.int32, shape, 0)

    def along_lanes(tile, column):
        return jnp.broadcast_to(tile[:, column : column + 1], shape)

    def along_rows(tile, row):
        return jnp.broadcast_to(tile[row : row + 1, :], shape)

    def stacked(rows):
        tile = rows[0]
        for i in range(1, 8):
            tile = jnp.where(sub == i, rows[i], tile)
        return tile

    columns = [along_lanes(tiles[0], m) for m in range(8)]
    for p in range(count):
        base = 8 * p
        group = (lane >= base) & (lane < base + 8)
        entry = {(i, j): along_rows(columns[j], i) for j in range(8) for i in range(j, 8)}
        start = jnp.where(group, (lane - base == sub).astype(F32), tiles[p])
        solved = [along_rows(start, i) for i in range(8)]
        following = None
        if p + 1 < count:
            ahead = [along_lanes(tiles[p + 1], base + m) for m in range(8)]
            columns = [along_lanes(tiles[p + 1], base + 8 + m) for m in range(8)]
            following = jnp.where(group, 0.0, tiles[p + 1])
        inverse, factor = [], {}
        for j in range(8):
            pivot = 1.0 / entry[j, j]
            inverse.append(pivot)
            if following is not None:
                scaled = ahead[j] * pivot
                columns = [c - scaled * along_rows(ahead[j], m) for m, c in enumerate(columns)]
                following = following - scaled * solved[j]
                for m in range(j + 1, 8):
                    ahead[m] = ahead[m] - scaled * entry[m, j]
            for i in range(j + 1, 8):
                factor[i, j] = entry[i, j] * pivot
            for i in range(j + 1, 8):
                for k in range(j + 1, i + 1):
                    entry[i, k] = entry[i, k] - factor[i, j] * entry[k, j]
                solved[i] = solved[i] - factor[i, j] * solved[j]
        result = stacked([solved[i] * lax.rsqrt(entry[i, i]) for i in range(8)])
        done.append(jnp.where(lane <= base + sub, result, 0.0))
        if p + 2 < count:
            back = [None] * 8
            for i in range(7, -1, -1):
                value = solved[i] * inverse[i]
                for k in range(i + 1, 8):
                    value = value - factor[k, i] * back[k]
                back[i] = value
            value = jnp.where(group, 0.0, tiles[p + 2])
            for m in range(8):
                value = value - along_lanes(tiles[p + 2], base + m) * back[m]
            tiles[p + 2] = value
            if p + 3 < count:
                spread = [stacked(back), jnp.zeros((LANES - 8 - base, LANES), F32)]
                if base:
                    spread = [jnp.zeros((base, LANES), F32)] + spread
                made = split_dot(
                    jnp.concatenate(tiles[p + 3 :], axis=0), jnp.concatenate(spread, axis=0)
                )
                for i in range(p + 3, count):
                    row = 8 * (i - p - 3)
                    tiles[i] = jnp.where(group, 0.0, tiles[i]) - made[row : row + 8, :]
        if following is not None:
            tiles[p + 1] = following
    return done


def inverse_kernel(over, place, mine_ref, other_ref, out_ref, packed_ref, work, small):
    half = mine_ref.shape[0]
    mine = pl.multiple_of(place[1] * half, half)
    packed_ref[pl.ds(mine, half), :] = mine_ref[...]
    packed_ref[pl.ds(half - mine, half), :] = other_ref[...]
    size = work.shape[0]
    blocks = size // LANES
    at = 0
    for i in range(blocks):
        for j in range(i + 1):
            block = packed_ref[at : at + LANES, :] * over
            work[i * LANES : (i + 1) * LANES, j * LANES : (j + 1) * LANES] = block
            if i != j:
                work[j * LANES : (j + 1) * LANES, i * LANES : (i + 1) * LANES] = block.T
            at += LANES
    out_ref[...] = jnp.zeros_like(out_ref)
    lane = lax.broadcasted_iota(jnp.int32, (8, LANES), 1)

    def step(k, _):
        base = pl.multiple_of(k * LANES, LANES)
        tiles = [
            work[pl.ds(pl.multiple_of(base + 8 * i, 8), 8), pl.ds(base, LANES)]
            for i in range(LANES // 8)
        ]
        for i, tile in enumerate(small_inverse(tiles, lane)):
            small[8 * i : 8 * i + 8, :] = tile
        for which in range(blocks):

            @pl.when(k == which)
            def _():
                a, b = which * LANES, (which + 1) * LANES
                diagonal = small[...]
                out_ref[a:b, a:b] = diagonal
                if which:
                    left = split_dot(diagonal, work[a:b, 0:a])
                    out_ref[a:b, 0:a] = left
                if b < size:
                    right = split_dot(diagonal, work[a:b, b:size])
                    column = split_dot(work[b:size, a:b], diagonal, (((1,), (1,)), ((), ())))
                    work[b:size, b:size] = work[b:size, b:size] - split_dot(column, right)
                    work[b:size, a:b] = -split_dot(column, diagonal)
                    if which:
                        work[b:size, 0:a] = work[b:size, 0:a] - split_dot(column, left)

        return 0

    lax.fori_loop(0, blocks, step, 0)


def inverse_factor(place, mine, other, size, over):
    return pl.pallas_call(
        functools.partial(inverse_kernel, over),
        out_shape=jax.ShapeDtypeStruct((size, size), F32),
        in_specs=[SM, VM, VM],
        out_specs=VM,
        scratch_shapes=[
            pltpu.VMEM((2 * mine.shape[0], LANES), F32),
            pltpu.VMEM((size, size), F32),
            pltpu.VMEM((LANES, LANES), F32),
        ],
        compiler_params=params(16),
        cost_estimate=cost(0, 70 << 20),
        name="inverse_factor",
    )(place, mine, other)


def output_kernel(band, factor_ref, *refs):
    out_ref, blocks_ref = refs[-2:]
    count = factor_ref.shape[0] // LANES
    firsts, rests = refs[:count], refs[count:-2]
    j = pl.program_id(0)

    @pl.when(j == 0)
    def _():
        row = pl.ds(pl.multiple_of(band[0] * LANES, LANES), LANES)
        for s in range(count):
            source = band[0] - s
            column = pl.ds(pl.multiple_of(jnp.maximum(source, 0) * LANES, LANES), LANES)
            block = jnp.where(source >= 0, factor_ref[row, column], 0.0).T
            high = block.astype(BF16)
            here = slice(s * LANES, (s + 1) * LANES)
            blocks_ref[here, 0:LANES] = high
            blocks_ref[here, LANES:] = (block - high.astype(F32)).astype(BF16)

    def put(pieces):
        rows = jnp.concatenate(pieces, axis=1)
        made = jnp.dot(rows, blocks_ref[...], preferred_element_type=F32)
        out_ref[...] = made[:, 0:LANES] + made[:, LANES:]

    rows = out_ref.shape[0]

    @pl.when(j == 0)
    def _():
        put([piece[...] for piece in firsts])

    @pl.when(j > 0)
    def _():
        here = pl.ds(pl.multiple_of((j - 1) * rows, rows), rows)
        put([piece[here, :] for piece in rests])


def output(band, factor, firsts, rests):
    count = len(firsts)
    rows = firsts[0].shape[0]
    return pl.pallas_call(
        output_kernel,
        out_shape=jax.ShapeDtypeStruct((rows * count, LANES), F32),
        grid_spec=pltpu.PrefetchScalarGridSpec(
            num_scalar_prefetch=1,
            grid=(count,),
            in_specs=[VM] * (1 + 2 * count),
            out_specs=pl.BlockSpec((rows, LANES), lambda j, band: (lax.rem(band[0] + j, count), 0)),
            scratch_shapes=[pltpu.VMEM((count * LANES, 2 * LANES), BF16)],
        ),
        compiler_params=params(24),
        cost_estimate=cost(0, 10 << 20),
        name="output",
    )(band, factor, *firsts, *rests)


def shards(states_block, cell_matrix, cell_scale, potential, connectivity, boundary_nodes):
    owned = states_block.shape[0]
    count = lax.axis_size("band")
    band = lax.axis_index("band").astype(jnp.int32).reshape(1)
    levels = potential.reshape(owned // LANES, LANES)

    start, words = prepare(boundary_nodes, states_block, connectivity)
    operator = functools.partial(apply_operator, words, cell_scale, cell_matrix, levels)
    sums, back = operator(*start)
    sums, back = operator(*first_term(boundary_nodes, sums, back))
    pieces, rest = second_term(band, boundary_nodes, sums, back, states_block, count)

    firsts = [pieces[0]] + [shifted(pieces[s], "band", s) for s in range(1, count)]
    firsts = list(ordered(*firsts))
    rests = [rest]
    domain = lax.axis_index("domain")
    place = jnp.stack([lax.axis_index("band"), domain % 2, domain // 2]).astype(jnp.int32)
    keep, send = partial_gram(place, firsts)
    mine, other = summed_beside(place, keep, send, rests, firsts)
    over = 1.0 / (owned * lax.axis_size("domain"))
    factor = inverse_factor(place, mine, other, count * LANES, over)
    return output(band, factor, firsts, rests)


def solution(mesh):
    return jax.shard_map(
        shards,
        mesh=mesh,
        in_specs=(
            P("domain", "band"),
            P(),
            P("domain"),
            P("domain"),
            P("domain", None),
            P("domain"),
        ),
        out_specs=P("domain", "band"),
        check_vma=False,
    )
```

```python
import functools

import jax
import jax.numpy as jnp
from jax import lax
from jax.experimental import pallas as pl
from jax.experimental.pallas import tpu as pltpu
from jax.sharding import PartitionSpec as P

CENTER = 1.5
HALF_WIDTH = 1.25
LANES = 128
CHAINS = 6
F32 = jnp.float32
BF16 = jnp.bfloat16
VM = pl.BlockSpec(memory_space=pltpu.VMEM)
SM = pl.BlockSpec(memory_space=pltpu.SMEM)


def params(mebibytes):
    return pltpu.CompilerParams(vmem_limit_bytes=mebibytes << 20)


def cost(flops, moved):
    return pl.CostEstimate(flops=flops, bytes_accessed=moved, transcendentals=0)


def shifted(value, axis, steps):
    count = lax.axis_size(axis)
    return lax.ppermute(value, axis, [(i, (i + steps) % count) for i in range(count)])


def spread_levels(potential_ref, block):
    return jnp.broadcast_to(potential_ref[block : block + 1, :], (LANES, LANES)).T - CENTER


def rows_out(rows_of, potential_ref, owned, base_ref, ext_ref):
    for block in range(owned // LANES):
        here = slice(block * LANES, (block + 1) * LANES)
        wide = rows_of(here)
        base_ref[here, :] = spread_levels(potential_ref, block) * wide
        ext_ref[here, :] = wide.astype(BF16).astype(F32)
    base_ref[owned:, :] = jnp.zeros_like(base_ref[owned:, :])


def prepare_kernel(nodes, rows_ref, links_ref, ext_ref, edge_ref, words_ref, picked):
    owned = rows_ref.shape[0]
    ext_ref[0:owned, :] = rows_ref[...].astype(F32)
    pack_links(links_ref, words_ref)

    def body(step, _):
        for k in range(16):
            i = step * 16 + k
            picked[pl.ds(i, 1), :] = ext_ref[pl.ds(nodes[i], 1), :]
        return 0

    lax.fori_loop(0, nodes.shape[0] // 16, body, 0)
    edge_ref[...] = picked[...].astype(BF16)


def prepare(nodes, rows, links):
    owned, plane = rows.shape[0], nodes.shape[0]
    cells, npc = links.shape
    groups = ((npc + 1) // 2 + LANES - 1) // LANES
    ext, edge, words = pl.pallas_call(
        prepare_kernel,
        out_shape=(
            jax.ShapeDtypeStruct((owned + plane, LANES), F32),
            jax.ShapeDtypeStruct((plane, LANES), BF16),
            jax.ShapeDtypeStruct((groups * cells, LANES), jnp.int32),
        ),
        in_specs=[SM, VM, VM],
        out_specs=(VM, VM, VM),
        scratch_shapes=[pltpu.VMEM((plane, LANES), F32)],
        compiler_params=params(8),
        cost_estimate=cost(0, 12 << 20),
        name="prepare",
    )(nodes, rows, links)
    return (ext, ext, edge), words.reshape(-1)


def pack_links(links_ref, words_ref):
    cells, npc = links_ref.shape
    half = (npc + 1) // 2
    early = links_ref[:, 0:half]
    late = jnp.concatenate(
        [links_ref[:, half:npc], jnp.zeros((cells, 2 * half - npc), jnp.int32)], axis=1
    )
    words = early | (late << 16)
    for k in range(0, half, LANES):
        width = min(LANES, half - k)
        words_ref[k // LANES * cells : (k // LANES + 1) * cells, 0:width] = words[:, k : k + width]


def each_row(words, cells, npc, cell, visit):
    half = (npc + 1) // 2
    base = cell * LANES
    for r in range(half):
        word = words[base + (r // LANES * cells * LANES + r % LANES)]
        visit(r, pl.ds(word & 0xFFFF, 1))
        if r + half < npc:
            visit(r + half, pl.ds(word >> 16, 1))


def gather_cells(words, cells, npc, ext_ref, gathered, first):
    def cell(c, _):
        def visit(r, row):
            gathered[c, r : r + 1, :] = ext_ref[row, :]

        each_row(words, cells, npc, first + c, visit)
        return 0

    lax.fori_loop(0, gathered.shape[0], cell, 0)


def multiply_cells(scale, matrix_ref, gathered, products, first):
    cells, npc = gathered.shape[0], matrix_ref.shape[0]
    for c in range(0, cells, 2):
        both = jnp.concatenate(
            [gathered[c, 0:npc, :].astype(BF16), gathered[c + 1, 0:npc, :].astype(BF16)], axis=1
        )
        made = jnp.dot(matrix_ref[...], both, preferred_element_type=F32)
        for half in range(2):
            products[c + half, 0:npc, :] = (
                made[:, half * LANES : (half + 1) * LANES] * scale[first + c + half]
            )


def scatter_cells(words, cells, npc, products, sums, first):
    def cell(c, _):
        seen = []

        def visit(r, row):
            total = sums[len(seen) % len(sums)]
            seen.append(r)
            total[row, :] = total[row, :] + products[c, r : r + 1, :]

        each_row(words, cells, npc, first + c, visit)
        return 0

    lax.fori_loop(0, products.shape[0], cell, 0)


def near_products_kernel(words, scale, ext_ref, matrix_ref, out_ref, gathered):
    gather_cells(words, 2 * gathered.shape[0], matrix_ref.shape[0], ext_ref, gathered, 0)
    multiply_cells(scale, matrix_ref, gathered, out_ref, 0)


def far_cells_kernel(
    words_ref, scale, ext_ref, ghost_ref, matrix_ref, wide_ref, potential_ref, out_ref, back_ref,
    ext, gathered, products, words, sem, *sums
):
    copy = pltpu.make_async_copy(words_ref, words, sem)
    copy.start()
    owned = out_ref.shape[0]
    half, npc = gathered.shape[0], matrix_ref.shape[0]
    ext[0:owned, :] = ext_ref[0:owned, :]
    ext[owned:, :] = ghost_ref[...].astype(F32)
    for block in range(owned // LANES):
        here = slice(block * LANES, (block + 1) * LANES)
        sums[0][here, :] = spread_levels(potential_ref, block) * wide_ref[here, :]
    sums[0][owned:, :] = jnp.zeros_like(sums[0][owned:, :])
    for total in sums[1:]:
        total[...] = jnp.zeros_like(total)
    copy.wait()
    gather_cells(words, 2 * half, npc, ext, gathered, half)
    multiply_cells(scale, matrix_ref, gathered, products, half)
    scatter_cells(words, 2 * half, npc, products, sums, half)
    back_ref[...] = sum(total[owned:, :] for total in sums).astype(BF16)
    out_ref[...] = sum(total[0:owned, :] for total in sums)


def near_sums_kernel(npc, words_ref, products_ref, start_ref, out_ref, words, sem, *sums):
    copy = pltpu.make_async_copy(words_ref, words, sem)
    copy.start()
    sums = (out_ref,) + sums
    out_ref[...] = start_ref[...]
    for total in sums[1:]:
        total[...] = jnp.zeros_like(total)
    copy.wait()
    scatter_cells(words, 2 * products_ref.shape[0], npc, products_ref, sums, 0)
    out_ref[...] = sum(total[...] for total in sums)


def apply_operator(links, scale, matrix, potential, wide, ext, edge):
    cells, npc = scale.shape[0], matrix.shape[0]
    half, padded = cells // 2, (npc + 7) // 8 * 8
    plane = edge.shape[0]
    whole = ext.shape
    owned = whole[0] - plane
    held = (half, padded, LANES)
    ghost = shifted(edge, "domain", -1)
    index = [pltpu.SMEM(links.shape, jnp.int32), pltpu.SemaphoreType.DMA]
    products = pl.pallas_call(
        near_products_kernel,
        out_shape=jax.ShapeDtypeStruct(held, F32),
        in_specs=[SM, SM, VM, VM],
        out_specs=VM,
        scratch_shapes=[pltpu.VMEM(held, F32)],
        compiler_params=params(16),
        cost_estimate=cost(0, 14 << 20),
        name="near_products",
    )(links, scale, ext, matrix)
    ghost, products = ordered(ghost, products)
    sums, back = pl.pallas_call(
        far_cells_kernel,
        out_shape=(
            jax.ShapeDtypeStruct((owned, LANES), F32),
            jax.ShapeDtypeStruct((plane, LANES), BF16),
        ),
        in_specs=[VM, SM, VM, VM, VM, VM, VM],
        out_specs=(VM, VM),
        scratch_shapes=[pltpu.VMEM(whole, F32), pltpu.VMEM(held, F32), pltpu.VMEM(held, F32)]
        + index
        + [pltpu.VMEM(whole, F32)] * CHAINS,
        compiler_params=params(22),
        cost_estimate=cost(0, 28 << 20),
        name="far_cells",
    )(links, scale, ext, ghost, matrix, wide, potential)
    back = shifted(back, "domain", 1)
    sums = pl.pallas_call(
        functools.partial(near_sums_kernel, npc),
        out_shape=jax.ShapeDtypeStruct((owned, LANES), F32),
        in_specs=[VM] * 3,
        out_specs=VM,
        scratch_shapes=index + [pltpu.VMEM((owned, LANES), F32)] * (CHAINS - 1),
        compiler_params=params(16),
        cost_estimate=cost(0, 14 << 20),
        name="near_sums",
    )(links, products, sums)
    return sums, back


def add_back(nodes, target, back_ref, factor, scaled, picked=None):
    scaled[...] = back_ref[...].astype(F32) * factor

    def body(step, _):
        at = [step * 16 + k for k in range(16)]
        rows = [pl.ds(nodes[i], 1) for i in at]
        new = [target[r, :] + scaled[pl.ds(i, 1), :] for i, r in zip(at, rows)]
        for i, r, value in zip(at, rows, new):
            target[r, :] = value
            if picked is not None:
                picked[pl.ds(i, 1), :] = value
        return 0

    lax.fori_loop(0, nodes.shape[0] // 16, body, 0)


def first_kernel(nodes, sums_ref, back_ref, term_ref, ext_ref, edge_ref, scaled, picked):
    owned = sums_ref.shape[0]
    term_ref[...] = sums_ref[...] * (1.0 / HALF_WIDTH)
    add_back(nodes, term_ref, back_ref, 1.0 / HALF_WIDTH, scaled, picked)
    edge_ref[...] = picked[...].astype(BF16)
    ext_ref[0:owned, :] = term_ref[...].astype(BF16).astype(F32)


def first_term(nodes, sums, back):
    owned, plane = sums.shape[0], nodes.shape[0]
    return pl.pallas_call(
        first_kernel,
        out_shape=(
            jax.ShapeDtypeStruct((owned, LANES), F32),
            jax.ShapeDtypeStruct((owned + plane, LANES), F32),
            jax.ShapeDtypeStruct((plane, LANES), BF16),
        ),
        in_specs=[SM, VM, VM],
        out_specs=(VM, VM, VM),
        scratch_shapes=[pltpu.VMEM((plane, LANES), F32)] * 2,
        compiler_params=params(16),
        cost_estimate=cost(0, 8 << 20),
        name="first_term",
    )(nodes, sums, back)


def second_kernel(nodes, sums_ref, back_ref, previous_ref, *refs):
    pieces, (rest_ref, total, scaled) = refs[:-3], refs[-3:]
    total[...] = sums_ref[...] * (2.0 / HALF_WIDTH) - previous_ref[...].astype(F32)
    add_back(nodes, total, back_ref, 2.0 / HALF_WIDTH, scaled)
    count = len(pieces)
    rows = total.shape[0] // count
    for k, piece in enumerate(pieces):
        start = pl.multiple_of(lax.rem(lax.axis_index("band") + k, count) * rows, rows)
        part = total[pl.ds(start, rows), :].astype(BF16)
        piece[...] = part
        if k:
            rest_ref[(k - 1) * rows : k * rows, :] = part


def second_term(nodes, sums, back, previous, count):
    owned = sums.shape[0]
    rows = owned // count
    made = pl.pallas_call(
        second_kernel,
        out_shape=[jax.ShapeDtypeStruct((rows, LANES), BF16)] * count
        + [jax.ShapeDtypeStruct((owned - rows, LANES), BF16)],
        in_specs=[SM, VM, VM, VM],
        out_specs=[VM] * (count + 1),
        scratch_shapes=[pltpu.VMEM(sums.shape, F32), pltpu.VMEM(back.shape, F32)],
        compiler_params=params(16),
        cost_estimate=cost(0, 6 << 20),
        name="second_term",
    )(nodes, sums, back, previous)
    return made[:count], made[count]


def gram_kernel(*refs):
    pieces, (keep_ref, send_ref, held) = refs[:-3], refs[-3:]
    count = len(pieces)
    for s, piece in enumerate(pieces):
        held[lax.rem(lax.axis_index("band") + (count - s), count)] = piece[...]
    half = keep_ref.shape[0]

    def write(*halves):
        at = 0
        for i in range(count):
            for j in range(i + 1):
                halves[at // half][at % half : at % half + LANES, :] = lax.dot_general(
                    held[i], held[j], (((0,), (0,)), ((), ())), preferred_element_type=F32
                )
                at += LANES

    side = lax.rem(lax.axis_index("domain"), 2)
    pl.when(side == 0)(lambda: write(keep_ref, send_ref))
    pl.when(side != 0)(lambda: write(send_ref, keep_ref))


def partial_gram(pieces):
    count = len(pieces)
    rows = count * (count + 1) // 2 * LANES
    return pl.pallas_call(
        gram_kernel,
        out_shape=[jax.ShapeDtypeStruct((rows // 2, LANES), F32)] * 2,
        in_specs=[VM] * count,
        out_specs=[VM] * 2,
        scratch_shapes=[pltpu.VMEM((count,) + pieces[0].shape, BF16)],
        compiler_params=params(16),
        cost_estimate=cost(0, 4 << 20),
        name="partial_gram",
    )(*pieces)


def quarters_kernel(a_ref, b_ref, *refs):
    outs, total = refs[:-1], refs[-1]
    total[...] = a_ref[...] + b_ref[...]
    rows = outs[0].shape[0]
    place = lax.axis_index("domain") // 2
    for m, out in enumerate(outs):
        out[...] = total[pl.ds(pl.multiple_of((place ^ m) * rows, rows), rows), :]


def quarters(a, b, count):
    rows = a.shape[0] // count
    return pl.pallas_call(
        quarters_kernel,
        out_shape=[jax.ShapeDtypeStruct((rows, LANES), F32)] * count,
        in_specs=[VM, VM],
        out_specs=[VM] * count,
        scratch_shapes=[pltpu.VMEM(a.shape, F32)],
        compiler_params=params(4),
        cost_estimate=cost(0, 1 << 20),
        name="quarters",
    )(a, b)


def joined_kernel(*refs):
    parts, out_ref = refs[:-1], refs[-1]
    rows = parts[0].shape[0]
    place = lax.axis_index("domain") // 2
    for m, part in enumerate(parts):
        out_ref[pl.ds(pl.multiple_of((place ^ m) * rows, rows), rows), :] = part[...]


def joined(parts):
    rows = parts[0].shape[0] * len(parts)
    return pl.pallas_call(
        joined_kernel,
        out_shape=jax.ShapeDtypeStruct((rows, LANES), F32),
        in_specs=[VM] * len(parts),
        out_specs=VM,
        compiler_params=params(4),
        cost_estimate=cost(0, 1 << 20),
        name="joined",
    )(*parts)


def paired(value, axis, mask):
    count = lax.axis_size(axis)
    return lax.ppermute(value, axis, [(i, i ^ mask) for i in range(count)])


def passed_up(rests, firsts, held):
    rows = firsts[held].shape[0]
    count = lax.axis_size("band")
    onward = jnp.concatenate([rests[held][rows:], firsts[held]])
    return lax.ppermute(onward, "band", [(i, i + 1) for i in range(held, count - 1)])


def ordered(*values):
    return lax.optimization_barrier(values)


def summed_beside(keep, send, rests, firsts):
    count = lax.axis_size("band")
    half = keep + paired(send, "domain", 1)
    if lax.axis_size("domain") != 8 or count != 4:
        for held in range(count - 1):
            rests.append(passed_up(rests, firsts, held))
        side = lax.axis_index("domain") % 2
        both = jnp.stack([half, jnp.zeros_like(half)])
        both = lax.psum(jnp.where(side == 0, both, both[::-1]) * 1.0, ("domain", "band"))
        return both[side], both[1 - side]
    rests.append(passed_up(rests, firsts, 0))
    total, *others = quarters(keep, paired(send, "domain", 1), 4)
    for part in [paired(other, "domain", 2 * m) for m, other in enumerate(others, 1)]:
        total = total + part
    parts = [total] + [shifted(total, "band", s) for s in range(1, count)]
    parts[1], rests[1] = ordered(parts[1], rests[1])
    rests.append(passed_up(rests, firsts, 1))
    rows = firsts[1].shape[0]
    skipping = jnp.concatenate([rests[1][2 * rows :], firsts[1], rests[1][:rows]])
    rests.append(lax.ppermute(skipping, "band", [(1, 3)]))
    total = sum(parts[1:], parts[0])
    half = joined([total] + [paired(total, "domain", 2 * m) for m in (1, 2, 3)])
    return half, paired(half, "domain", 1)


def split_dot(a, b, dims=(((1,), (0,)), ((), ()))):
    def parts(x):
        high = x.astype(BF16)
        return high, (x - high.astype(F32)).astype(BF16)

    def dot(x, y):
        return lax.dot_general(x, y, dims, preferred_element_type=F32)

    (a_high, a_low), (b_high, b_low) = parts(a), parts(b)
    return dot(a_high, b_high) + (dot(a_high, b_low) + dot(a_low, b_high))


def small_inverse(tiles, lane):
    count, tiles, done = len(tiles), list(tiles), []
    shape = tiles[0].shape
    sub = lax.broadcasted_iota(jnp.int32, shape, 0)

    def along_lanes(tile, column):
        return jnp.broadcast_to(tile[:, column : column + 1], shape)

    def along_rows(tile, row):
        return jnp.broadcast_to(tile[row : row + 1, :], shape)

    def stacked(rows):
        tile = rows[0]
        for i in range(1, 8):
            tile = jnp.where(sub == i, rows[i], tile)
        return tile

    columns = [along_lanes(tiles[0], m) for m in range(8)]
    for p in range(count):
        base = 8 * p
        group = (lane >= base) & (lane < base + 8)
        entry = {(i, j): along_rows(columns[j], i) for j in range(8) for i in range(j, 8)}
        start = jnp.where(group, (lane - base == sub).astype(F32), tiles[p])
        solved = [along_rows(start, i) for i in range(8)]
        following = None
        if p + 1 < count:
            ahead = [along_lanes(tiles[p + 1], base + m) for m in range(8)]
            columns = [along_lanes(tiles[p + 1], base + 8 + m) for m in range(8)]
            following = jnp.where(group, 0.0, tiles[p + 1])
        inverse, factor = [], {}
        for j in range(8):
            pivot = 1.0 / entry[j, j]
            inverse.append(pivot)
            if following is not None:
                scaled = ahead[j] * pivot
                columns = [c - scaled * along_rows(ahead[j], m) for m, c in enumerate(columns)]
                following = following - scaled * solved[j]
                for m in range(j + 1, 8):
                    ahead[m] = ahead[m] - scaled * entry[m, j]
            for i in range(j + 1, 8):
                factor[i, j] = entry[i, j] * pivot
            for i in range(j + 1, 8):
                for k in range(j + 1, i + 1):
                    entry[i, k] = entry[i, k] - factor[i, j] * entry[k, j]
                solved[i] = solved[i] - factor[i, j] * solved[j]
        result = stacked([solved[i] * lax.rsqrt(entry[i, i]) for i in range(8)])
        done.append(jnp.where(lane <= base + sub, result, 0.0))
        if p + 2 < count:
            back = [None] * 8
            for i in range(7, -1, -1):
                value = solved[i] * inverse[i]
                for k in range(i + 1, 8):
                    value = value - factor[k, i] * back[k]
                back[i] = value
            value = jnp.where(group, 0.0, tiles[p + 2])
            for m in range(8):
                value = value - along_lanes(tiles[p + 2], base + m) * back[m]
            tiles[p + 2] = value
            if p + 3 < count:
                spread = [stacked(back), jnp.zeros((LANES - 8 - base, LANES), F32)]
                if base:
                    spread = [jnp.zeros((base, LANES), F32)] + spread
                made = split_dot(
                    jnp.concatenate(tiles[p + 3 :], axis=0), jnp.concatenate(spread, axis=0)
                )
                for i in range(p + 3, count):
                    row = 8 * (i - p - 3)
                    tiles[i] = jnp.where(group, 0.0, tiles[i]) - made[row : row + 8, :]
        if following is not None:
            tiles[p + 1] = following
    return done


def inverse_kernel(over, mine_ref, other_ref, out_ref, work, small):
    half = mine_ref.shape[0]
    side = lax.rem(lax.axis_index("domain"), 2)
    size = work.shape[0]
    blocks = size // LANES
    at = 0
    for i in range(blocks):
        for j in range(i + 1):
            here = slice(at % half, at % half + LANES)
            block = jnp.where(side == at // half, mine_ref[here, :], other_ref[here, :]) * over
            work[i * LANES : (i + 1) * LANES, j * LANES : (j + 1) * LANES] = block
            if i != j:
                work[j * LANES : (j + 1) * LANES, i * LANES : (i + 1) * LANES] = block.T
            at += LANES
    out_ref[...] = jnp.zeros_like(out_ref)
    lane = lax.broadcasted_iota(jnp.int32, (8, LANES), 1)

    def step(k, _):
        base = pl.multiple_of(k * LANES, LANES)
        tiles = [
            work[pl.ds(pl.multiple_of(base + 8 * i, 8), 8), pl.ds(base, LANES)]
            for i in range(LANES // 8)
        ]
        for i, tile in enumerate(small_inverse(tiles, lane)):
            small[8 * i : 8 * i + 8, :] = tile
        for which in range(blocks):

            @pl.when(k == which)
            def _():
                a, b = which * LANES, (which + 1) * LANES
                diagonal = small[...]
                out_ref[a:b, a:b] = diagonal
                if which:
                    left = split_dot(diagonal, work[a:b, 0:a])
                    out_ref[a:b, 0:a] = left
                if b < size:
                    right = split_dot(diagonal, work[a:b, b:size])
                    column = split_dot(work[b:size, a:b], diagonal, (((1,), (1,)), ((), ())))
                    work[b:size, b:size] = work[b:size, b:size] - split_dot(column, right)
                    work[b:size, a:b] = -split_dot(column, diagonal)
                    if which:
                        work[b:size, 0:a] = work[b:size, 0:a] - split_dot(column, left)

        return 0

    lax.fori_loop(0, blocks, step, 0)


def inverse_factor(mine, other, size, over):
    return pl.pallas_call(
        functools.partial(inverse_kernel, over),
        out_shape=jax.ShapeDtypeStruct((size, size), F32),
        in_specs=[VM, VM],
        out_specs=VM,
        scratch_shapes=[
            pltpu.VMEM((size, size), F32),
            pltpu.VMEM((LANES, LANES), F32),
        ],
        compiler_params=params(16),
        cost_estimate=cost(0, 70 << 20),
        name="inverse_factor",
    )(mine, other)


def output_kernel(factor_ref, *refs):
    band = lax.axis_index("band")
    out_ref, blocks_ref, made_ref, sems = refs[-4:]
    count = factor_ref.shape[0] // LANES
    firsts, rests = refs[:count], refs[count:-4]
    rows = firsts[0].shape[0]
    row = pl.ds(pl.multiple_of(band * LANES, LANES), LANES)
    for s in range(count):
        source = band - s
        column = pl.ds(pl.multiple_of(jnp.maximum(source, 0) * LANES, LANES), LANES)
        block = jnp.where(source >= 0, factor_ref[row, column], 0.0).T
        high = block.astype(BF16)
        here = slice(s * LANES, (s + 1) * LANES)
        blocks_ref[here, 0:LANES] = high
        blocks_ref[here, LANES:] = (block - high.astype(F32)).astype(BF16)
    copies = []
    for j in range(count):
        here = slice((j - 1) * rows, j * rows)
        pieces = [piece[...] for piece in firsts] if j == 0 else [piece[here, :] for piece in rests]
        made = jnp.dot(
            jnp.concatenate(pieces, axis=1), blocks_ref[...], preferred_element_type=F32
        )
        made_ref[j] = made[:, 0:LANES] + made[:, LANES:]
        start = pl.multiple_of(lax.rem(band + j, count) * rows, rows)
        copies.append(
            pltpu.make_async_copy(made_ref.at[j], out_ref.at[pl.ds(start, rows), :], sems.at[j])
        )
        copies[-1].start()
    for copy in copies:
        copy.wait()


def output(factor, firsts, rests):
    count = len(firsts)
    rows = firsts[0].shape[0]
    return pl.pallas_call(
        output_kernel,
        out_shape=jax.ShapeDtypeStruct((rows * count, LANES), F32),
        in_specs=[VM] * (1 + 2 * count),
        out_specs=pl.BlockSpec(memory_space=pl.ANY),
        scratch_shapes=[
            pltpu.VMEM((count * LANES, 2 * LANES), BF16),
            pltpu.VMEM((count, rows, LANES), F32),
            pltpu.SemaphoreType.DMA((count,)),
        ],
        compiler_params=params(24),
        cost_estimate=cost(0, 10 << 20),
        name="output",
    )(factor, *firsts, *rests)


def shards(states_block, cell_matrix, cell_scale, potential, connectivity, boundary_nodes):
    owned = states_block.shape[0]
    count = lax.axis_size("band")
    levels = potential.reshape(owned // LANES, LANES)

    start, words = prepare(boundary_nodes, states_block, connectivity)
    operator = functools.partial(apply_operator, words, cell_scale, cell_matrix, levels)
    sums, back = operator(*start)
    sums, back = operator(*first_term(boundary_nodes, sums, back))
    pieces, rest = second_term(boundary_nodes, sums, back, states_block, count)

    firsts = [pieces[0]] + [shifted(pieces[s], "band", s) for s in range(1, count)]
    firsts = list(ordered(*firsts))
    rests = [rest]
    keep, send = partial_gram(firsts)
    mine, other = summed_beside(keep, send, rests, firsts)
    over = 1.0 / (owned * lax.axis_size("domain"))
    factor = inverse_factor(mine, other, count * LANES, over)
    return output(factor, firsts, rests)


def solution(mesh):
    return jax.shard_map(
        shards,
        mesh=mesh,
        in_specs=(
            P("domain", "band"),
            P(),
            P("domain"),
            P("domain"),
            P("domain", None),
            P("domain"),
        ),
        out_specs=P("domain", "band"),
        check_vma=False,
    )
```

```python
import functools

import jax
import jax.numpy as jnp
from jax import lax
from jax.experimental import pallas as pl
from jax.experimental.pallas import tpu as pltpu
from jax.sharding import PartitionSpec as P

CENTER = 1.5
HALF_WIDTH = 1.25
LANES = 128
CHAINS = 7
F32 = jnp.float32
BF16 = jnp.bfloat16
VM = pl.BlockSpec(memory_space=pltpu.VMEM)
SM = pl.BlockSpec(memory_space=pltpu.SMEM)


def params(mebibytes):
    return pltpu.CompilerParams(vmem_limit_bytes=mebibytes << 20)


def cost(flops, moved):
    return pl.CostEstimate(flops=flops, bytes_accessed=moved, transcendentals=0)


def shifted(value, axis, steps):
    count = lax.axis_size(axis)
    return lax.ppermute(value, axis, [(i, (i + steps) % count) for i in range(count)])


def spread_levels(potential_ref, block):
    return jnp.broadcast_to(potential_ref[block : block + 1, :], (LANES, LANES)).T - CENTER


def rows_out(rows_of, potential_ref, owned, base_ref, ext_ref):
    for block in range(owned // LANES):
        here = slice(block * LANES, (block + 1) * LANES)
        wide = rows_of(here)
        base_ref[here, :] = spread_levels(potential_ref, block) * wide
        ext_ref[here, :] = wide.astype(BF16).astype(F32)
    base_ref[owned:, :] = jnp.zeros_like(base_ref[owned:, :])


def prepare_kernel(nodes, rows_ref, links_ref, ext_ref, edge_ref, words_ref, picked):
    owned = rows_ref.shape[0]
    ext_ref[0:owned, :] = rows_ref[...].astype(F32)
    pack_links(links_ref, words_ref)

    def body(step, _):
        for k in range(16):
            i = step * 16 + k
            picked[pl.ds(i, 1), :] = ext_ref[pl.ds(nodes[i], 1), :]
        return 0

    lax.fori_loop(0, nodes.shape[0] // 16, body, 0)
    edge_ref[...] = picked[...].astype(BF16)


def prepare(nodes, rows, links):
    owned, plane = rows.shape[0], nodes.shape[0]
    cells, npc = links.shape
    groups = ((npc + 1) // 2 + LANES - 1) // LANES
    ext, edge, words = pl.pallas_call(
        prepare_kernel,
        out_shape=(
            jax.ShapeDtypeStruct((owned + plane, LANES), F32),
            jax.ShapeDtypeStruct((plane, LANES), BF16),
            jax.ShapeDtypeStruct((groups * cells, LANES), jnp.int32),
        ),
        in_specs=[SM, VM, VM],
        out_specs=(VM, VM, VM),
        scratch_shapes=[pltpu.VMEM((plane, LANES), F32)],
        compiler_params=params(8),
        cost_estimate=cost(0, 12 << 20),
        name="prepare",
    )(nodes, rows, links)
    return (ext, ext, edge), words.reshape(-1)


def pack_links(links_ref, words_ref):
    cells, npc = links_ref.shape
    half = (npc + 1) // 2
    early = links_ref[:, 0:half]
    late = jnp.concatenate(
        [links_ref[:, half:npc], jnp.zeros((cells, 2 * half - npc), jnp.int32)], axis=1
    )
    words = early | (late << 16)
    for k in range(0, half, LANES):
        width = min(LANES, half - k)
        words_ref[k // LANES * cells : (k // LANES + 1) * cells, 0:width] = words[:, k : k + width]


def each_row(words, cells, npc, cell, visit):
    half = (npc + 1) // 2
    base = cell * LANES
    for r in range(half):
        word = words[base + (r // LANES * cells * LANES + r % LANES)]
        visit(r, pl.ds(word & 0xFFFF, 1))
        if r + half < npc:
            visit(r + half, pl.ds(word >> 16, 1))


def gather_cells(words, cells, npc, ext_ref, gathered, first):
    def cell(c, _):
        def visit(r, row):
            gathered[c, r : r + 1, :] = ext_ref[row, :]

        each_row(words, cells, npc, first + c, visit)
        return 0

    lax.fori_loop(0, gathered.shape[0], cell, 0)


def multiply_cells(scale, matrix_ref, gathered, products, first):
    cells, npc = gathered.shape[0], matrix_ref.shape[0]
    for c in range(0, cells, 2):
        both = jnp.concatenate(
            [gathered[c, 0:npc, :].astype(BF16), gathered[c + 1, 0:npc, :].astype(BF16)], axis=1
        )
        made = jnp.dot(matrix_ref[...], both, preferred_element_type=F32)
        for half in range(2):
            products[c + half, 0:npc, :] = (
                made[:, half * LANES : (half + 1) * LANES] * scale[first + c + half]
            )


def scatter_cells(words, cells, npc, products, sums, first):
    def cell(c, _):
        seen = []

        def visit(r, row):
            total = sums[len(seen) % len(sums)]
            seen.append(r)
            total[row, :] = total[row, :] + products[c, r : r + 1, :]

        each_row(words, cells, npc, first + c, visit)
        return 0

    lax.fori_loop(0, products.shape[0], cell, 0)


def near_products_kernel(words, scale, ext_ref, matrix_ref, out_ref, gathered):
    gather_cells(words, 2 * gathered.shape[0], matrix_ref.shape[0], ext_ref, gathered, 0)
    multiply_cells(scale, matrix_ref, gathered, out_ref, 0)


def far_cells_kernel(
    words_ref, scale, ext_ref, ghost_ref, matrix_ref, wide_ref, potential_ref, out_ref, back_ref,
    ext, gathered, products, words, sem, *sums
):
    copy = pltpu.make_async_copy(words_ref, words, sem)
    copy.start()
    owned = out_ref.shape[0]
    half, npc = gathered.shape[0], matrix_ref.shape[0]
    ext[0:owned, :] = ext_ref[0:owned, :]
    ext[owned:, :] = ghost_ref[...].astype(F32)
    for block in range(owned // LANES):
        here = slice(block * LANES, (block + 1) * LANES)
        sums[0][here, :] = spread_levels(potential_ref, block) * wide_ref[here, :]
    sums[0][owned:, :] = jnp.zeros_like(sums[0][owned:, :])
    for total in sums[1:]:
        total[...] = jnp.zeros_like(total)
    copy.wait()
    gather_cells(words, 2 * half, npc, ext, gathered, half)
    multiply_cells(scale, matrix_ref, gathered, products, half)
    scatter_cells(words, 2 * half, npc, products, sums, half)
    back_ref[...] = sum(total[owned:, :] for total in sums).astype(BF16)
    out_ref[...] = sum(total[0:owned, :] for total in sums)


def near_sums_kernel(npc, words_ref, products_ref, start_ref, out_ref, words, sem, *sums):
    copy = pltpu.make_async_copy(words_ref, words, sem)
    copy.start()
    sums = (out_ref,) + sums
    out_ref[...] = start_ref[...]
    for total in sums[1:]:
        total[...] = jnp.zeros_like(total)
    copy.wait()
    scatter_cells(words, 2 * products_ref.shape[0], npc, products_ref, sums, 0)
    out_ref[...] = sum(total[...] for total in sums)


def apply_operator(links, scale, matrix, potential, wide, ext, edge):
    cells, npc = scale.shape[0], matrix.shape[0]
    half, padded = cells // 2, (npc + 7) // 8 * 8
    plane = edge.shape[0]
    whole = ext.shape
    owned = whole[0] - plane
    held = (half, padded, LANES)
    ghost = shifted(edge, "domain", -1)
    index = [pltpu.SMEM(links.shape, jnp.int32), pltpu.SemaphoreType.DMA]
    products = pl.pallas_call(
        near_products_kernel,
        out_shape=jax.ShapeDtypeStruct(held, F32),
        in_specs=[SM, SM, VM, VM],
        out_specs=VM,
        scratch_shapes=[pltpu.VMEM(held, F32)],
        compiler_params=params(16),
        cost_estimate=cost(0, 14 << 20),
        name="near_products",
    )(links, scale, ext, matrix)
    ghost, products = ordered(ghost, products)
    sums, back = pl.pallas_call(
        far_cells_kernel,
        out_shape=(
            jax.ShapeDtypeStruct((owned, LANES), F32),
            jax.ShapeDtypeStruct((plane, LANES), BF16),
        ),
        in_specs=[VM, SM, VM, VM, VM, VM, VM],
        out_specs=(VM, VM),
        scratch_shapes=[pltpu.VMEM(whole, F32), pltpu.VMEM(held, F32), pltpu.VMEM(held, F32)]
        + index
        + [pltpu.VMEM(whole, F32)] * CHAINS,
        compiler_params=params(22),
        cost_estimate=cost(0, 28 << 20),
        name="far_cells",
    )(links, scale, ext, ghost, matrix, wide, potential)
    back = shifted(back, "domain", 1)
    sums = pl.pallas_call(
        functools.partial(near_sums_kernel, npc),
        out_shape=jax.ShapeDtypeStruct((owned, LANES), F32),
        in_specs=[VM] * 3,
        out_specs=VM,
        scratch_shapes=index + [pltpu.VMEM((owned, LANES), F32)] * (CHAINS - 1),
        compiler_params=params(16),
        cost_estimate=cost(0, 14 << 20),
        name="near_sums",
    )(links, products, sums)
    return sums, back


def add_back(nodes, target, back_ref, factor, scaled, picked=None):
    scaled[...] = back_ref[...].astype(F32) * factor

    def body(step, _):
        at = [step * 16 + k for k in range(16)]
        rows = [pl.ds(nodes[i], 1) for i in at]
        new = [target[r, :] + scaled[pl.ds(i, 1), :] for i, r in zip(at, rows)]
        for i, r, value in zip(at, rows, new):
            target[r, :] = value
            if picked is not None:
                picked[pl.ds(i, 1), :] = value
        return 0

    lax.fori_loop(0, nodes.shape[0] // 16, body, 0)


def first_kernel(nodes, sums_ref, back_ref, term_ref, ext_ref, edge_ref, scaled, picked):
    owned = sums_ref.shape[0]
    term_ref[...] = sums_ref[...] * (1.0 / HALF_WIDTH)
    add_back(nodes, term_ref, back_ref, 1.0 / HALF_WIDTH, scaled, picked)
    edge_ref[...] = picked[...].astype(BF16)
    ext_ref[0:owned, :] = term_ref[...].astype(BF16).astype(F32)


def first_term(nodes, sums, back):
    owned, plane = sums.shape[0], nodes.shape[0]
    return pl.pallas_call(
        first_kernel,
        out_shape=(
            jax.ShapeDtypeStruct((owned, LANES), F32),
            jax.ShapeDtypeStruct((owned + plane, LANES), F32),
            jax.ShapeDtypeStruct((plane, LANES), BF16),
        ),
        in_specs=[SM, VM, VM],
        out_specs=(VM, VM, VM),
        scratch_shapes=[pltpu.VMEM((plane, LANES), F32)] * 2,
        compiler_params=params(16),
        cost_estimate=cost(0, 8 << 20),
        name="first_term",
    )(nodes, sums, back)


def second_kernel(nodes, sums_ref, back_ref, previous_ref, *refs):
    pieces, (rest_ref, total, scaled) = refs[:-3], refs[-3:]
    total[...] = sums_ref[...] * (2.0 / HALF_WIDTH) - previous_ref[...].astype(F32)
    add_back(nodes, total, back_ref, 2.0 / HALF_WIDTH, scaled)
    count = len(pieces)
    rows = total.shape[0] // count
    for k, piece in enumerate(pieces):
        start = pl.multiple_of(lax.rem(lax.axis_index("band") + k, count) * rows, rows)
        part = total[pl.ds(start, rows), :].astype(BF16)
        piece[...] = part
        if k:
            rest_ref[(k - 1) * rows : k * rows, :] = part


def second_term(nodes, sums, back, previous, count):
    owned = sums.shape[0]
    rows = owned // count
    made = pl.pallas_call(
        second_kernel,
        out_shape=[jax.ShapeDtypeStruct((rows, LANES), BF16)] * count
        + [jax.ShapeDtypeStruct((owned - rows, LANES), BF16)],
        in_specs=[SM, VM, VM, VM],
        out_specs=[VM] * (count + 1),
        scratch_shapes=[pltpu.VMEM(sums.shape, F32), pltpu.VMEM(back.shape, F32)],
        compiler_params=params(16),
        cost_estimate=cost(0, 6 << 20),
        name="second_term",
    )(nodes, sums, back, previous)
    return made[:count], made[count]


def gram_kernel(*refs):
    pieces, (keep_ref, send_ref, held) = refs[:-3], refs[-3:]
    count = len(pieces)
    for s, piece in enumerate(pieces):
        held[lax.rem(lax.axis_index("band") + (count - s), count)] = piece[...]
    half = keep_ref.shape[0]

    def write(*halves):
        at = 0
        for i in range(count):
            for j in range(i + 1):
                halves[at // half][at % half : at % half + LANES, :] = lax.dot_general(
                    held[i], held[j], (((0,), (0,)), ((), ())), preferred_element_type=F32
                )
                at += LANES

    side = lax.rem(lax.axis_index("domain"), 2)
    pl.when(side == 0)(lambda: write(keep_ref, send_ref))
    pl.when(side != 0)(lambda: write(send_ref, keep_ref))


def partial_gram(pieces):
    count = len(pieces)
    rows = count * (count + 1) // 2 * LANES
    return pl.pallas_call(
        gram_kernel,
        out_shape=[jax.ShapeDtypeStruct((rows // 2, LANES), F32)] * 2,
        in_specs=[VM] * count,
        out_specs=[VM] * 2,
        scratch_shapes=[pltpu.VMEM((count,) + pieces[0].shape, BF16)],
        compiler_params=params(16),
        cost_estimate=cost(0, 4 << 20),
        name="partial_gram",
    )(*pieces)


def quarters_kernel(a_ref, b_ref, *refs):
    outs, total = refs[:-1], refs[-1]
    total[...] = a_ref[...] + b_ref[...]
    rows = outs[0].shape[0]
    place = lax.axis_index("domain") // 2
    for m, out in enumerate(outs):
        out[...] = total[pl.ds(pl.multiple_of((place ^ m) * rows, rows), rows), :]


def quarters(a, b, count):
    rows = a.shape[0] // count
    return pl.pallas_call(
        quarters_kernel,
        out_shape=[jax.ShapeDtypeStruct((rows, LANES), F32)] * count,
        in_specs=[VM, VM],
        out_specs=[VM] * count,
        scratch_shapes=[pltpu.VMEM(a.shape, F32)],
        compiler_params=params(4),
        cost_estimate=cost(0, 1 << 20),
        name="quarters",
    )(a, b)


def joined_kernel(*refs):
    parts, out_ref = refs[:-1], refs[-1]
    rows = parts[0].shape[0]
    place = lax.axis_index("domain") // 2
    for m, part in enumerate(parts):
        out_ref[pl.ds(pl.multiple_of((place ^ m) * rows, rows), rows), :] = part[...]


def joined(parts):
    rows = parts[0].shape[0] * len(parts)
    return pl.pallas_call(
        joined_kernel,
        out_shape=jax.ShapeDtypeStruct((rows, LANES), F32),
        in_specs=[VM] * len(parts),
        out_specs=VM,
        compiler_params=params(4),
        cost_estimate=cost(0, 1 << 20),
        name="joined",
    )(*parts)


def paired(value, axis, mask):
    count = lax.axis_size(axis)
    return lax.ppermute(value, axis, [(i, i ^ mask) for i in range(count)])


def passed_up(rests, firsts, held):
    rows = firsts[held].shape[0]
    count = lax.axis_size("band")
    onward = jnp.concatenate([rests[held][rows:], firsts[held]])
    return lax.ppermute(onward, "band", [(i, i + 1) for i in range(held, count - 1)])


def ordered(*values):
    return lax.optimization_barrier(values)


def summed_beside(keep, send, rests, firsts):
    count = lax.axis_size("band")
    half = keep + paired(send, "domain", 1)
    if lax.axis_size("domain") != 8 or count != 4:
        for held in range(count - 1):
            rests.append(passed_up(rests, firsts, held))
        side = lax.axis_index("domain") % 2
        both = jnp.stack([half, jnp.zeros_like(half)])
        both = lax.psum(jnp.where(side == 0, both, both[::-1]) * 1.0, ("domain", "band"))
        return both[side], both[1 - side]
    rests.append(passed_up(rests, firsts, 0))
    total, *others = quarters(keep, paired(send, "domain", 1), 4)
    for part in [paired(other, "domain", 2 * m) for m, other in enumerate(others, 1)]:
        total = total + part
    parts = [total] + [shifted(total, "band", s) for s in range(1, count)]
    parts[1], rests[1] = ordered(parts[1], rests[1])
    rests.append(passed_up(rests, firsts, 1))
    rows = firsts[1].shape[0]
    skipping = jnp.concatenate([rests[1][2 * rows :], firsts[1], rests[1][:rows]])
    rests.append(lax.ppermute(skipping, "band", [(1, 3)]))
    total = sum(parts[1:], parts[0])
    half = joined([total] + [paired(total, "domain", 2 * m) for m in (1, 2, 3)])
    return half, paired(half, "domain", 1)


def split_dot(a, b, dims=(((1,), (0,)), ((), ()))):
    def parts(x):
        high = x.astype(BF16)
        return high, (x - high.astype(F32)).astype(BF16)

    def dot(x, y):
        return lax.dot_general(x, y, dims, preferred_element_type=F32)

    (a_high, a_low), (b_high, b_low) = parts(a), parts(b)
    return dot(a_high, b_high) + (dot(a_high, b_low) + dot(a_low, b_high))


def small_inverse(tiles, lane):
    count, tiles, done = len(tiles), list(tiles), []
    shape = tiles[0].shape
    sub = lax.broadcasted_iota(jnp.int32, shape, 0)

    def along_lanes(tile, column):
        return jnp.broadcast_to(tile[:, column : column + 1], shape)

    def along_rows(tile, row):
        return jnp.broadcast_to(tile[row : row + 1, :], shape)

    def stacked(rows):
        tile = rows[0]
        for i in range(1, 8):
            tile = jnp.where(sub == i, rows[i], tile)
        return tile

    columns = [along_lanes(tiles[0], m) for m in range(8)]
    for p in range(count):
        base = 8 * p
        group = (lane >= base) & (lane < base + 8)
        entry = {(i, j): along_rows(columns[j], i) for j in range(8) for i in range(j, 8)}
        start = jnp.where(group, (lane - base == sub).astype(F32), tiles[p])
        solved = [along_rows(start, i) for i in range(8)]
        following = None
        if p + 1 < count:
            ahead = [along_lanes(tiles[p + 1], base + m) for m in range(8)]
            columns = [along_lanes(tiles[p + 1], base + 8 + m) for m in range(8)]
            following = jnp.where(group, 0.0, tiles[p + 1])
        inverse, factor = [], {}
        for j in range(8):
            pivot = 1.0 / entry[j, j]
            inverse.append(pivot)
            if following is not None:
                scaled = ahead[j] * pivot
                columns = [c - scaled * along_rows(ahead[j], m) for m, c in enumerate(columns)]
                following = following - scaled * solved[j]
                for m in range(j + 1, 8):
                    ahead[m] = ahead[m] - scaled * entry[m, j]
            for i in range(j + 1, 8):
                factor[i, j] = entry[i, j] * pivot
            for i in range(j + 1, 8):
                for k in range(j + 1, i + 1):
                    entry[i, k] = entry[i, k] - factor[i, j] * entry[k, j]
                solved[i] = solved[i] - factor[i, j] * solved[j]
        result = stacked([solved[i] * lax.rsqrt(entry[i, i]) for i in range(8)])
        done.append(jnp.where(lane <= base + sub, result, 0.0))
        if p + 2 < count:
            back = [None] * 8
            for i in range(7, -1, -1):
                value = solved[i] * inverse[i]
                for k in range(i + 1, 8):
                    value = value - factor[k, i] * back[k]
                back[i] = value
            value = jnp.where(group, 0.0, tiles[p + 2])
            for m in range(8):
                value = value - along_lanes(tiles[p + 2], base + m) * back[m]
            tiles[p + 2] = value
            if p + 3 < count:
                spread = [stacked(back), jnp.zeros((LANES - 8 - base, LANES), F32)]
                if base:
                    spread = [jnp.zeros((base, LANES), F32)] + spread
                made = split_dot(
                    jnp.concatenate(tiles[p + 3 :], axis=0), jnp.concatenate(spread, axis=0)
                )
                for i in range(p + 3, count):
                    row = 8 * (i - p - 3)
                    tiles[i] = jnp.where(group, 0.0, tiles[i]) - made[row : row + 8, :]
        if following is not None:
            tiles[p + 1] = following
    return done


def inverse_kernel(over, mine_ref, other_ref, out_ref, work, small):
    half = mine_ref.shape[0]
    side = lax.rem(lax.axis_index("domain"), 2)
    size = work.shape[0]
    blocks = size // LANES
    at = 0
    for i in range(blocks):
        for j in range(i + 1):
            here = slice(at % half, at % half + LANES)
            block = jnp.where(side == at // half, mine_ref[here, :], other_ref[here, :]) * over
            work[i * LANES : (i + 1) * LANES, j * LANES : (j + 1) * LANES] = block
            if i != j:
                work[j * LANES : (j + 1) * LANES, i * LANES : (i + 1) * LANES] = block.T
            at += LANES
    out_ref[...] = jnp.zeros_like(out_ref)
    lane = lax.broadcasted_iota(jnp.int32, (8, LANES), 1)

    def step(k, _):
        base = pl.multiple_of(k * LANES, LANES)
        tiles = [
            work[pl.ds(pl.multiple_of(base + 8 * i, 8), 8), pl.ds(base, LANES)]
            for i in range(LANES // 8)
        ]
        for i, tile in enumerate(small_inverse(tiles, lane)):
            small[8 * i : 8 * i + 8, :] = tile
        for which in range(blocks):

            @pl.when(k == which)
            def _():
                a, b = which * LANES, (which + 1) * LANES
                diagonal = small[...]
                out_ref[a:b, a:b] = diagonal
                if which:
                    left = split_dot(diagonal, work[a:b, 0:a])
                    out_ref[a:b, 0:a] = left
                if b < size:
                    right = split_dot(diagonal, work[a:b, b:size])
                    column = split_dot(work[b:size, a:b], diagonal, (((1,), (1,)), ((), ())))
                    work[b:size, b:size] = work[b:size, b:size] - split_dot(column, right)
                    work[b:size, a:b] = -split_dot(column, diagonal)
                    if which:
                        work[b:size, 0:a] = work[b:size, 0:a] - split_dot(column, left)

        return 0

    lax.fori_loop(0, blocks, step, 0)


def inverse_factor(mine, other, size, over):
    return pl.pallas_call(
        functools.partial(inverse_kernel, over),
        out_shape=jax.ShapeDtypeStruct((size, size), F32),
        in_specs=[VM, VM],
        out_specs=VM,
        scratch_shapes=[
            pltpu.VMEM((size, size), F32),
            pltpu.VMEM((LANES, LANES), F32),
        ],
        compiler_params=params(16),
        cost_estimate=cost(0, 70 << 20),
        name="inverse_factor",
    )(mine, other)


def factor_blocks(factor_ref, blocks_ref, sources):
    band = lax.axis_index("band")
    row = pl.ds(pl.multiple_of(band * LANES, LANES), LANES)
    for k, s in enumerate(sources):
        source = band - s
        column = pl.ds(pl.multiple_of(jnp.maximum(source, 0) * LANES, LANES), LANES)
        block = jnp.where(source >= 0, factor_ref[row, column], 0.0).T
        high = block.astype(BF16)
        here = slice(k * LANES, (k + 1) * LANES)
        blocks_ref[here, 0:LANES] = high
        blocks_ref[here, LANES:] = (block - high.astype(F32)).astype(BF16)


def both_parts(pieces, blocks):
    made = jnp.dot(jnp.concatenate(pieces, axis=1), blocks, preferred_element_type=F32)
    return made[:, 0:LANES] + made[:, LANES:]


def early_kernel(factor_ref, *refs):
    made_ref, blocks_ref = refs[-2:]
    count = made_ref.shape[0]
    firsts, rests = refs[:count], refs[count:-2]
    rows = made_ref.shape[1]
    factor_blocks(factor_ref, blocks_ref, range(count))
    made_ref[0] = both_parts([first[...] for first in firsts], blocks_ref[...])
    for j in range(1, count):
        pieces = [rest[(j - 1) * rows : j * rows, :] for rest in rests]
        made_ref[j] = both_parts(pieces, blocks_ref[0 : len(rests) * LANES, :])


def late_kernel(factor_ref, early_ref, *refs):
    out_ref, blocks_ref, made_ref, sems = refs[-4:]
    rests = refs[:-4]
    count, rows = early_ref.shape[:2]
    band = lax.axis_index("band")

    def put(source, j):
        start = pl.multiple_of(lax.rem(band + j, count) * rows, rows)
        copy = pltpu.make_async_copy(source, out_ref.at[pl.ds(start, rows), :], sems.at[j])
        copy.start()
        return copy

    copies = [put(early_ref.at[0], 0)]
    factor_blocks(factor_ref, blocks_ref, range(count - len(rests), count))
    for j in range(1, count):
        pieces = [rest[(j - 1) * rows : j * rows, :] for rest in rests]
        made_ref[j - 1] = early_ref[j] + both_parts(pieces, blocks_ref[...])
        copies.append(put(made_ref.at[j - 1], j))
    for copy in copies:
        copy.wait()


def output(factor, firsts, rests):
    count = len(firsts)
    rows = firsts[0].shape[0]
    soon = (count + 1) // 2
    early = pl.pallas_call(
        early_kernel,
        out_shape=jax.ShapeDtypeStruct((count, rows, LANES), F32),
        in_specs=[VM] * (1 + count + soon),
        out_specs=VM,
        scratch_shapes=[pltpu.VMEM((count * LANES, 2 * LANES), BF16)],
        compiler_params=params(16),
        cost_estimate=cost(0, 6 << 20),
        name="output_early",
    )(factor, *firsts, *rests[:soon])
    return pl.pallas_call(
        late_kernel,
        out_shape=jax.ShapeDtypeStruct((rows * count, LANES), F32),
        in_specs=[VM] * (2 + count - soon),
        out_specs=pl.BlockSpec(memory_space=pl.ANY),
        scratch_shapes=[
            pltpu.VMEM(((count - soon) * LANES, 2 * LANES), BF16),
            pltpu.VMEM((count - 1, rows, LANES), F32),
            pltpu.SemaphoreType.DMA((count,)),
        ],
        compiler_params=params(16),
        cost_estimate=cost(0, 6 << 20),
        name="output_late",
    )(factor, early, *rests[soon:])


def shards(states_block, cell_matrix, cell_scale, potential, connectivity, boundary_nodes):
    owned = states_block.shape[0]
    count = lax.axis_size("band")
    levels = potential.reshape(owned // LANES, LANES)

    start, words = prepare(boundary_nodes, states_block, connectivity)
    operator = functools.partial(apply_operator, words, cell_scale, cell_matrix, levels)
    sums, back = operator(*start)
    sums, back = operator(*first_term(boundary_nodes, sums, back))
    pieces, rest = second_term(boundary_nodes, sums, back, states_block, count)

    firsts = [pieces[0]] + [shifted(pieces[s], "band", s) for s in range(1, count)]
    firsts = list(ordered(*firsts))
    rests = [rest]
    keep, send = partial_gram(firsts)
    mine, other = summed_beside(keep, send, rests, firsts)
    over = 1.0 / (owned * lax.axis_size("domain"))
    factor = inverse_factor(mine, other, count * LANES, over)
    return output(factor, firsts, rests)


def solution(mesh):
    return jax.shard_map(
        shards,
        mesh=mesh,
        in_specs=(
            P("domain", "band"),
            P(),
            P("domain"),
            P("domain"),
            P("domain", None),
            P("domain"),
        ),
        out_specs=P("domain", "band"),
        check_vma=False,
    )
```

```python
import functools

import jax
import jax.numpy as jnp
from jax import lax
from jax.experimental import pallas as pl
from jax.experimental.pallas import tpu as pltpu
from jax.sharding import PartitionSpec as P

CENTER = 1.5
HALF_WIDTH = 1.25
LANES = 128
CHAINS = 7
F32 = jnp.float32
BF16 = jnp.bfloat16
VM = pl.BlockSpec(memory_space=pltpu.VMEM)
SM = pl.BlockSpec(memory_space=pltpu.SMEM)


def params(mebibytes):
    return pltpu.CompilerParams(vmem_limit_bytes=mebibytes << 20)


def cost(flops, moved):
    return pl.CostEstimate(flops=flops, bytes_accessed=moved, transcendentals=0)


def shifted(value, axis, steps):
    count = lax.axis_size(axis)
    return lax.ppermute(value, axis, [(i, (i + steps) % count) for i in range(count)])


def spread_levels(potential_ref, block):
    return jnp.broadcast_to(potential_ref[block : block + 1, :], (LANES, LANES)).T - CENTER


def rows_out(rows_of, potential_ref, owned, base_ref, ext_ref):
    for block in range(owned // LANES):
        here = slice(block * LANES, (block + 1) * LANES)
        wide = rows_of(here)
        base_ref[here, :] = spread_levels(potential_ref, block) * wide
        ext_ref[here, :] = wide.astype(BF16).astype(F32)
    base_ref[owned:, :] = jnp.zeros_like(base_ref[owned:, :])


def prepare_kernel(nodes, rows_ref, links_ref, ext_ref, edge_ref, words_ref, picked):
    owned = rows_ref.shape[0]
    ext_ref[0:owned, :] = rows_ref[...].astype(F32)
    pack_links(links_ref, words_ref)

    def body(step, _):
        for k in range(16):
            i = step * 16 + k
            picked[pl.ds(i, 1), :] = ext_ref[pl.ds(nodes[i], 1), :]
        return 0

    lax.fori_loop(0, nodes.shape[0] // 16, body, 0)
    edge_ref[...] = picked[...].astype(BF16)


def prepare(nodes, rows, links):
    owned, plane = rows.shape[0], nodes.shape[0]
    cells, npc = links.shape
    groups = ((npc + 1) // 2 + LANES - 1) // LANES
    ext, edge, words = pl.pallas_call(
        prepare_kernel,
        out_shape=(
            jax.ShapeDtypeStruct((owned + plane, LANES), F32),
            jax.ShapeDtypeStruct((plane, LANES), BF16),
            jax.ShapeDtypeStruct((groups * cells, LANES), jnp.int32),
        ),
        in_specs=[SM, VM, VM],
        out_specs=(VM, VM, VM),
        scratch_shapes=[pltpu.VMEM((plane, LANES), F32)],
        compiler_params=params(8),
        cost_estimate=cost(0, 12 << 20),
        name="prepare",
    )(nodes, rows, links)
    return (ext, ext, edge), words.reshape(-1)


def pack_links(links_ref, words_ref):
    cells, npc = links_ref.shape
    half = (npc + 1) // 2
    early = links_ref[:, 0:half]
    late = jnp.concatenate(
        [links_ref[:, half:npc], jnp.zeros((cells, 2 * half - npc), jnp.int32)], axis=1
    )
    words = early | (late << 16)
    for k in range(0, half, LANES):
        width = min(LANES, half - k)
        words_ref[k // LANES * cells : (k // LANES + 1) * cells, 0:width] = words[:, k : k + width]


def each_row(words, cells, npc, cell, visit):
    half = (npc + 1) // 2
    base = cell * LANES
    for r in range(half):
        word = words[base + (r // LANES * cells * LANES + r % LANES)]
        visit(r, pl.ds(word & 0xFFFF, 1))
        if r + half < npc:
            visit(r + half, pl.ds(word >> 16, 1))


def gather_cells(words, cells, npc, ext_ref, gathered, first):
    def cell(c, _):
        def visit(r, row):
            gathered[c, r : r + 1, :] = ext_ref[row, :]

        each_row(words, cells, npc, first + c, visit)
        return 0

    lax.fori_loop(0, gathered.shape[0], cell, 0)


def multiply_cells(matrix_ref, gathered, products):
    cells, npc = gathered.shape[0], matrix_ref.shape[0]
    for c in range(0, cells, 2):
        both = jnp.concatenate(
            [gathered[c, 0:npc, :].astype(BF16), gathered[c + 1, 0:npc, :].astype(BF16)], axis=1
        )
        made = jnp.dot(matrix_ref[...], both, preferred_element_type=F32)
        for half in range(2):
            products[c + half, 0:npc, :] = made[:, half * LANES : (half + 1) * LANES]


def scatter_cells(words, scale, cells, npc, products, sums, first):
    def cell(c, _):
        seen = []
        factor = jnp.full((1, LANES), scale[first + c], F32)

        def visit(r, row):
            total = sums[len(seen) % len(sums)]
            seen.append(r)
            total[row, :] = total[row, :] + factor * products[c, r : r + 1, :]

        each_row(words, cells, npc, first + c, visit)
        return 0

    lax.fori_loop(0, products.shape[0], cell, 0)


def near_products_kernel(words, ext_ref, matrix_ref, out_ref, gathered):
    gather_cells(words, 2 * gathered.shape[0], matrix_ref.shape[0], ext_ref, gathered, 0)
    multiply_cells(matrix_ref, gathered, out_ref)


def far_cells_kernel(
    words_ref, scale, ext_ref, ghost_ref, matrix_ref, wide_ref, potential_ref, out_ref, back_ref,
    ext, gathered, products, words, sem, *sums
):
    copy = pltpu.make_async_copy(words_ref, words, sem)
    copy.start()
    owned = out_ref.shape[0]
    half, npc = gathered.shape[0], matrix_ref.shape[0]
    ext[0:owned, :] = ext_ref[0:owned, :]
    ext[owned:, :] = ghost_ref[...].astype(F32)
    for block in range(owned // LANES):
        here = slice(block * LANES, (block + 1) * LANES)
        sums[0][here, :] = spread_levels(potential_ref, block) * wide_ref[here, :]
    sums[0][owned:, :] = jnp.zeros_like(sums[0][owned:, :])
    for total in sums[1:]:
        total[...] = jnp.zeros_like(total)
    copy.wait()
    gather_cells(words, 2 * half, npc, ext, gathered, half)
    multiply_cells(matrix_ref, gathered, products)
    scatter_cells(words, scale, 2 * half, npc, products, sums, half)
    back_ref[...] = sum(total[owned:, :] for total in sums).astype(BF16)
    out_ref[...] = sum(total[0:owned, :] for total in sums)


def near_sums_kernel(
    npc, words_ref, scale_ref, products_ref, start_ref, out_ref, words, sem, scale, scale_sem, *sums
):
    copy = pltpu.make_async_copy(words_ref, words, sem)
    copy.start()
    scale_copy = pltpu.make_async_copy(scale_ref, scale, scale_sem)
    scale_copy.start()
    sums = (out_ref,) + sums
    out_ref[...] = start_ref[...]
    for total in sums[1:]:
        total[...] = jnp.zeros_like(total)
    copy.wait()
    scale_copy.wait()
    scatter_cells(words, scale, 2 * products_ref.shape[0], npc, products_ref, sums, 0)
    out_ref[...] = sum(total[...] for total in sums)


def apply_operator(links, scale, matrix, potential, wide, ext, edge):
    cells, npc = scale.shape[0], matrix.shape[0]
    half, padded = cells // 2, (npc + 7) // 8 * 8
    plane = edge.shape[0]
    whole = ext.shape
    owned = whole[0] - plane
    held = (half, padded, LANES)
    ghost = shifted(edge, "domain", -1)
    index = [pltpu.SMEM(links.shape, jnp.int32), pltpu.SemaphoreType.DMA]
    products = pl.pallas_call(
        near_products_kernel,
        out_shape=jax.ShapeDtypeStruct(held, F32),
        in_specs=[SM, VM, VM],
        out_specs=VM,
        scratch_shapes=[pltpu.VMEM(held, F32)],
        compiler_params=params(16),
        cost_estimate=cost(0, 14 << 20),
        name="near_products",
    )(links, ext, matrix)
    ghost, products = ordered(ghost, products)
    sums, back = pl.pallas_call(
        far_cells_kernel,
        out_shape=(
            jax.ShapeDtypeStruct((owned, LANES), F32),
            jax.ShapeDtypeStruct((plane, LANES), BF16),
        ),
        in_specs=[VM, SM, VM, VM, VM, VM, VM],
        out_specs=(VM, VM),
        scratch_shapes=[pltpu.VMEM(whole, F32), pltpu.VMEM(held, F32), pltpu.VMEM(held, F32)]
        + index
        + [pltpu.VMEM(whole, F32)] * CHAINS,
        compiler_params=params(22),
        cost_estimate=cost(0, 28 << 20),
        name="far_cells",
    )(links, scale, ext, ghost, matrix, wide, potential)
    back = shifted(back, "domain", 1)
    sums = pl.pallas_call(
        functools.partial(near_sums_kernel, npc),
        out_shape=jax.ShapeDtypeStruct((owned, LANES), F32),
        in_specs=[VM] * 4,
        out_specs=VM,
        scratch_shapes=index
        + [pltpu.SMEM(scale.shape, F32), pltpu.SemaphoreType.DMA]
        + [pltpu.VMEM((owned, LANES), F32)] * (CHAINS - 1),
        compiler_params=params(16),
        cost_estimate=cost(0, 14 << 20),
        name="near_sums",
    )(links, scale, products, sums)
    return sums, back


def add_back(nodes, target, back_ref, factor, scaled, picked=None):
    scaled[...] = back_ref[...].astype(F32) * factor

    def body(step, _):
        at = [step * 16 + k for k in range(16)]
        rows = [pl.ds(nodes[i], 1) for i in at]
        new = [target[r, :] + scaled[pl.ds(i, 1), :] for i, r in zip(at, rows)]
        for i, r, value in zip(at, rows, new):
            target[r, :] = value
            if picked is not None:
                picked[pl.ds(i, 1), :] = value
        return 0

    lax.fori_loop(0, nodes.shape[0] // 16, body, 0)


def first_kernel(nodes, sums_ref, back_ref, term_ref, ext_ref, edge_ref, scaled, picked):
    owned = sums_ref.shape[0]
    term_ref[...] = sums_ref[...] * (1.0 / HALF_WIDTH)
    add_back(nodes, term_ref, back_ref, 1.0 / HALF_WIDTH, scaled, picked)
    edge_ref[...] = picked[...].astype(BF16)
    ext_ref[0:owned, :] = term_ref[...].astype(BF16).astype(F32)


def first_term(nodes, sums, back):
    owned, plane = sums.shape[0], nodes.shape[0]
    return pl.pallas_call(
        first_kernel,
        out_shape=(
            jax.ShapeDtypeStruct((owned, LANES), F32),
            jax.ShapeDtypeStruct((owned + plane, LANES), F32),
            jax.ShapeDtypeStruct((plane, LANES), BF16),
        ),
        in_specs=[SM, VM, VM],
        out_specs=(VM, VM, VM),
        scratch_shapes=[pltpu.VMEM((plane, LANES), F32)] * 2,
        compiler_params=params(16),
        cost_estimate=cost(0, 8 << 20),
        name="first_term",
    )(nodes, sums, back)


def second_kernel(nodes, sums_ref, back_ref, previous_ref, *refs):
    pieces, (rest_ref, total, scaled) = refs[:-3], refs[-3:]
    total[...] = sums_ref[...] * (2.0 / HALF_WIDTH) - previous_ref[...].astype(F32)
    add_back(nodes, total, back_ref, 2.0 / HALF_WIDTH, scaled)
    count = len(pieces)
    rows = total.shape[0] // count
    for k, piece in enumerate(pieces):
        start = pl.multiple_of(lax.rem(lax.axis_index("band") + k, count) * rows, rows)
        part = total[pl.ds(start, rows), :].astype(BF16)
        piece[...] = part
        if k:
            rest_ref[(k - 1) * rows : k * rows, :] = part


def second_term(nodes, sums, back, previous, count):
    owned = sums.shape[0]
    rows = owned // count
    made = pl.pallas_call(
        second_kernel,
        out_shape=[jax.ShapeDtypeStruct((rows, LANES), BF16)] * count
        + [jax.ShapeDtypeStruct((owned - rows, LANES), BF16)],
        in_specs=[SM, VM, VM, VM],
        out_specs=[VM] * (count + 1),
        scratch_shapes=[pltpu.VMEM(sums.shape, F32), pltpu.VMEM(back.shape, F32)],
        compiler_params=params(16),
        cost_estimate=cost(0, 6 << 20),
        name="second_term",
    )(nodes, sums, back, previous)
    return made[:count], made[count]


def gram_kernel(*refs):
    pieces, (keep_ref, send_ref, held) = refs[:-3], refs[-3:]
    count = len(pieces)
    for s, piece in enumerate(pieces):
        held[lax.rem(lax.axis_index("band") + (count - s), count)] = piece[...]
    half = keep_ref.shape[0]

    def write(*halves):
        at = 0
        for i in range(count):
            for j in range(i + 1):
                halves[at // half][at % half : at % half + LANES, :] = lax.dot_general(
                    held[i], held[j], (((0,), (0,)), ((), ())), preferred_element_type=F32
                )
                at += LANES

    side = lax.rem(lax.axis_index("domain"), 2)
    pl.when(side == 0)(lambda: write(keep_ref, send_ref))
    pl.when(side != 0)(lambda: write(send_ref, keep_ref))


def partial_gram(pieces):
    count = len(pieces)
    rows = count * (count + 1) // 2 * LANES
    return pl.pallas_call(
        gram_kernel,
        out_shape=[jax.ShapeDtypeStruct((rows // 2, LANES), F32)] * 2,
        in_specs=[VM] * count,
        out_specs=[VM] * 2,
        scratch_shapes=[pltpu.VMEM((count,) + pieces[0].shape, BF16)],
        compiler_params=params(16),
        cost_estimate=cost(0, 4 << 20),
        name="partial_gram",
    )(*pieces)


def quarters_kernel(a_ref, b_ref, *refs):
    outs, total = refs[:-1], refs[-1]
    total[...] = a_ref[...] + b_ref[...]
    rows = outs[0].shape[0]
    place = lax.axis_index("domain") // 2
    for m, out in enumerate(outs):
        out[...] = total[pl.ds(pl.multiple_of((place ^ m) * rows, rows), rows), :]


def quarters(a, b, count):
    rows = a.shape[0] // count
    return pl.pallas_call(
        quarters_kernel,
        out_shape=[jax.ShapeDtypeStruct((rows, LANES), F32)] * count,
        in_specs=[VM, VM],
        out_specs=[VM] * count,
        scratch_shapes=[pltpu.VMEM(a.shape, F32)],
        compiler_params=params(4),
        cost_estimate=cost(0, 1 << 20),
        name="quarters",
    )(a, b)


def joined_kernel(*refs):
    parts, out_ref = refs[:-1], refs[-1]
    rows = parts[0].shape[0]
    place = lax.axis_index("domain") // 2
    for m, part in enumerate(parts):
        out_ref[pl.ds(pl.multiple_of((place ^ m) * rows, rows), rows), :] = part[...]


def joined(parts):
    rows = parts[0].shape[0] * len(parts)
    return pl.pallas_call(
        joined_kernel,
        out_shape=jax.ShapeDtypeStruct((rows, LANES), F32),
        in_specs=[VM] * len(parts),
        out_specs=VM,
        compiler_params=params(4),
        cost_estimate=cost(0, 1 << 20),
        name="joined",
    )(*parts)


def paired(value, axis, mask):
    count = lax.axis_size(axis)
    return lax.ppermute(value, axis, [(i, i ^ mask) for i in range(count)])


def passed_up(rests, firsts, held):
    rows = firsts[held].shape[0]
    count = lax.axis_size("band")
    onward = jnp.concatenate([rests[held][rows:], firsts[held]])
    return lax.ppermute(onward, "band", [(i, i + 1) for i in range(held, count - 1)])


def passed_up_last(rows):
    count = lax.axis_size("band")
    return lax.ppermute(rows, "band", [(count - 2, count - 1)])


def ordered(*values):
    return lax.optimization_barrier(values)


def summed_beside(keep, send, rests, firsts):
    count = lax.axis_size("band")
    half = keep + paired(send, "domain", 1)
    if lax.axis_size("domain") != 8 or count != 4:
        for held in range(count - 1):
            rests.append(passed_up(rests, firsts, held))
        side = lax.axis_index("domain") % 2
        both = jnp.stack([half, jnp.zeros_like(half)])
        both = lax.psum(jnp.where(side == 0, both, both[::-1]) * 1.0, ("domain", "band"))
        return both[side], both[1 - side]
    rests.append(passed_up(rests, firsts, 0))
    total, *others = quarters(keep, paired(send, "domain", 1), 4)
    for part in [paired(other, "domain", 2 * m) for m, other in enumerate(others, 1)]:
        total = total + part
    parts = [total] + [shifted(total, "band", s) for s in range(1, count)]
    parts[1], rests[1] = ordered(parts[1], rests[1])
    rests.append(passed_up(rests, firsts, 1))
    rows = firsts[1].shape[0]
    skipping = jnp.concatenate([rests[1][2 * rows :], firsts[1]])
    relayed = ordered(parts[1], firsts[2])[1]
    rests.append((lax.ppermute(skipping, "band", [(1, 3)]), passed_up_last(relayed)))
    total = sum(parts[1:], parts[0])
    half = joined([total] + [paired(total, "domain", 2 * m) for m in (1, 2, 3)])
    return half, paired(half, "domain", 1)


def split_dot(a, b, dims=(((1,), (0,)), ((), ()))):
    def parts(x):
        high = x.astype(BF16)
        return high, (x - high.astype(F32)).astype(BF16)

    def dot(x, y):
        return lax.dot_general(x, y, dims, preferred_element_type=F32)

    (a_high, a_low), (b_high, b_low) = parts(a), parts(b)
    return dot(a_high, b_high) + (dot(a_high, b_low) + dot(a_low, b_high))


def small_inverse(tiles, lane):
    count, tiles, done = len(tiles), list(tiles), []
    shape = tiles[0].shape
    sub = lax.broadcasted_iota(jnp.int32, shape, 0)

    def along_lanes(tile, column):
        return jnp.broadcast_to(tile[:, column : column + 1], shape)

    def along_rows(tile, row):
        return jnp.broadcast_to(tile[row : row + 1, :], shape)

    def stacked(rows):
        tile = rows[0]
        for i in range(1, 8):
            tile = jnp.where(sub == i, rows[i], tile)
        return tile

    columns = [along_lanes(tiles[0], m) for m in range(8)]
    for p in range(count):
        base = 8 * p
        group = (lane >= base) & (lane < base + 8)
        entry = {(i, j): along_rows(columns[j], i) for j in range(8) for i in range(j, 8)}
        start = jnp.where(group, (lane - base == sub).astype(F32), tiles[p])
        solved = [along_rows(start, i) for i in range(8)]
        following = None
        if p + 1 < count:
            ahead = [along_lanes(tiles[p + 1], base + m) for m in range(8)]
            columns = [along_lanes(tiles[p + 1], base + 8 + m) for m in range(8)]
            following = jnp.where(group, 0.0, tiles[p + 1])
        inverse, factor = [], {}
        for j in range(8):
            pivot = 1.0 / entry[j, j]
            inverse.append(pivot)
            if following is not None:
                scaled = ahead[j] * pivot
                columns = [c - scaled * along_rows(ahead[j], m) for m, c in enumerate(columns)]
                following = following - scaled * solved[j]
                for m in range(j + 1, 8):
                    ahead[m] = ahead[m] - scaled * entry[m, j]
            for i in range(j + 1, 8):
                factor[i, j] = entry[i, j] * pivot
            for i in range(j + 1, 8):
                for k in range(j + 1, i + 1):
                    entry[i, k] = entry[i, k] - factor[i, j] * entry[k, j]
                solved[i] = solved[i] - factor[i, j] * solved[j]
        result = stacked([solved[i] * lax.rsqrt(entry[i, i]) for i in range(8)])
        done.append(jnp.where(lane <= base + sub, result, 0.0))
        if p + 2 < count:
            back = [None] * 8
            for i in range(7, -1, -1):
                value = solved[i] * inverse[i]
                for k in range(i + 1, 8):
                    value = value - factor[k, i] * back[k]
                back[i] = value
            value = jnp.where(group, 0.0, tiles[p + 2])
            for m in range(8):
                value = value - along_lanes(tiles[p + 2], base + m) * back[m]
            tiles[p + 2] = value
            if p + 3 < count:
                spread = [stacked(back), jnp.zeros((LANES - 8 - base, LANES), F32)]
                if base:
                    spread = [jnp.zeros((base, LANES), F32)] + spread
                made = split_dot(
                    jnp.concatenate(tiles[p + 3 :], axis=0), jnp.concatenate(spread, axis=0)
                )
                for i in range(p + 3, count):
                    row = 8 * (i - p - 3)
                    tiles[i] = jnp.where(group, 0.0, tiles[i]) - made[row : row + 8, :]
        if following is not None:
            tiles[p + 1] = following
    return done


def inverse_kernel(over, mine_ref, other_ref, out_ref, work, small):
    half = mine_ref.shape[0]
    side = lax.rem(lax.axis_index("domain"), 2)
    size = work.shape[0]
    blocks = size // LANES
    at = 0
    for i in range(blocks):
        for j in range(i + 1):
            here = slice(at % half, at % half + LANES)
            block = jnp.where(side == at // half, mine_ref[here, :], other_ref[here, :]) * over
            work[i * LANES : (i + 1) * LANES, j * LANES : (j + 1) * LANES] = block
            if i != j:
                work[j * LANES : (j + 1) * LANES, i * LANES : (i + 1) * LANES] = block.T
            at += LANES
    out_ref[...] = jnp.zeros_like(out_ref)
    lane = lax.broadcasted_iota(jnp.int32, (8, LANES), 1)

    def step(k, _):
        base = pl.multiple_of(k * LANES, LANES)
        tiles = [
            work[pl.ds(pl.multiple_of(base + 8 * i, 8), 8), pl.ds(base, LANES)]
            for i in range(LANES // 8)
        ]
        for i, tile in enumerate(small_inverse(tiles, lane)):
            small[8 * i : 8 * i + 8, :] = tile
        for which in range(blocks):

            @pl.when(k == which)
            def _():
                a, b = which * LANES, (which + 1) * LANES
                diagonal = small[...]
                out_ref[a:b, a:b] = diagonal
                if which:
                    left = split_dot(diagonal, work[a:b, 0:a])
                    out_ref[a:b, 0:a] = left
                if b < size:
                    right = split_dot(diagonal, work[a:b, b:size])
                    column = split_dot(work[b:size, a:b], diagonal, (((1,), (1,)), ((), ())))
                    work[b:size, b:size] = work[b:size, b:size] - split_dot(column, right)
                    work[b:size, a:b] = -split_dot(column, diagonal)
                    if which:
                        work[b:size, 0:a] = work[b:size, 0:a] - split_dot(column, left)

        return 0

    lax.fori_loop(0, blocks, step, 0)


def inverse_factor(mine, other, size, over):
    return pl.pallas_call(
        functools.partial(inverse_kernel, over),
        out_shape=jax.ShapeDtypeStruct((size, size), F32),
        in_specs=[VM, VM],
        out_specs=VM,
        scratch_shapes=[
            pltpu.VMEM((size, size), F32),
            pltpu.VMEM((LANES, LANES), F32),
        ],
        compiler_params=params(16),
        cost_estimate=cost(0, 70 << 20),
        name="inverse_factor",
    )(mine, other)


def factor_blocks(factor_ref, blocks_ref, sources):
    band = lax.axis_index("band")
    row = pl.ds(pl.multiple_of(band * LANES, LANES), LANES)
    for k, s in enumerate(sources):
        source = band - s
        column = pl.ds(pl.multiple_of(jnp.maximum(source, 0) * LANES, LANES), LANES)
        block = jnp.where(source >= 0, factor_ref[row, column], 0.0).T
        high = block.astype(BF16)
        here = slice(k * LANES, (k + 1) * LANES)
        blocks_ref[here, 0:LANES] = high
        blocks_ref[here, LANES:] = (block - high.astype(F32)).astype(BF16)


def both_parts(pieces, blocks):
    made = jnp.dot(jnp.concatenate(pieces, axis=1), blocks, preferred_element_type=F32)
    return made[:, 0:LANES] + made[:, LANES:]


def early_kernel(factor_ref, *refs):
    made_ref, blocks_ref = refs[-2:]
    count = made_ref.shape[0]
    firsts, rests = refs[:count], refs[count:-2]
    rows = made_ref.shape[1]
    factor_blocks(factor_ref, blocks_ref, range(count))
    made_ref[0] = both_parts([first[...] for first in firsts], blocks_ref[...])
    for j in range(1, count):
        pieces = [rest[(j - 1) * rows : j * rows, :] for rest in rests]
        made_ref[j] = both_parts(pieces, blocks_ref[0 : len(rests) * LANES, :])


def late_kernel(shape, factor_ref, early_ref, *refs):
    out_ref, blocks_ref, made_ref, sems = refs[-4:]
    others = list(refs[:-4])
    count, rows = early_ref.shape[:2]
    rests = [
        [
            ref.at[k : k + rows, :]
            for ref in [others.pop(0) for _ in range(size)]
            for k in range(0, ref.shape[0], rows)
        ]
        for size in shape
    ]
    band = lax.axis_index("band")

    def put(source, j):
        start = pl.multiple_of(lax.rem(band + j, count) * rows, rows)
        copy = pltpu.make_async_copy(source, out_ref.at[pl.ds(start, rows), :], sems.at[j])
        copy.start()
        return copy

    copies = [put(early_ref.at[0], 0)]
    factor_blocks(factor_ref, blocks_ref, range(count - len(rests), count))
    for j in range(1, count):
        pieces = [rest[j - 1][...] for rest in rests]
        made_ref[j - 1] = early_ref[j] + both_parts(pieces, blocks_ref[...])
        copies.append(put(made_ref.at[j - 1], j))
    for copy in copies:
        copy.wait()


def output(factor, firsts, rests):
    count = len(firsts)
    rows = firsts[0].shape[0]
    soon = (count + 1) // 2
    early = pl.pallas_call(
        early_kernel,
        out_shape=jax.ShapeDtypeStruct((count, rows, LANES), F32),
        in_specs=[VM] * (1 + count + soon),
        out_specs=VM,
        scratch_shapes=[pltpu.VMEM((count * LANES, 2 * LANES), BF16)],
        compiler_params=params(16),
        cost_estimate=cost(0, 6 << 20),
        name="output_early",
    )(factor, *firsts, *rests[:soon])
    late = [rest if isinstance(rest, tuple) else (rest,) for rest in rests[soon:]]
    flat = [part for rest in late for part in rest]
    return pl.pallas_call(
        functools.partial(late_kernel, [len(rest) for rest in late]),
        out_shape=jax.ShapeDtypeStruct((rows * count, LANES), F32),
        in_specs=[VM] * (2 + len(flat)),
        out_specs=pl.BlockSpec(memory_space=pl.ANY),
        scratch_shapes=[
            pltpu.VMEM(((count - soon) * LANES, 2 * LANES), BF16),
            pltpu.VMEM((count - 1, rows, LANES), F32),
            pltpu.SemaphoreType.DMA((count,)),
        ],
        compiler_params=params(16),
        cost_estimate=cost(0, 6 << 20),
        name="output_late",
    )(factor, early, *flat)


def shards(states_block, cell_matrix, cell_scale, potential, connectivity, boundary_nodes):
    owned = states_block.shape[0]
    count = lax.axis_size("band")
    levels = potential.reshape(owned // LANES, LANES)

    start, words = prepare(boundary_nodes, states_block, connectivity)
    operator = functools.partial(apply_operator, words, cell_scale, cell_matrix, levels)
    sums, back = operator(*start)
    sums, back = operator(*first_term(boundary_nodes, sums, back))
    pieces, rest = second_term(boundary_nodes, sums, back, states_block, count)

    firsts = [pieces[0]] + [shifted(pieces[s], "band", s) for s in range(1, count)]
    firsts = list(ordered(*firsts))
    rests = [rest]
    keep, send = partial_gram(firsts)
    mine, other = summed_beside(keep, send, rests, firsts)
    over = 1.0 / (owned * lax.axis_size("domain"))
    factor = inverse_factor(mine, other, count * LANES, over)
    return output(factor, firsts, rests)


def solution(mesh):
    return jax.shard_map(
        shards,
        mesh=mesh,
        in_specs=(
            P("domain", "band"),
            P(),
            P("domain"),
            P("domain"),
            P("domain", None),
            P("domain"),
        ),
        out_specs=P("domain", "band"),
        check_vma=False,
    )
```

```python
import functools

import jax
import jax.numpy as jnp
from jax import lax
from jax.experimental import pallas as pl
from jax.experimental.pallas import tpu as pltpu
from jax.sharding import PartitionSpec as P

CENTER = 1.5
HALF_WIDTH = 1.25
LANES = 128
CHAINS = 7
F32 = jnp.float32
BF16 = jnp.bfloat16
VM = pl.BlockSpec(memory_space=pltpu.VMEM)
SM = pl.BlockSpec(memory_space=pltpu.SMEM)


def params(mebibytes):
    return pltpu.CompilerParams(vmem_limit_bytes=mebibytes << 20)


def cost(flops, moved):
    return pl.CostEstimate(flops=flops, bytes_accessed=moved, transcendentals=0)


def shifted(value, axis, steps):
    count = lax.axis_size(axis)
    return lax.ppermute(value, axis, [(i, (i + steps) % count) for i in range(count)])


def spread_levels(potential_ref, block):
    return jnp.broadcast_to(potential_ref[block : block + 1, :], (LANES, LANES)).T - CENTER


def rows_out(rows_of, potential_ref, owned, base_ref, ext_ref):
    for block in range(owned // LANES):
        here = slice(block * LANES, (block + 1) * LANES)
        wide = rows_of(here)
        base_ref[here, :] = spread_levels(potential_ref, block) * wide
        ext_ref[here, :] = wide.astype(BF16).astype(F32)
    base_ref[owned:, :] = jnp.zeros_like(base_ref[owned:, :])


def prepare_kernel(nodes, rows_ref, links_ref, ext_ref, edge_ref, words_ref, picked):
    owned = rows_ref.shape[0]
    ext_ref[0:owned, :] = rows_ref[...].astype(F32)
    pack_links(links_ref, words_ref)

    def body(step, _):
        for k in range(48):
            i = step * 48 + k
            picked[pl.ds(i, 1), :] = ext_ref[pl.ds(nodes[i], 1), :]
        return 0

    lax.fori_loop(0, nodes.shape[0] // 48, body, 0)
    edge_ref[...] = picked[...].astype(BF16)


def prepare(nodes, rows, links):
    owned, plane = rows.shape[0], nodes.shape[0]
    cells, npc = links.shape
    groups = ((npc + 1) // 2 + LANES - 1) // LANES
    ext, edge, words = pl.pallas_call(
        prepare_kernel,
        out_shape=(
            jax.ShapeDtypeStruct((owned + plane, LANES), F32),
            jax.ShapeDtypeStruct((plane, LANES), BF16),
            jax.ShapeDtypeStruct((groups * cells, LANES), jnp.int32),
        ),
        in_specs=[SM, VM, VM],
        out_specs=(VM, VM, VM),
        scratch_shapes=[pltpu.VMEM((plane, LANES), F32)],
        compiler_params=params(8),
        cost_estimate=cost(0, 12 << 20),
        name="prepare",
    )(nodes, rows, links)
    return (ext, ext, edge), words.reshape(-1)


def pack_links(links_ref, words_ref):
    cells, npc = links_ref.shape
    half = (npc + 1) // 2
    early = links_ref[:, 0:half]
    late = jnp.concatenate(
        [links_ref[:, half:npc], jnp.zeros((cells, 2 * half - npc), jnp.int32)], axis=1
    )
    words = early | (late << 16)
    for k in range(0, half, LANES):
        width = min(LANES, half - k)
        words_ref[k // LANES * cells : (k // LANES + 1) * cells, 0:width] = words[:, k : k + width]


def each_row(words, cells, npc, cell, visit):
    half = (npc + 1) // 2
    base = cell * LANES
    for r in range(half):
        word = words[base + (r // LANES * cells * LANES + r % LANES)]
        visit(r, pl.ds(word & 0xFFFF, 1))
        if r + half < npc:
            visit(r + half, pl.ds(word >> 16, 1))


def gather_cells(words, cells, npc, ext_ref, gathered, first):
    def cell(c, _):
        def visit(r, row):
            gathered[c, r : r + 1, :] = ext_ref[row, :]

        each_row(words, cells, npc, first + c, visit)
        return 0

    lax.fori_loop(0, gathered.shape[0], cell, 0)


def multiply_cells(matrix_ref, gathered, products):
    cells, npc = gathered.shape[0], matrix_ref.shape[0]
    for c in range(0, cells, 2):
        both = jnp.concatenate(
            [gathered[c, 0:npc, :].astype(BF16), gathered[c + 1, 0:npc, :].astype(BF16)], axis=1
        )
        made = jnp.dot(matrix_ref[...], both, preferred_element_type=F32)
        for half in range(2):
            products[c + half, 0:npc, :] = made[:, half * LANES : (half + 1) * LANES]


def scatter_cells(words, scale, cells, npc, products, sums, first):
    def cell(c, _):
        seen = []
        factor = jnp.full((1, LANES), scale[first + c], F32)

        def visit(r, row):
            total = sums[len(seen) % len(sums)]
            seen.append(r)
            total[row, :] = total[row, :] + factor * products[c, r : r + 1, :]

        each_row(words, cells, npc, first + c, visit)
        return 0

    lax.fori_loop(0, products.shape[0], cell, 0)


def near_products_kernel(words, ext_ref, matrix_ref, out_ref, gathered):
    gather_cells(words, 2 * gathered.shape[0], matrix_ref.shape[0], ext_ref, gathered, 0)
    multiply_cells(matrix_ref, gathered, out_ref)


def far_cells_kernel(
    words_ref, scale, ext_ref, ghost_ref, matrix_ref, wide_ref, potential_ref, out_ref, back_ref,
    ext, gathered, products, words, sem, *sums
):
    copy = pltpu.make_async_copy(words_ref, words, sem)
    copy.start()
    owned = out_ref.shape[0]
    half, npc = gathered.shape[0], matrix_ref.shape[0]
    ext[0:owned, :] = ext_ref[0:owned, :]
    ext[owned:, :] = ghost_ref[...].astype(F32)
    for block in range(owned // LANES):
        here = slice(block * LANES, (block + 1) * LANES)
        sums[0][here, :] = spread_levels(potential_ref, block) * wide_ref[here, :]
    sums[0][owned:, :] = jnp.zeros_like(sums[0][owned:, :])
    for total in sums[1:]:
        total[...] = jnp.zeros_like(total)
    copy.wait()
    gather_cells(words, 2 * half, npc, ext, gathered, half)
    multiply_cells(matrix_ref, gathered, products)
    scatter_cells(words, scale, 2 * half, npc, products, sums, half)
    back_ref[...] = sum(total[owned:, :] for total in sums).astype(BF16)
    out_ref[...] = sum(total[0:owned, :] for total in sums)


def near_sums_kernel(
    npc, words_ref, scale_ref, products_ref, start_ref, out_ref, words, sem, scale, scale_sem, *sums
):
    copy = pltpu.make_async_copy(words_ref, words, sem)
    copy.start()
    scale_copy = pltpu.make_async_copy(scale_ref, scale, scale_sem)
    scale_copy.start()
    sums = (out_ref,) + sums
    out_ref[...] = start_ref[...]
    for total in sums[1:]:
        total[...] = jnp.zeros_like(total)
    copy.wait()
    scale_copy.wait()
    scatter_cells(words, scale, 2 * products_ref.shape[0], npc, products_ref, sums, 0)
    out_ref[...] = sum(total[...] for total in sums)


def apply_operator(links, scale, matrix, potential, wide, ext, edge):
    cells, npc = scale.shape[0], matrix.shape[0]
    half, padded = cells // 2, (npc + 7) // 8 * 8
    plane = edge.shape[0]
    whole = ext.shape
    owned = whole[0] - plane
    held = (half, padded, LANES)
    ghost = shifted(edge, "domain", -1)
    index = [pltpu.SMEM(links.shape, jnp.int32), pltpu.SemaphoreType.DMA]
    products = pl.pallas_call(
        near_products_kernel,
        out_shape=jax.ShapeDtypeStruct(held, F32),
        in_specs=[SM, VM, VM],
        out_specs=VM,
        scratch_shapes=[pltpu.VMEM(held, F32)],
        compiler_params=params(16),
        cost_estimate=cost(0, 14 << 20),
        name="near_products",
    )(links, ext, matrix)
    ghost, products = ordered(ghost, products)
    sums, back = pl.pallas_call(
        far_cells_kernel,
        out_shape=(
            jax.ShapeDtypeStruct((owned, LANES), F32),
            jax.ShapeDtypeStruct((plane, LANES), BF16),
        ),
        in_specs=[VM, SM, VM, VM, VM, VM, VM],
        out_specs=(VM, VM),
        scratch_shapes=[pltpu.VMEM(whole, F32), pltpu.VMEM(held, F32), pltpu.VMEM(held, F32)]
        + index
        + [pltpu.VMEM(whole, F32)] * CHAINS,
        compiler_params=params(22),
        cost_estimate=cost(0, 28 << 20),
        name="far_cells",
    )(links, scale, ext, ghost, matrix, wide, potential)
    back = shifted(back, "domain", 1)
    sums = pl.pallas_call(
        functools.partial(near_sums_kernel, npc),
        out_shape=jax.ShapeDtypeStruct((owned, LANES), F32),
        in_specs=[VM] * 4,
        out_specs=VM,
        scratch_shapes=index
        + [pltpu.SMEM(scale.shape, F32), pltpu.SemaphoreType.DMA]
        + [pltpu.VMEM((owned, LANES), F32)] * (CHAINS - 1),
        compiler_params=params(16),
        cost_estimate=cost(0, 14 << 20),
        name="near_sums",
    )(links, scale, products, sums)
    return sums, back


def add_back(nodes, target, back_ref, factor, scaled, picked=None):
    scaled[...] = back_ref[...].astype(F32) * factor

    def body(step, _):
        at = [step * 16 + k for k in range(16)]
        rows = [pl.ds(nodes[i], 1) for i in at]
        new = [target[r, :] + scaled[pl.ds(i, 1), :] for i, r in zip(at, rows)]
        for i, r, value in zip(at, rows, new):
            target[r, :] = value
            if picked is not None:
                picked[pl.ds(i, 1), :] = value
        return 0

    lax.fori_loop(0, nodes.shape[0] // 16, body, 0)


def first_kernel(nodes, sums_ref, back_ref, term_ref, ext_ref, edge_ref, scaled, picked):
    owned = sums_ref.shape[0]
    term_ref[...] = sums_ref[...] * (1.0 / HALF_WIDTH)
    add_back(nodes, term_ref, back_ref, 1.0 / HALF_WIDTH, scaled, picked)
    edge_ref[...] = picked[...].astype(BF16)
    ext_ref[0:owned, :] = term_ref[...].astype(BF16).astype(F32)


def first_term(nodes, sums, back):
    owned, plane = sums.shape[0], nodes.shape[0]
    return pl.pallas_call(
        first_kernel,
        out_shape=(
            jax.ShapeDtypeStruct((owned, LANES), F32),
            jax.ShapeDtypeStruct((owned + plane, LANES), F32),
            jax.ShapeDtypeStruct((plane, LANES), BF16),
        ),
        in_specs=[SM, VM, VM],
        out_specs=(VM, VM, VM),
        scratch_shapes=[pltpu.VMEM((plane, LANES), F32)] * 2,
        compiler_params=params(16),
        cost_estimate=cost(0, 8 << 20),
        name="first_term",
    )(nodes, sums, back)


def second_kernel(nodes, sums_ref, back_ref, previous_ref, *refs):
    pieces, (total, scaled) = refs[:-2], refs[-2:]
    total[...] = sums_ref[...] * (2.0 / HALF_WIDTH) - previous_ref[...].astype(F32)
    add_back(nodes, total, back_ref, 2.0 / HALF_WIDTH, scaled)
    count = len(pieces)
    rows = total.shape[0] // count
    for k, piece in enumerate(pieces):
        start = pl.multiple_of(lax.rem(lax.axis_index("band") + k, count) * rows, rows)
        piece[...] = total[pl.ds(start, rows), :].astype(BF16)


def second_term(nodes, sums, back, previous, count):
    owned = sums.shape[0]
    rows = owned // count
    made = pl.pallas_call(
        second_kernel,
        out_shape=[jax.ShapeDtypeStruct((rows, LANES), BF16)] * count,
        in_specs=[SM, VM, VM, VM],
        out_specs=[VM] * count,
        scratch_shapes=[pltpu.VMEM(sums.shape, F32), pltpu.VMEM(back.shape, F32)],
        compiler_params=params(16),
        cost_estimate=cost(0, 6 << 20),
        name="second_term",
    )(nodes, sums, back, previous)
    return made


def gram_kernel(*refs):
    pieces, (keep_ref, send_ref, held) = refs[:-3], refs[-3:]
    count = len(pieces)
    for s, piece in enumerate(pieces):
        held[lax.rem(lax.axis_index("band") + (count - s), count)] = piece[...]
    half = keep_ref.shape[0]

    def write(*halves):
        at = 0
        for i in range(count):
            for j in range(i + 1):
                halves[at // half][at % half : at % half + LANES, :] = lax.dot_general(
                    held[i], held[j], (((0,), (0,)), ((), ())), preferred_element_type=F32
                )
                at += LANES

    side = lax.rem(lax.axis_index("domain"), 2)
    pl.when(side == 0)(lambda: write(keep_ref, send_ref))
    pl.when(side != 0)(lambda: write(send_ref, keep_ref))


def partial_gram(pieces):
    count = len(pieces)
    rows = count * (count + 1) // 2 * LANES
    return pl.pallas_call(
        gram_kernel,
        out_shape=[jax.ShapeDtypeStruct((rows // 2, LANES), F32)] * 2,
        in_specs=[VM] * count,
        out_specs=[VM] * 2,
        scratch_shapes=[pltpu.VMEM((count,) + pieces[0].shape, BF16)],
        compiler_params=params(16),
        cost_estimate=cost(0, 4 << 20),
        name="partial_gram",
    )(*pieces)


def quarters_kernel(a_ref, b_ref, *refs):
    outs, total = refs[:-1], refs[-1]
    total[...] = a_ref[...] + b_ref[...]
    rows = outs[0].shape[0]
    place = lax.axis_index("domain") // 2
    for m, out in enumerate(outs):
        out[...] = total[pl.ds(pl.multiple_of((place ^ m) * rows, rows), rows), :]


def quarters(a, b, count):
    rows = a.shape[0] // count
    return pl.pallas_call(
        quarters_kernel,
        out_shape=[jax.ShapeDtypeStruct((rows, LANES), F32)] * count,
        in_specs=[VM, VM],
        out_specs=[VM] * count,
        scratch_shapes=[pltpu.VMEM(a.shape, F32)],
        compiler_params=params(4),
        cost_estimate=cost(0, 1 << 20),
        name="quarters",
    )(a, b)


def joined_kernel(*refs):
    parts, out_ref = refs[:-1], refs[-1]
    rows = parts[0].shape[0]
    place = lax.axis_index("domain") // 2
    for m, part in enumerate(parts):
        out_ref[pl.ds(pl.multiple_of((place ^ m) * rows, rows), rows), :] = part[...]


def joined(parts):
    rows = parts[0].shape[0] * len(parts)
    return pl.pallas_call(
        joined_kernel,
        out_shape=jax.ShapeDtypeStruct((rows, LANES), F32),
        in_specs=[VM] * len(parts),
        out_specs=VM,
        compiler_params=params(4),
        cost_estimate=cost(0, 1 << 20),
        name="joined",
    )(*parts)


def paired(value, axis, mask):
    count = lax.axis_size(axis)
    return lax.ppermute(value, axis, [(i, i ^ mask) for i in range(count)])


def passed_up(rests, firsts, held):
    rows = firsts[held].shape[0]
    count = lax.axis_size("band")
    onward = jnp.concatenate([rests[held][rows:], firsts[held]])
    return lax.ppermute(onward, "band", [(i, i + 1) for i in range(held, count - 1)])


def passed_up_last(rows):
    count = lax.axis_size("band")
    return lax.ppermute(rows, "band", [(count - 2, count - 1)])


def ordered(*values):
    return lax.optimization_barrier(values)


def summed_beside(keep, send, rests, firsts):
    count = lax.axis_size("band")
    half = keep + paired(send, "domain", 1)
    if lax.axis_size("domain") != 8 or count != 4:
        for held in range(count - 1):
            rests.append(passed_up(rests, firsts, held))
        side = lax.axis_index("domain") % 2
        both = jnp.stack([half, jnp.zeros_like(half)])
        both = lax.psum(jnp.where(side == 0, both, both[::-1]) * 1.0, ("domain", "band"))
        return both[side], both[1 - side]
    rests.append(passed_up(rests, firsts, 0))
    total, *others = quarters(keep, paired(send, "domain", 1), 4)
    for part in [paired(other, "domain", 2 * m) for m, other in enumerate(others, 1)]:
        total = total + part
    parts = [total] + [shifted(total, "band", s) for s in range(1, count)]
    parts[1], rests[1] = ordered(parts[1], rests[1])
    rests.append(passed_up(rests, firsts, 1))
    rows = firsts[1].shape[0]
    skipping = jnp.concatenate([rests[1][2 * rows :], firsts[1]])
    relayed = ordered(parts[1], firsts[2])[1]
    rests.append((lax.ppermute(skipping, "band", [(1, 3)]), passed_up_last(relayed)))
    total = sum(parts[1:], parts[0])
    half = joined([total] + [paired(total, "domain", 2 * m) for m in (1, 2, 3)])
    return half, paired(half, "domain", 1)


def split_dot(a, b, dims=(((1,), (0,)), ((), ()))):
    def parts(x):
        high = x.astype(BF16)
        return high, (x - high.astype(F32)).astype(BF16)

    def dot(x, y):
        return lax.dot_general(x, y, dims, preferred_element_type=F32)

    (a_high, a_low), (b_high, b_low) = parts(a), parts(b)
    return dot(a_high, b_high) + (dot(a_high, b_low) + dot(a_low, b_high))


def small_inverse(tiles, lane):
    count, tiles, done = len(tiles), list(tiles), []
    shape = tiles[0].shape
    sub = lax.broadcasted_iota(jnp.int32, shape, 0)

    def along_lanes(tile, column):
        return jnp.broadcast_to(tile[:, column : column + 1], shape)

    def along_rows(tile, row):
        return jnp.broadcast_to(tile[row : row + 1, :], shape)

    def stacked(rows):
        tile = rows[0]
        for i in range(1, 8):
            tile = jnp.where(sub == i, rows[i], tile)
        return tile

    columns = [along_lanes(tiles[0], m) for m in range(8)]
    for p in range(count):
        base = 8 * p
        group = (lane >= base) & (lane < base + 8)
        entry = {(i, j): along_rows(columns[j], i) for j in range(8) for i in range(j, 8)}
        start = jnp.where(group, (lane - base == sub).astype(F32), tiles[p])
        solved = [along_rows(start, i) for i in range(8)]
        following = None
        if p + 1 < count:
            ahead = [along_lanes(tiles[p + 1], base + m) for m in range(8)]
            columns = [along_lanes(tiles[p + 1], base + 8 + m) for m in range(8)]
            following = jnp.where(group, 0.0, tiles[p + 1])
        inverse, factor = [], {}
        for j in range(8):
            pivot = 1.0 / entry[j, j]
            inverse.append(pivot)
            if following is not None:
                scaled = ahead[j] * pivot
                columns = [c - scaled * along_rows(ahead[j], m) for m, c in enumerate(columns)]
                following = following - scaled * solved[j]
                for m in range(j + 1, 8):
                    ahead[m] = ahead[m] - scaled * entry[m, j]
            for i in range(j + 1, 8):
                factor[i, j] = entry[i, j] * pivot
            for i in range(j + 1, 8):
                for k in range(j + 1, i + 1):
                    entry[i, k] = entry[i, k] - factor[i, j] * entry[k, j]
                solved[i] = solved[i] - factor[i, j] * solved[j]
        result = stacked([solved[i] * lax.rsqrt(entry[i, i]) for i in range(8)])
        done.append(jnp.where(lane <= base + sub, result, 0.0))
        if p + 2 < count:
            back = [None] * 8
            for i in range(7, -1, -1):
                value = solved[i] * inverse[i]
                for k in range(i + 1, 8):
                    value = value - factor[k, i] * back[k]
                back[i] = value
            value = jnp.where(group, 0.0, tiles[p + 2])
            for m in range(8):
                value = value - along_lanes(tiles[p + 2], base + m) * back[m]
            tiles[p + 2] = value
            if p + 3 < count:
                spread = [stacked(back), jnp.zeros((LANES - 8 - base, LANES), F32)]
                if base:
                    spread = [jnp.zeros((base, LANES), F32)] + spread
                made = split_dot(
                    jnp.concatenate(tiles[p + 3 :], axis=0), jnp.concatenate(spread, axis=0)
                )
                for i in range(p + 3, count):
                    row = 8 * (i - p - 3)
                    tiles[i] = jnp.where(group, 0.0, tiles[i]) - made[row : row + 8, :]
        if following is not None:
            tiles[p + 1] = following
    return done


def inverse_kernel(over, mine_ref, other_ref, out_ref, work, small):
    half = mine_ref.shape[0]
    side = lax.rem(lax.axis_index("domain"), 2)
    size = work.shape[0]
    blocks = size // LANES
    at = 0
    for i in range(blocks):
        for j in range(i + 1):
            here = slice(at % half, at % half + LANES)
            block = jnp.where(side == at // half, mine_ref[here, :], other_ref[here, :]) * over
            work[i * LANES : (i + 1) * LANES, j * LANES : (j + 1) * LANES] = block
            if i != j:
                work[j * LANES : (j + 1) * LANES, i * LANES : (i + 1) * LANES] = block.T
            at += LANES
    out_ref[...] = jnp.zeros_like(out_ref)
    lane = lax.broadcasted_iota(jnp.int32, (8, LANES), 1)

    def step(k, _):
        base = pl.multiple_of(k * LANES, LANES)
        tiles = [
            work[pl.ds(pl.multiple_of(base + 8 * i, 8), 8), pl.ds(base, LANES)]
            for i in range(LANES // 8)
        ]
        for i, tile in enumerate(small_inverse(tiles, lane)):
            small[8 * i : 8 * i + 8, :] = tile
        for which in range(blocks):

            @pl.when(k == which)
            def _():
                a, b = which * LANES, (which + 1) * LANES
                diagonal = small[...]
                out_ref[a:b, a:b] = diagonal
                if which:
                    left = split_dot(diagonal, work[a:b, 0:a])
                    out_ref[a:b, 0:a] = left
                if b < size:
                    right = split_dot(diagonal, work[a:b, b:size])
                    column = split_dot(work[b:size, a:b], diagonal, (((1,), (1,)), ((), ())))
                    work[b:size, b:size] = work[b:size, b:size] - split_dot(column, right)
                    work[b:size, a:b] = -split_dot(column, diagonal)
                    if which:
                        work[b:size, 0:a] = work[b:size, 0:a] - split_dot(column, left)

        return 0

    lax.fori_loop(0, blocks, step, 0)


def inverse_factor(mine, other, size, over):
    return pl.pallas_call(
        functools.partial(inverse_kernel, over),
        out_shape=jax.ShapeDtypeStruct((size, size), F32),
        in_specs=[VM, VM],
        out_specs=VM,
        scratch_shapes=[
            pltpu.VMEM((size, size), F32),
            pltpu.VMEM((LANES, LANES), F32),
        ],
        compiler_params=params(16),
        cost_estimate=cost(0, 70 << 20),
        name="inverse_factor",
    )(mine, other)


def factor_blocks(factor_ref, blocks_ref, sources):
    band = lax.axis_index("band")
    row = pl.ds(pl.multiple_of(band * LANES, LANES), LANES)
    for k, s in enumerate(sources):
        source = band - s
        column = pl.ds(pl.multiple_of(jnp.maximum(source, 0) * LANES, LANES), LANES)
        block = jnp.where(source >= 0, factor_ref[row, column], 0.0).T
        high = block.astype(BF16)
        here = slice(k * LANES, (k + 1) * LANES)
        blocks_ref[here, 0:LANES] = high
        blocks_ref[here, LANES:] = (block - high.astype(F32)).astype(BF16)


def both_parts(pieces, blocks):
    made = jnp.dot(jnp.concatenate(pieces, axis=1), blocks, preferred_element_type=F32)
    return made[:, 0:LANES] + made[:, LANES:]


def early_kernel(factor_ref, *refs):
    made_ref, blocks_ref = refs[-2:]
    count = made_ref.shape[0]
    firsts, rests = refs[:count], refs[count:-2]
    rows = made_ref.shape[1]
    factor_blocks(factor_ref, blocks_ref, range(count))
    made_ref[0] = both_parts([first[...] for first in firsts], blocks_ref[...])
    for j in range(1, count):
        pieces = [rest[(j - 1) * rows : j * rows, :] for rest in rests]
        made_ref[j] = both_parts(pieces, blocks_ref[0 : len(rests) * LANES, :])


def late_kernel(shape, factor_ref, early_ref, *refs):
    out_ref, blocks_ref, made_ref, sems = refs[-4:]
    others = list(refs[:-4])
    count, rows = early_ref.shape[:2]
    rests = [
        [
            ref.at[k : k + rows, :]
            for ref in [others.pop(0) for _ in range(size)]
            for k in range(0, ref.shape[0], rows)
        ]
        for size in shape
    ]
    band = lax.axis_index("band")

    def put(source, j):
        start = pl.multiple_of(lax.rem(band + j, count) * rows, rows)
        copy = pltpu.make_async_copy(source, out_ref.at[pl.ds(start, rows), :], sems.at[j])
        copy.start()
        return copy

    copies = [put(early_ref.at[0], 0)]
    factor_blocks(factor_ref, blocks_ref, range(count - len(rests), count))
    for j in range(1, count):
        pieces = [rest[j - 1][...] for rest in rests]
        made_ref[j - 1] = early_ref[j] + both_parts(pieces, blocks_ref[...])
        copies.append(put(made_ref.at[j - 1], j))
    for copy in copies:
        copy.wait()


def output(factor, firsts, rests):
    count = len(firsts)
    rows = firsts[0].shape[0]
    soon = (count + 1) // 2
    early = pl.pallas_call(
        early_kernel,
        out_shape=jax.ShapeDtypeStruct((count, rows, LANES), F32),
        in_specs=[VM] * (1 + count + soon),
        out_specs=VM,
        scratch_shapes=[pltpu.VMEM((count * LANES, 2 * LANES), BF16)],
        compiler_params=params(16),
        cost_estimate=cost(0, 6 << 20),
        name="output_early",
    )(factor, *firsts, *rests[:soon])
    late = [rest if isinstance(rest, tuple) else (rest,) for rest in rests[soon:]]
    flat = [part for rest in late for part in rest]
    return pl.pallas_call(
        functools.partial(late_kernel, [len(rest) for rest in late]),
        out_shape=jax.ShapeDtypeStruct((rows * count, LANES), F32),
        in_specs=[VM] * (2 + len(flat)),
        out_specs=pl.BlockSpec(memory_space=pl.ANY),
        scratch_shapes=[
            pltpu.VMEM(((count - soon) * LANES, 2 * LANES), BF16),
            pltpu.VMEM((count - 1, rows, LANES), F32),
            pltpu.SemaphoreType.DMA((count,)),
        ],
        compiler_params=params(16),
        cost_estimate=cost(0, 6 << 20),
        name="output_late",
    )(factor, early, *flat)


def shards(states_block, cell_matrix, cell_scale, potential, connectivity, boundary_nodes):
    owned = states_block.shape[0]
    count = lax.axis_size("band")
    levels = potential.reshape(owned // LANES, LANES)

    start, words = prepare(boundary_nodes, states_block, connectivity)
    operator = functools.partial(apply_operator, words, cell_scale, cell_matrix, levels)
    sums, back = operator(*start)
    sums, back = operator(*first_term(boundary_nodes, sums, back))
    pieces = second_term(boundary_nodes, sums, back, states_block, count)

    firsts = [pieces[0]] + [shifted(pieces[s], "band", s) for s in range(1, count)]
    firsts = list(ordered(*firsts))
    rests = [jnp.concatenate(pieces[1:])]
    keep, send = partial_gram(firsts)
    mine, other = summed_beside(keep, send, rests, firsts)
    over = 1.0 / (owned * lax.axis_size("domain"))
    factor = inverse_factor(mine, other, count * LANES, over)
    return output(factor, firsts, rests)


def solution(mesh):
    return jax.shard_map(
        shards,
        mesh=mesh,
        in_specs=(
            P("domain", "band"),
            P(),
            P("domain"),
            P("domain"),
            P("domain", None),
            P("domain"),
        ),
        out_specs=P("domain", "band"),
        check_vma=False,
    )
```

```python
import functools

import jax
import jax.numpy as jnp
from jax import lax
from jax.experimental import pallas as pl
from jax.experimental.pallas import tpu as pltpu
from jax.sharding import PartitionSpec as P

CENTER = 1.5
HALF_WIDTH = 1.25
LANES = 128
CHAINS = 7
F32 = jnp.float32
BF16 = jnp.bfloat16
VM = pl.BlockSpec(memory_space=pltpu.VMEM)
SM = pl.BlockSpec(memory_space=pltpu.SMEM)


def params(mebibytes):
    return pltpu.CompilerParams(vmem_limit_bytes=mebibytes << 20)


def cost(flops, moved):
    return pl.CostEstimate(flops=flops, bytes_accessed=moved, transcendentals=0)


def shifted(value, axis, steps):
    count = lax.axis_size(axis)
    return lax.ppermute(value, axis, [(i, (i + steps) % count) for i in range(count)])


def spread_levels(potential_ref, block):
    return jnp.broadcast_to(potential_ref[block : block + 1, :], (LANES, LANES)).T - CENTER


def rows_out(rows_of, potential_ref, owned, base_ref, ext_ref):
    for block in range(owned // LANES):
        here = slice(block * LANES, (block + 1) * LANES)
        wide = rows_of(here)
        base_ref[here, :] = spread_levels(potential_ref, block) * wide
        ext_ref[here, :] = wide.astype(BF16).astype(F32)
    base_ref[owned:, :] = jnp.zeros_like(base_ref[owned:, :])


def prepare_kernel(nodes, rows_ref, links_ref, ext_ref, edge_ref, words_ref, picked):
    owned = rows_ref.shape[0]
    ext_ref[0:owned, :] = rows_ref[...].astype(F32)
    pack_links(links_ref, words_ref)

    def body(step, _):
        for k in range(16):
            i = step * 16 + k
            picked[pl.ds(i, 1), :] = ext_ref[pl.ds(nodes[i], 1), :]
        return 0

    lax.fori_loop(0, nodes.shape[0] // 16, body, 0)
    edge_ref[...] = picked[...].astype(BF16)


def prepare(nodes, rows, links):
    owned, plane = rows.shape[0], nodes.shape[0]
    cells, npc = links.shape
    groups = ((npc + 1) // 2 + LANES - 1) // LANES
    ext, edge, words = pl.pallas_call(
        prepare_kernel,
        out_shape=(
            jax.ShapeDtypeStruct((owned + plane, LANES), F32),
            jax.ShapeDtypeStruct((plane, LANES), BF16),
            jax.ShapeDtypeStruct((groups * cells, LANES), jnp.int32),
        ),
        in_specs=[SM, VM, VM],
        out_specs=(VM, VM, VM),
        scratch_shapes=[pltpu.VMEM((plane, LANES), F32)],
        compiler_params=params(8),
        cost_estimate=cost(0, 12 << 20),
        name="prepare",
    )(nodes, rows, links)
    return (ext, ext, edge), words.reshape(-1)


def pack_links(links_ref, words_ref):
    cells, npc = links_ref.shape
    half = (npc + 1) // 2
    early = links_ref[:, 0:half]
    late = jnp.concatenate(
        [links_ref[:, half:npc], jnp.zeros((cells, 2 * half - npc), jnp.int32)], axis=1
    )
    words = early | (late << 16)
    for k in range(0, half, LANES):
        width = min(LANES, half - k)
        words_ref[k // LANES * cells : (k // LANES + 1) * cells, 0:width] = words[:, k : k + width]


def each_row(words, cells, npc, cell, visit):
    half = (npc + 1) // 2
    base = cell * LANES
    for r in range(half):
        word = words[base + (r // LANES * cells * LANES + r % LANES)]
        visit(r, pl.ds(word & 0xFFFF, 1))
        if r + half < npc:
            visit(r + half, pl.ds(word >> 16, 1))


def gather_cells(words, cells, npc, ext_ref, gathered, first):
    def cell(c, _):
        def visit(r, row):
            gathered[c, r : r + 1, :] = ext_ref[row, :]

        each_row(words, cells, npc, first + c, visit)
        return 0

    lax.fori_loop(0, gathered.shape[0], cell, 0)


def multiply_cells(matrix_ref, gathered, products):
    cells, npc = gathered.shape[0], matrix_ref.shape[0]
    for c in range(0, cells, 2):
        both = jnp.concatenate(
            [gathered[c, 0:npc, :].astype(BF16), gathered[c + 1, 0:npc, :].astype(BF16)], axis=1
        )
        made = jnp.dot(matrix_ref[...], both, preferred_element_type=F32)
        for half in range(2):
            products[c + half, 0:npc, :] = made[:, half * LANES : (half + 1) * LANES]


def scatter_cells(words, scale, cells, npc, products, sums, first):
    def cell(c, _):
        seen = []
        factor = jnp.full((1, LANES), scale[first + c], F32)

        def visit(r, row):
            total = sums[len(seen) % len(sums)]
            seen.append(r)
            total[row, :] = total[row, :] + factor * products[c, r : r + 1, :]

        each_row(words, cells, npc, first + c, visit)
        return 0

    lax.fori_loop(0, products.shape[0], cell, 0)


def near_products_kernel(words, ext_ref, matrix_ref, out_ref, gathered):
    gather_cells(words, 2 * gathered.shape[0], matrix_ref.shape[0], ext_ref, gathered, 0)
    multiply_cells(matrix_ref, gathered, out_ref)


def far_cells_kernel(
    words_ref, scale, ext_ref, ghost_ref, matrix_ref, wide_ref, potential_ref, out_ref, back_ref,
    ext, gathered, products, words, sem, *sums
):
    copy = pltpu.make_async_copy(words_ref, words, sem)
    copy.start()
    owned = out_ref.shape[0]
    half, npc = gathered.shape[0], matrix_ref.shape[0]
    ext[0:owned, :] = ext_ref[0:owned, :]
    ext[owned:, :] = ghost_ref[...].astype(F32)
    for block in range(owned // LANES):
        here = slice(block * LANES, (block + 1) * LANES)
        sums[0][here, :] = spread_levels(potential_ref, block) * wide_ref[here, :]
    sums[0][owned:, :] = jnp.zeros_like(sums[0][owned:, :])
    for total in sums[1:]:
        total[...] = jnp.zeros_like(total)
    copy.wait()
    gather_cells(words, 2 * half, npc, ext, gathered, half)
    multiply_cells(matrix_ref, gathered, products)
    scatter_cells(words, scale, 2 * half, npc, products, sums, half)
    back_ref[...] = sum(total[owned:, :] for total in sums).astype(BF16)
    out_ref[...] = sum(total[0:owned, :] for total in sums)


def near_sums_kernel(
    npc, words_ref, scale_ref, products_ref, start_ref, out_ref, words, sem, scale, scale_sem, *sums
):
    copy = pltpu.make_async_copy(words_ref, words, sem)
    copy.start()
    scale_copy = pltpu.make_async_copy(scale_ref, scale, scale_sem)
    scale_copy.start()
    sums = (out_ref,) + sums
    out_ref[...] = start_ref[...]
    for total in sums[1:]:
        total[...] = jnp.zeros_like(total)
    copy.wait()
    scale_copy.wait()
    scatter_cells(words, scale, 2 * products_ref.shape[0], npc, products_ref, sums, 0)
    out_ref[...] = sum(total[...] for total in sums)


def apply_operator(links, scale, matrix, potential, wide, ext, edge):
    cells, npc = scale.shape[0], matrix.shape[0]
    half, padded = cells // 2, (npc + 7) // 8 * 8
    plane = edge.shape[0]
    whole = ext.shape
    owned = whole[0] - plane
    held = (half, padded, LANES)
    ghost = shifted(edge, "domain", -1)
    index = [pltpu.SMEM(links.shape, jnp.int32), pltpu.SemaphoreType.DMA]
    products = pl.pallas_call(
        near_products_kernel,
        out_shape=jax.ShapeDtypeStruct(held, F32),
        in_specs=[SM, VM, VM],
        out_specs=VM,
        scratch_shapes=[pltpu.VMEM(held, F32)],
        compiler_params=params(16),
        cost_estimate=cost(0, 14 << 20),
        name="near_products",
    )(links, ext, matrix)
    ghost, products = ordered(ghost, products)
    sums, back = pl.pallas_call(
        far_cells_kernel,
        out_shape=(
            jax.ShapeDtypeStruct((owned, LANES), F32),
            jax.ShapeDtypeStruct((plane, LANES), BF16),
        ),
        in_specs=[VM, SM, VM, VM, VM, VM, VM],
        out_specs=(VM, VM),
        scratch_shapes=[pltpu.VMEM(whole, F32), pltpu.VMEM(held, F32), pltpu.VMEM(held, F32)]
        + index
        + [pltpu.VMEM(whole, F32)] * CHAINS,
        compiler_params=params(22),
        cost_estimate=cost(0, 28 << 20),
        name="far_cells",
    )(links, scale, ext, ghost, matrix, wide, potential)
    back = shifted(back, "domain", 1)
    sums = pl.pallas_call(
        functools.partial(near_sums_kernel, npc),
        out_shape=jax.ShapeDtypeStruct((owned, LANES), F32),
        in_specs=[VM] * 4,
        out_specs=VM,
        scratch_shapes=index
        + [pltpu.SMEM(scale.shape, F32), pltpu.SemaphoreType.DMA]
        + [pltpu.VMEM((owned, LANES), F32)] * (CHAINS - 1),
        compiler_params=params(16),
        cost_estimate=cost(0, 14 << 20),
        name="near_sums",
    )(links, scale, products, sums)
    return sums, back


def add_back(nodes, target, back_ref, factor, scaled, picked=None):
    scaled[...] = back_ref[...].astype(F32) * factor

    def body(step, _):
        at = [step * 8 + k for k in range(8)]
        rows = [pl.ds(nodes[i], 1) for i in at]
        new = [target[r, :] + scaled[pl.ds(i, 1), :] for i, r in zip(at, rows)]
        for i, r, value in zip(at, rows, new):
            target[r, :] = value
            if picked is not None:
                picked[pl.ds(i, 1), :] = value
        return 0

    lax.fori_loop(0, nodes.shape[0] // 8, body, 0)


def first_kernel(nodes, sums_ref, back_ref, term_ref, ext_ref, edge_ref, scaled, picked):
    owned = sums_ref.shape[0]
    term_ref[...] = sums_ref[...] * (1.0 / HALF_WIDTH)
    add_back(nodes, term_ref, back_ref, 1.0 / HALF_WIDTH, scaled, picked)
    edge_ref[...] = picked[...].astype(BF16)
    ext_ref[0:owned, :] = term_ref[...].astype(BF16).astype(F32)


def first_term(nodes, sums, back):
    owned, plane = sums.shape[0], nodes.shape[0]
    return pl.pallas_call(
        first_kernel,
        out_shape=(
            jax.ShapeDtypeStruct((owned, LANES), F32),
            jax.ShapeDtypeStruct((owned + plane, LANES), F32),
            jax.ShapeDtypeStruct((plane, LANES), BF16),
        ),
        in_specs=[SM, VM, VM],
        out_specs=(VM, VM, VM),
        scratch_shapes=[pltpu.VMEM((plane, LANES), F32)] * 2,
        compiler_params=params(16),
        cost_estimate=cost(0, 8 << 20),
        name="first_term",
    )(nodes, sums, back)


def second_kernel(nodes, sums_ref, back_ref, previous_ref, *refs):
    pieces, (rest_ref, total, scaled) = refs[:-3], refs[-3:]
    total[...] = sums_ref[...] * (2.0 / HALF_WIDTH) - previous_ref[...].astype(F32)
    add_back(nodes, total, back_ref, 2.0 / HALF_WIDTH, scaled)
    count = len(pieces)
    rows = total.shape[0] // count
    for k, piece in enumerate(pieces):
        start = pl.multiple_of(lax.rem(lax.axis_index("band") + k, count) * rows, rows)
        part = total[pl.ds(start, rows), :].astype(BF16)
        piece[...] = part
        if k:
            rest_ref[(k - 1) * rows : k * rows, :] = part


def second_term(nodes, sums, back, previous, count):
    owned = sums.shape[0]
    rows = owned // count
    made = pl.pallas_call(
        second_kernel,
        out_shape=[jax.ShapeDtypeStruct((rows, LANES), BF16)] * count
        + [jax.ShapeDtypeStruct((owned - rows, LANES), BF16)],
        in_specs=[SM, VM, VM, VM],
        out_specs=[VM] * (count + 1),
        scratch_shapes=[pltpu.VMEM(sums.shape, F32), pltpu.VMEM(back.shape, F32)],
        compiler_params=params(16),
        cost_estimate=cost(0, 6 << 20),
        name="second_term",
    )(nodes, sums, back, previous)
    return made[:count], made[count]


def gram_kernel(*refs):
    pieces, (keep_ref, send_ref, held) = refs[:-3], refs[-3:]
    count = len(pieces)
    for s, piece in enumerate(pieces):
        held[lax.rem(lax.axis_index("band") + (count - s), count)] = piece[...]
    half = keep_ref.shape[0]

    def write(*halves):
        at = 0
        for i in range(count):
            for j in range(i + 1):
                halves[at // half][at % half : at % half + LANES, :] = lax.dot_general(
                    held[i], held[j], (((0,), (0,)), ((), ())), preferred_element_type=F32
                )
                at += LANES

    side = lax.rem(lax.axis_index("domain"), 2)
    pl.when(side == 0)(lambda: write(keep_ref, send_ref))
    pl.when(side != 0)(lambda: write(send_ref, keep_ref))


def partial_gram(pieces):
    count = len(pieces)
    rows = count * (count + 1) // 2 * LANES
    return pl.pallas_call(
        gram_kernel,
        out_shape=[jax.ShapeDtypeStruct((rows // 2, LANES), F32)] * 2,
        in_specs=[VM] * count,
        out_specs=[VM] * 2,
        scratch_shapes=[pltpu.VMEM((count,) + pieces[0].shape, BF16)],
        compiler_params=params(16),
        cost_estimate=cost(0, 4 << 20),
        name="partial_gram",
    )(*pieces)


def quarters_kernel(a_ref, b_ref, *refs):
    outs, total = refs[:-1], refs[-1]
    total[...] = a_ref[...] + b_ref[...]
    rows = outs[0].shape[0]
    place = lax.axis_index("domain") // 2
    for m, out in enumerate(outs):
        out[...] = total[pl.ds(pl.multiple_of((place ^ m) * rows, rows), rows), :]


def quarters(a, b, count):
    rows = a.shape[0] // count
    return pl.pallas_call(
        quarters_kernel,
        out_shape=[jax.ShapeDtypeStruct((rows, LANES), F32)] * count,
        in_specs=[VM, VM],
        out_specs=[VM] * count,
        scratch_shapes=[pltpu.VMEM(a.shape, F32)],
        compiler_params=params(4),
        cost_estimate=cost(0, 1 << 20),
        name="quarters",
    )(a, b)


def joined_kernel(*refs):
    parts, out_ref = refs[:-1], refs[-1]
    rows = parts[0].shape[0]
    place = lax.axis_index("domain") // 2
    for m, part in enumerate(parts):
        out_ref[pl.ds(pl.multiple_of((place ^ m) * rows, rows), rows), :] = part[...]


def joined(parts):
    rows = parts[0].shape[0] * len(parts)
    return pl.pallas_call(
        joined_kernel,
        out_shape=jax.ShapeDtypeStruct((rows, LANES), F32),
        in_specs=[VM] * len(parts),
        out_specs=VM,
        compiler_params=params(4),
        cost_estimate=cost(0, 1 << 20),
        name="joined",
    )(*parts)


def paired(value, axis, mask):
    count = lax.axis_size(axis)
    return lax.ppermute(value, axis, [(i, i ^ mask) for i in range(count)])


def passed_up(rests, firsts, held):
    rows = firsts[held].shape[0]
    count = lax.axis_size("band")
    onward = jnp.concatenate([rests[held][rows:], firsts[held]])
    return lax.ppermute(onward, "band", [(i, i + 1) for i in range(held, count - 1)])


def passed_up_last(rows):
    count = lax.axis_size("band")
    return lax.ppermute(rows, "band", [(count - 2, count - 1)])


def ordered(*values):
    return lax.optimization_barrier(values)


def summed_beside(keep, send, rests, firsts):
    count = lax.axis_size("band")
    half = keep + paired(send, "domain", 1)
    if lax.axis_size("domain") != 8 or count != 4:
        for held in range(count - 1):
            rests.append(passed_up(rests, firsts, held))
        side = lax.axis_index("domain") % 2
        both = jnp.stack([half, jnp.zeros_like(half)])
        both = lax.psum(jnp.where(side == 0, both, both[::-1]) * 1.0, ("domain", "band"))
        return both[side], both[1 - side]
    rests.append(passed_up(rests, firsts, 0))
    total, *others = quarters(keep, paired(send, "domain", 1), 4)
    for part in [paired(other, "domain", 2 * m) for m, other in enumerate(others, 1)]:
        total = total + part
    parts = [total] + [shifted(total, "band", s) for s in range(1, count)]
    parts[1], rests[1] = ordered(parts[1], rests[1])
    rests.append(passed_up(rests, firsts, 1))
    rows = firsts[1].shape[0]
    skipping = jnp.concatenate([rests[1][2 * rows :], firsts[1]])
    relayed = ordered(parts[1], firsts[2])[1]
    rests.append((lax.ppermute(skipping, "band", [(1, 3)]), passed_up_last(relayed)))
    total = sum(parts[1:], parts[0])
    half = joined([total] + [paired(total, "domain", 2 * m) for m in (1, 2, 3)])
    return half, paired(half, "domain", 1)


def split_dot(a, b, dims=(((1,), (0,)), ((), ()))):
    def parts(x):
        high = x.astype(BF16)
        return high, (x - high.astype(F32)).astype(BF16)

    def dot(x, y):
        return lax.dot_general(x, y, dims, preferred_element_type=F32)

    (a_high, a_low), (b_high, b_low) = parts(a), parts(b)
    return dot(a_high, b_high) + (dot(a_high, b_low) + dot(a_low, b_high))


def small_inverse(tiles, lane):
    count, tiles, done = len(tiles), list(tiles), []
    shape = tiles[0].shape
    sub = lax.broadcasted_iota(jnp.int32, shape, 0)

    def along_lanes(tile, column):
        return jnp.broadcast_to(tile[:, column : column + 1], shape)

    def along_rows(tile, row):
        return jnp.broadcast_to(tile[row : row + 1, :], shape)

    def stacked(rows):
        tile = rows[0]
        for i in range(1, 8):
            tile = jnp.where(sub == i, rows[i], tile)
        return tile

    columns = [along_lanes(tiles[0], m) for m in range(8)]
    for p in range(count):
        base = 8 * p
        group = (lane >= base) & (lane < base + 8)
        entry = {(i, j): along_rows(columns[j], i) for j in range(8) for i in range(j, 8)}
        start = jnp.where(group, (lane - base == sub).astype(F32), tiles[p])
        solved = [along_rows(start, i) for i in range(8)]
        following = None
        if p + 1 < count:
            ahead = [along_lanes(tiles[p + 1], base + m) for m in range(8)]
            columns = [along_lanes(tiles[p + 1], base + 8 + m) for m in range(8)]
            following = jnp.where(group, 0.0, tiles[p + 1])
        inverse, factor = [], {}
        for j in range(8):
            pivot = 1.0 / entry[j, j]
            inverse.append(pivot)
            if following is not None:
                scaled = ahead[j] * pivot
                columns = [c - scaled * along_rows(ahead[j], m) for m, c in enumerate(columns)]
                following = following - scaled * solved[j]
                for m in range(j + 1, 8):
                    ahead[m] = ahead[m] - scaled * entry[m, j]
            for i in range(j + 1, 8):
                factor[i, j] = entry[i, j] * pivot
            for i in range(j + 1, 8):
                for k in range(j + 1, i + 1):
                    entry[i, k] = entry[i, k] - factor[i, j] * entry[k, j]
                solved[i] = solved[i] - factor[i, j] * solved[j]
        result = stacked([solved[i] * lax.rsqrt(entry[i, i]) for i in range(8)])
        done.append(jnp.where(lane <= base + sub, result, 0.0))
        if p + 2 < count:
            back = [None] * 8
            for i in range(7, -1, -1):
                value = solved[i] * inverse[i]
                for k in range(i + 1, 8):
                    value = value - factor[k, i] * back[k]
                back[i] = value
            value = jnp.where(group, 0.0, tiles[p + 2])
            for m in range(8):
                value = value - along_lanes(tiles[p + 2], base + m) * back[m]
            tiles[p + 2] = value
            if p + 3 < count:
                spread = [stacked(back), jnp.zeros((LANES - 8 - base, LANES), F32)]
                if base:
                    spread = [jnp.zeros((base, LANES), F32)] + spread
                made = split_dot(
                    jnp.concatenate(tiles[p + 3 :], axis=0), jnp.concatenate(spread, axis=0)
                )
                for i in range(p + 3, count):
                    row = 8 * (i - p - 3)
                    tiles[i] = jnp.where(group, 0.0, tiles[i]) - made[row : row + 8, :]
        if following is not None:
            tiles[p + 1] = following
    return done


def inverse_kernel(over, mine_ref, other_ref, out_ref, work, small):
    half = mine_ref.shape[0]
    side = lax.rem(lax.axis_index("domain"), 2)
    size = work.shape[0]
    blocks = size // LANES
    at = 0
    for i in range(blocks):
        for j in range(i + 1):
            here = slice(at % half, at % half + LANES)
            block = jnp.where(side == at // half, mine_ref[here, :], other_ref[here, :]) * over
            work[i * LANES : (i + 1) * LANES, j * LANES : (j + 1) * LANES] = block
            if i != j:
                work[j * LANES : (j + 1) * LANES, i * LANES : (i + 1) * LANES] = block.T
            at += LANES
    out_ref[...] = jnp.zeros_like(out_ref)
    lane = lax.broadcasted_iota(jnp.int32, (8, LANES), 1)

    def step(k, _):
        base = pl.multiple_of(k * LANES, LANES)
        tiles = [
            work[pl.ds(pl.multiple_of(base + 8 * i, 8), 8), pl.ds(base, LANES)]
            for i in range(LANES // 8)
        ]
        for i, tile in enumerate(small_inverse(tiles, lane)):
            small[8 * i : 8 * i + 8, :] = tile
        for which in range(blocks):

            @pl.when(k == which)
            def _():
                a, b = which * LANES, (which + 1) * LANES
                diagonal = small[...]
                out_ref[a:b, a:b] = diagonal
                if which:
                    left = split_dot(diagonal, work[a:b, 0:a])
                    out_ref[a:b, 0:a] = left
                if b < size:
                    right = split_dot(diagonal, work[a:b, b:size])
                    column = split_dot(work[b:size, a:b], diagonal, (((1,), (1,)), ((), ())))
                    work[b:size, b:size] = work[b:size, b:size] - split_dot(column, right)
                    work[b:size, a:b] = -split_dot(column, diagonal)
                    if which:
                        work[b:size, 0:a] = work[b:size, 0:a] - split_dot(column, left)

        return 0

    lax.fori_loop(0, blocks, step, 0)


def inverse_factor(mine, other, size, over):
    return pl.pallas_call(
        functools.partial(inverse_kernel, over),
        out_shape=jax.ShapeDtypeStruct((size, size), F32),
        in_specs=[VM, VM],
        out_specs=VM,
        scratch_shapes=[
            pltpu.VMEM((size, size), F32),
            pltpu.VMEM((LANES, LANES), F32),
        ],
        compiler_params=params(16),
        cost_estimate=cost(0, 70 << 20),
        name="inverse_factor",
    )(mine, other)


def factor_blocks(factor_ref, blocks_ref, sources):
    band = lax.axis_index("band")
    row = pl.ds(pl.multiple_of(band * LANES, LANES), LANES)
    for k, s in enumerate(sources):
        source = band - s
        column = pl.ds(pl.multiple_of(jnp.maximum(source, 0) * LANES, LANES), LANES)
        block = jnp.where(source >= 0, factor_ref[row, column], 0.0).T
        high = block.astype(BF16)
        here = slice(k * LANES, (k + 1) * LANES)
        blocks_ref[here, 0:LANES] = high
        blocks_ref[here, LANES:] = (block - high.astype(F32)).astype(BF16)


def both_parts(pieces, blocks):
    made = jnp.dot(jnp.concatenate(pieces, axis=1), blocks, preferred_element_type=F32)
    return made[:, 0:LANES] + made[:, LANES:]


def early_kernel(factor_ref, *refs):
    made_ref, blocks_ref = refs[-2:]
    count = made_ref.shape[0]
    firsts, rests = refs[:count], refs[count:-2]
    rows = made_ref.shape[1]
    factor_blocks(factor_ref, blocks_ref, range(count))
    made_ref[0] = both_parts([first[...] for first in firsts], blocks_ref[...])
    for j in range(1, count):
        pieces = [rest[(j - 1) * rows : j * rows, :] for rest in rests]
        made_ref[j] = both_parts(pieces, blocks_ref[0 : len(rests) * LANES, :])


def late_kernel(shape, factor_ref, early_ref, *refs):
    out_ref, blocks_ref, made_ref, sems = refs[-4:]
    others = list(refs[:-4])
    count, rows = early_ref.shape[:2]
    rests = [
        [
            ref.at[k : k + rows, :]
            for ref in [others.pop(0) for _ in range(size)]
            for k in range(0, ref.shape[0], rows)
        ]
        for size in shape
    ]
    band = lax.axis_index("band")

    def put(source, j):
        start = pl.multiple_of(lax.rem(band + j, count) * rows, rows)
        copy = pltpu.make_async_copy(source, out_ref.at[pl.ds(start, rows), :], sems.at[j])
        copy.start()
        return copy

    copies = [put(early_ref.at[0], 0)]
    factor_blocks(factor_ref, blocks_ref, range(count - len(rests), count))
    for j in range(1, count):
        pieces = [rest[j - 1][...] for rest in rests]
        made_ref[j - 1] = early_ref[j] + both_parts(pieces, blocks_ref[...])
        copies.append(put(made_ref.at[j - 1], j))
    for copy in copies:
        copy.wait()


def output(factor, firsts, rests):
    count = len(firsts)
    rows = firsts[0].shape[0]
    soon = (count + 1) // 2
    early = pl.pallas_call(
        early_kernel,
        out_shape=jax.ShapeDtypeStruct((count, rows, LANES), F32),
        in_specs=[VM] * (1 + count + soon),
        out_specs=VM,
        scratch_shapes=[pltpu.VMEM((count * LANES, 2 * LANES), BF16)],
        compiler_params=params(16),
        cost_estimate=cost(0, 6 << 20),
        name="output_early",
    )(factor, *firsts, *rests[:soon])
    late = [rest if isinstance(rest, tuple) else (rest,) for rest in rests[soon:]]
    flat = [part for rest in late for part in rest]
    return pl.pallas_call(
        functools.partial(late_kernel, [len(rest) for rest in late]),
        out_shape=jax.ShapeDtypeStruct((rows * count, LANES), F32),
        in_specs=[VM] * (2 + len(flat)),
        out_specs=pl.BlockSpec(memory_space=pl.ANY),
        scratch_shapes=[
            pltpu.VMEM(((count - soon) * LANES, 2 * LANES), BF16),
            pltpu.VMEM((count - 1, rows, LANES), F32),
            pltpu.SemaphoreType.DMA((count,)),
        ],
        compiler_params=params(16),
        cost_estimate=cost(0, 6 << 20),
        name="output_late",
    )(factor, early, *flat)


def shards(states_block, cell_matrix, cell_scale, potential, connectivity, boundary_nodes):
    owned = states_block.shape[0]
    count = lax.axis_size("band")
    levels = potential.reshape(owned // LANES, LANES)

    start, words = prepare(boundary_nodes, states_block, connectivity)
    operator = functools.partial(apply_operator, words, cell_scale, cell_matrix, levels)
    sums, back = operator(*start)
    sums, back = operator(*first_term(boundary_nodes, sums, back))
    pieces, rest = second_term(boundary_nodes, sums, back, states_block, count)

    firsts = [pieces[0]] + [shifted(pieces[s], "band", s) for s in range(1, count)]
    firsts = list(ordered(*firsts))
    rests = [rest]
    keep, send = partial_gram(firsts)
    mine, other = summed_beside(keep, send, rests, firsts)
    over = 1.0 / (owned * lax.axis_size("domain"))
    factor = inverse_factor(mine, other, count * LANES, over)
    return output(factor, firsts, rests)


def solution(mesh):
    return jax.shard_map(
        shards,
        mesh=mesh,
        in_specs=(
            P("domain", "band"),
            P(),
            P("domain"),
            P("domain"),
            P("domain", None),
            P("domain"),
        ),
        out_specs=P("domain", "band"),
        check_vma=False,
    )
```
